32 devices in a mesh: dp: 2 (over x), row: 4 (over y, core), col: 4 (over z).
Axes of the slice: x: 2, y: 2, z: 4, core: 2. Of those that a mesh axis runs over, the one named last changes fastest.
Arguments:
- tokens: bfloat16 [8192, 1024], P(('dp', 'col'), 'row'), may hold values from -8 to 8
- w_qkv: bfloat16 [3, 1024, 1024], P(None, 'row', 'col'), may hold values from -0.1875 to 0.1875
- bias_qv: bfloat16 [2, 1024], P(None, 'col'), may hold values from -3 to 3
- w_out: bfloat16 [1024, 1024], P('col', 'row'), may hold values from -2 to 2
- bias_out: bfloat16 [1024], P('row'), may hold values from -3 to 3
- gain_one: bfloat16 [1024], P('row'), may hold values from 0.25 to 1.75
- shift_one: bfloat16 [1024], P('row'), may hold values from -3 to 3
- w_in: bfloat16 [1024, 4096], P('row', 'col'), may hold values from -0.1875 to 0.1875
- bias_in: bfloat16 [4096], P('col'), may hold values from -3 to 3
- w_back: bfloat16 [4096, 1024], P('col', 'row'), may hold values from -0.09375 to 0.09375
- bias_back: bfloat16 [1024], P('row'), may hold values from -3 to 3
- gain_two: bfloat16 [1024], P('row'), may hold values from 0.25 to 1.75
- shift_two: bfloat16 [1024], P('row'), may hold values from -3 to 3
- cotangent: bfloat16 [8192, 1024], P(('dp', 'col'), 'row'), may hold values from -8 to 8
Outputs:
- output: bfloat16 [8192, 1024], P(('dp', 'col'), 'row')
- grad_tokens: float32 [8192, 1024], P(('dp', 'col'), 'row')
- grad_w_qkv: float32 [3, 1024, 1024], P(None, 'row', 'col')
- grad_bias_qv: float32 [2, 1024], P(None, 'col')
- grad_w_out: float32 [1024, 1024], P('col', 'row')
- grad_bias_out: float32 [1024], P('row')
- grad_gain_one: float32 [1024], P('row')
- grad_shift_one: float32 [1024], P('row')
- grad_w_in: float32 [1024, 4096], P('row', 'col')
- grad_bias_in: float32 [4096], P('col')
- grad_w_back: float32 [4096, 1024], P('col', 'row')
- grad_bias_back: float32 [1024], P('row')
- grad_gain_two: float32 [1024], P('row')
- grad_shift_two: float32 [1024], P('row')
The draws below stay inside these ranges and needn't reach their ends.
All inputs are finite; a program needn't handle non-finite values.
Results may differ from the reference program's by a relative error of at most 0.012.
The reference program's roundings to bfloat16 on the way count: a program that leaves them out, or rounds other values in their place, can miss the bound.
Values may be sent and summed in bfloat16 or wider, within the bound.
No kernel may reach another device: no remote copies, remote signals or barrier semaphores. Data moves between devices by JAX's collectives and lax.ppermute only.
A program may use at most 128 MiB of HBM per device.

```python
import jax
import jax.numpy as jnp
from jax import lax

D = 1024
FF = 4096
HEADS = 16
HEAD_DIM = 64
SEQ_LEN = 512
TOKENS = 8192


def rising_field(key):
    column = jnp.arange(D, dtype=jnp.float32) / D
    col_scale = 0.6 * 3.0 ** column
    base = jnp.clip(jax.random.normal(key, (TOKENS, D), jnp.float32), -4.0, 4.0)
    return base * col_scale


def draw_tokens(key, part):
    return rising_field(jax.random.fold_in(key, 11)).astype(jnp.bfloat16)


def draw_cotangent(key, part):
    return rising_field(jax.random.fold_in(key, 23)).astype(jnp.bfloat16)


def levels(rng, extent, pieces, smallest, high):
    loudness, own = 1.0, jax.random.fold_in(rng, 6)
    for dim, parts in pieces:
        draws = jnp.exp(jax.random.uniform(jax.random.fold_in(own, dim), (parts,), jnp.float32, smallest / len(pieces), high / len(pieces)))
        loudness = loudness * jnp.repeat(draws, extent[dim] // parts).reshape([-1 if axis == dim else 1 for axis in range(len(extent))])
    return loudness


def normal_values(rng, shape, width, most, pieces=(), held_as=jnp.bfloat16):
    values = jax.random.normal(rng, shape, jnp.float32) * width
    if len(pieces) > 0:
        values = levels(rng, shape, pieces, -0.22, 0.18) * values
    return jnp.clip(values, min=-most, max=most).astype(held_as)


def setup_inputs(seed: int = 0) -> dict:
    key_list = jax.random.split(jax.random.key(seed), 15)
    return {
        "tokens": draw_tokens(jax.random.fold_in(key_list[14], 71), 0),
        "w_qkv": normal_values(key_list[1], (3, D, D), D ** -0.5, 0.1875, ((1, 4), (2, 4))),
        "bias_qv": normal_values(key_list[2], (2, D), 0.5, 3.0, ((1, 4),)),
        "w_out": normal_values(key_list[3], (D, D), (max(D // 128, 2)) ** -0.5, 2.0, ((0, 4), (1, 4))),
        "bias_out": normal_values(key_list[4], (D,), 0.5, 3.0, ((0, 4),)),
        "gain_one": jnp.clip(1.0 + 0.15 * jax.random.normal(key_list[5], (D,), jnp.float32), 0.25, 1.75).astype(jnp.bfloat16),
        "shift_one": normal_values(key_list[6], (D,), 0.5, 3.0, ((0, 4),)),
        "w_in": normal_values(key_list[7], (D, FF), D ** -0.5, 0.1875, ((0, 4), (1, 4))),
        "bias_in": normal_values(key_list[8], (FF,), 0.5, 3.0, ((0, 4),)),
        "w_back": normal_values(key_list[9], (FF, D), FF ** -0.5, 0.09375, ((0, 4), (1, 4))),
        "bias_back": normal_values(key_list[10], (D,), 0.5, 3.0, ((0, 4),)),
        "gain_two": jnp.clip(1.0 + 0.15 * jax.random.normal(key_list[11], (D,), jnp.float32), 0.25, 1.75).astype(jnp.bfloat16),
        "shift_two": normal_values(key_list[12], (D,), 0.5, 3.0, ((0, 4),)),
        "cotangent": draw_cotangent(jax.random.fold_in(key_list[14], 71), 0),
    }


norm_eps = 1e-12

@jax.custom_vjp
def low(v):
    return lax.optimization_barrier(v.astype(jnp.bfloat16)).astype(jnp.float32)

@jax.custom_vjp
def low_back(v):
    return v

def low_keep(v):
    return (low(v), None)

def low_pass(kept, grad):
    return (grad,)

def back_keep(v):
    return (v, None)

def back_low(kept, grad):
    return (low(grad),)
low.defvjp(low_keep, low_pass)
low_back.defvjp(back_keep, back_low)

def matmul_high(left, right):
    return jnp.dot(left, right, precision=lax.Precision.HIGHEST, preferred_element_type=jnp.float32)

def layer_norm(resid, gain, shift):
    row_mean = lax.optimization_barrier(jnp.mean(resid, -1, keepdims=True))
    centered = resid - row_mean
    variance = lax.optimization_barrier(jnp.mean(centered * centered, -1, keepdims=True))
    return centered * lax.rsqrt(variance + norm_eps) * gain + shift

def attend(seq_block):
    queries, key_rows, value_rows = seq_block
    scores = jnp.einsum('qhd,khd->hqk', queries, key_rows, precision=lax.Precision.HIGHEST) * HEAD_DIM ** (-0.5)
    scores = low_back(scores)
    attn_weights = low(jax.nn.softmax(scores, axis=-1))
    return jnp.einsum('hqk,khd->qhd', attn_weights, value_rows, precision=lax.Precision.HIGHEST)

def forward(tokens_f, w_qkv, bias_qv, w_out, bias_out, gain_one, shift_one, w_in, bias_in, w_back, bias_back, gain_two, shift_two):
    token_count = tokens_f.shape[0]
    seq_count = token_count // SEQ_LEN
    joined_rows = jnp.einsum('td,jde->tje', tokens_f, w_qkv, precision=lax.Precision.HIGHEST)
    queries = low(low_back(joined_rows[:, 0] + bias_qv[0]))
    key_rows = low(low_back(joined_rows[:, 1]))
    value_rows = low(low_back(joined_rows[:, 2] + bias_qv[1]))
    seq_shape = (seq_count, SEQ_LEN, HEADS, HEAD_DIM)
    context = lax.map(jax.checkpoint(attend), (queries.reshape(seq_shape), key_rows.reshape(seq_shape), value_rows.reshape(seq_shape)))
    context = low(low_back(context.reshape(token_count, D)))
    attended = low_back(matmul_high(context, w_out) + bias_out)
    hidden_one = layer_norm(tokens_f + attended, gain_one, shift_one)
    pre_act = low_back(matmul_high(low(hidden_one), w_in) + bias_in)
    activated = low(jax.nn.gelu(pre_act, approximate=False))
    mlp_out = low_back(matmul_high(activated, w_back) + bias_back)
    return layer_norm(hidden_one + mlp_out, gain_two, shift_two)

def reference(tokens, w_qkv, bias_qv, w_out, bias_out, gain_one, shift_one, w_in, bias_in, w_back, bias_back, gain_two, shift_two, cotangent):
    inputs = [a.astype(jnp.float32) for a in (tokens, w_qkv, bias_qv, w_out, bias_out, gain_one, shift_one, w_in, bias_in, w_back, bias_back, gain_two, shift_two)]
    result, pullback = jax.vjp(forward, *inputs)
    grads = pullback(cotangent.astype(jnp.float32))
    return (result.astype(jnp.bfloat16), grads[0], grads[1], grads[2], grads[3], grads[4], grads[5], grads[6], grads[7], grads[8], grads[9], grads[10], grads[11], grads[12])
```

```python
import jax
import jax.numpy as jnp
from jax import lax
from jax.sharding import PartitionSpec as P

HEAD_DIM = 64
SEQ_LEN = 512
norm_eps = 1e-12

f32 = jnp.float32
bf16 = jnp.bfloat16


def swap(values, axis, bit):
    size = lax.axis_size(axis)
    return lax.ppermute(values, axis, [(i, i ^ bit) for i in range(size)])


def dot(left, right, left_dim, right_dim):
    return lax.dot_general(
        left, right, (((left_dim,), (right_dim,)), ((), ())), preferred_element_type=f32
    )


def row_gather(block):
    across = swap(block, "row", 2)
    beside = swap(block, "row", 1)
    return [block, beside, across, swap(across, "row", 1)]


def row_reduce(parts):
    far = parts[2] + swap(parts[3].astype(bf16), "row", 1).astype(f32)
    far = swap(far.astype(bf16), "row", 2).astype(f32)
    near = parts[0] + swap(parts[1].astype(bf16), "row", 1).astype(f32)
    return near + far


def col_gather(block):
    size = lax.axis_size("col")
    here = lax.axis_index("col")
    up, down = [block], [block]
    for step in range(1, size):
        up.append(lax.ppermute(up[-1], "col", [(i, i - 1) for i in range(1, size - step + 1)]))
        down.append(lax.ppermute(down[-1], "col", [(i, i + 1) for i in range(step - 1, size - 1)]))
    return [block] + [
        jnp.where(here + step < size, up[step], down[size - step]) for step in range(1, size)
    ]


def col_reduce(parts):
    size = lax.axis_size("col")
    up = down = None
    for step in range(1, size):
        send_down, send_up = parts[size - step].astype(f32), parts[step].astype(f32)
        if step > 1:
            send_down, send_up = send_down + down.astype(f32), send_up + up.astype(f32)
        down = lax.ppermute(send_down.astype(bf16), "col", [(i, i + 1) for i in range(step)])
        up = lax.ppermute(
            send_up.astype(bf16), "col", [(i, i - 1) for i in range(size - step, size)]
        )
    return parts[0].astype(f32) + down.astype(f32) + up.astype(f32)


def dp_sum(values):
    size = lax.axis_size("dp")
    bit = 1
    while bit < size:
        low = values.astype(bf16)
        values = low.astype(f32) + swap(low, "dp", bit).astype(f32)
        bit *= 2
    return values


def normalize(resid):
    row_mean = jnp.mean(resid, 1, keepdims=True)
    centered = resid - row_mean
    variance = jnp.mean(centered * centered, 1, keepdims=True)
    inv_std = lax.rsqrt(variance + norm_eps)
    return centered * inv_std, inv_std


def norm_backward(incoming, normed, inv_std, gain):
    scaled = incoming * gain
    return inv_std * (
        scaled
        - jnp.mean(scaled, 1, keepdims=True)
        - normed * jnp.mean(scaled * normed, 1, keepdims=True)
    )


def row_swap(values, split, concat):
    return lax.all_to_all(values, "row", split, concat, tiled=True)


def per_device(
    tokens,
    w_qkv,
    bias_qv,
    w_out,
    bias_out,
    gain_one,
    shift_one,
    w_in,
    bias_in,
    w_back,
    bias_back,
    gain_two,
    shift_two,
    cotangent,
):
    rows, cols = lax.axis_size("row"), lax.axis_size("col")
    r, c = lax.axis_index("row"), lax.axis_index("col")
    group, width_local = tokens.shape
    block = group // rows
    width = width_local * rows
    heads_tile = w_qkv.shape[2]
    head_piece = heads_tile // rows
    hid_tile = w_in.shape[1]
    hid_piece = hid_tile // rows
    seq_count = group // SEQ_LEN
    head_count = cols * head_piece // HEAD_DIM
    score_scale = HEAD_DIM ** (-0.5)
    seq_shape = (seq_count, SEQ_LEN, head_count, HEAD_DIM)

    wq = jnp.transpose(w_qkv, (2, 0, 1)).reshape(rows, head_piece, 3, width_local)
    wq = jnp.transpose(wq, (0, 2, 1, 3)).reshape(rows * 3 * head_piece, width_local)
    wq = row_swap(wq, 0, 1)
    wq_blocks = [b.reshape(3, 1, head_piece, width) for b in col_gather(wq)]
    wq_all = jnp.concatenate(wq_blocks, 1).reshape(3 * cols * head_piece, width)

    across = swap(tokens, "row", 2)
    low_y = (r & 2) == 0
    pair = jnp.concatenate(
        [jnp.where(low_y, tokens, across), jnp.where(low_y, across, tokens)], 1
    )
    other = swap(pair, "row", 1)
    low_core = (r & 1) == 0
    even, odd = jnp.where(low_core, pair, other), jnp.where(low_core, other, pair)
    tokens_all = jnp.concatenate(
        [even[:, :width_local], odd[:, :width_local], even[:, width_local:], odd[:, width_local:]],
        1,
    )

    vectors = jnp.stack([bias_out, gain_one, shift_one, bias_back, gain_two, shift_two])
    vectors = lax.all_gather(vectors, "row", axis=1, tiled=True).astype(f32)
    bias_out_f, gain_one_f, shift_one_f, bias_back_f, gain_two_f, shift_two_f = [
        vectors[i] for i in range(6)
    ]
    hid_bias = lax.dynamic_slice(bias_in, (r * hid_piece,), (hid_piece,))
    head_bias = lax.dynamic_slice(bias_qv, (0, r * head_piece), (2, head_piece)).reshape(-1)
    col_bias = lax.all_gather(jnp.concatenate([hid_bias, head_bias]), "col", axis=0)
    col_bias = jnp.concatenate([col_bias, col_bias])
    col_bias = lax.dynamic_slice(col_bias, (c, 0), (cols, col_bias.shape[1])).astype(f32)
    bias_in_f = col_bias[:, :hid_piece].reshape(-1)
    bias_q = col_bias[:, hid_piece : hid_piece + head_piece].reshape(-1)
    bias_v = col_bias[:, hid_piece + head_piece :].reshape(-1)

    wo = row_swap(w_out, 0, 1)
    wo_all = jnp.concatenate(col_gather(wo), 0)
    wi = row_swap(w_in, 1, 0)
    wi_all = jnp.concatenate(col_gather(wi), 1)
    wb = row_swap(w_back, 0, 1)
    wb_all = jnp.concatenate(col_gather(wb), 0)
    cot = row_swap(cotangent, 0, 1).astype(f32)

    heads_width = cols * head_piece
    joined = dot(tokens_all, wq_all, 1, 1)
    queries = (joined[:, :heads_width] + bias_q).astype(bf16).reshape(seq_shape)
    key_rows = joined[:, heads_width : 2 * heads_width].astype(bf16).reshape(seq_shape)
    value_rows = (joined[:, 2 * heads_width :] + bias_v).astype(bf16).reshape(seq_shape)
    scores = (
        jnp.einsum("sqhd,skhd->shqk", queries, key_rows, preferred_element_type=f32) * score_scale
    )
    row_peak = jnp.max(scores, -1, keepdims=True)
    expo_scores = jnp.exp(scores - row_peak)
    row_total = jnp.sum(expo_scores, -1, keepdims=True)
    attn_weights = expo_scores / row_total
    log_total = row_peak + jnp.log(row_total)
    context = jnp.einsum(
        "shqk,skhd->sqhd", attn_weights.astype(bf16), value_rows, preferred_element_type=f32
    )
    context = context.reshape(group, heads_width).astype(bf16)

    def token_blocks(values):
        return [
            lax.dynamic_slice(values, ((r ^ j) * block, 0), (block, values.shape[1]))
            for j in range(rows)
        ]

    attended = row_reduce([dot(b, wo_all, 1, 0) for b in token_blocks(context)]) + bias_out_f
    tokens_own = lax.dynamic_slice(tokens_all, (r * block, 0), (block, width)).astype(f32)
    normed_one, inv_one = normalize(tokens_own + attended)
    hidden_one = normed_one * gain_one_f + shift_one_f

    hidden_all = jnp.concatenate(row_gather(hidden_one.astype(bf16)), 0)
    pre_act = dot(hidden_all, wi_all, 1, 0) + bias_in_f
    normal_cdf = 0.5 * (1.0 + lax.erf(pre_act * 0.7071067811865476))
    activated = (pre_act * normal_cdf).astype(bf16)
    mlp = dot(activated, wb_all, 1, 0)
    mlp_out = row_reduce([mlp[j * block : (j + 1) * block] for j in range(rows)]) + bias_back_f
    normed_two, inv_two = normalize(hidden_one + mlp_out)
    output = row_swap((normed_two * gain_two_f + shift_two_f).astype(bf16), 1, 0)

    d_two = norm_backward(cot, normed_two, inv_two, gain_two_f)
    d_mlp = d_two.astype(bf16)
    d_mlp_all = jnp.concatenate(row_gather(d_mlp), 0)
    d_activated = dot(d_mlp_all, wb_all, 1, 1)
    normal_pdf = jnp.exp(-0.5 * pre_act * pre_act) * 0.3989422804014327
    d_pre = (d_activated * (normal_cdf + pre_act * normal_pdf)).astype(bf16)
    d_hid = dot(d_pre, wi_all, 1, 1)
    d_hidden = d_two + row_reduce([d_hid[j * block : (j + 1) * block] for j in range(rows)])

    grad_wb = dot(activated, d_mlp_all, 0, 0).astype(bf16)
    grad_wb = dp_sum(
        col_reduce([grad_wb[d * hid_piece : (d + 1) * hid_piece] for d in range(cols)])
    )
    grad_w_back = row_swap(grad_wb.astype(bf16), 1, 0).astype(f32)
    grad_wi = dot(hidden_all, d_pre, 0, 0).astype(bf16)
    grad_wi = dp_sum(
        col_reduce([grad_wi[:, d * hid_piece : (d + 1) * hid_piece] for d in range(cols)])
    )
    grad_w_in = row_swap(grad_wi.astype(bf16), 0, 1).astype(f32)

    d_one = norm_backward(d_hidden, normed_one, inv_one, gain_one_f)
    d_att = d_one.astype(bf16)
    d_att_blocks = row_gather(d_att)
    d_att_rel = jnp.concatenate(d_att_blocks, 0)

    def by_position(blocks):
        joint = jnp.concatenate(blocks, 0).reshape(rows, block, -1)
        return jnp.take(joint, r ^ jnp.arange(rows), axis=0).reshape(group, -1)

    d_one_cols = row_swap(d_one, 1, 0)
    d_att_all = by_position(d_att_blocks)
    grad_wo = dot(context, d_att_all, 0, 0).astype(bf16)
    grad_wo = dp_sum(
        col_reduce([grad_wo[d * head_piece : (d + 1) * head_piece] for d in range(cols)])
    )
    grad_w_out = row_swap(grad_wo.astype(bf16), 1, 0).astype(f32)

    vector_grads = jnp.stack(
        [
            jnp.sum(d_att, 0, dtype=f32),
            jnp.sum(d_hidden * normed_one, 0),
            jnp.sum(d_hidden, 0),
            jnp.sum(d_mlp, 0, dtype=f32),
            jnp.sum(cot * normed_two, 0),
            jnp.sum(cot, 0),
        ]
    )

    def from_col(values):
        doubled = jnp.concatenate([values, values])
        start = (cols - c) % cols
        return lax.dynamic_slice_in_dim(doubled, start, cols, 0)

    hid_sums = from_col(jnp.sum(d_pre, 0, dtype=f32).reshape(cols, 1, hid_piece))
    hid_sums = jnp.where(jnp.arange(rows)[None, :, None] == r, hid_sums, 0.0)
    vector_grads, hid_sums = lax.psum((vector_grads, hid_sums), ("dp", "row", "col"))
    vector_grads = lax.dynamic_slice(vector_grads, (0, r * width_local), (6, width_local))
    grad_bias_in = lax.dynamic_slice_in_dim(hid_sums, c, 1, 0).reshape(hid_tile)

    d_context = dot(d_att_all, wo_all, 1, 1).astype(bf16).reshape(seq_shape)
    scores_again = (
        jnp.einsum("sqhd,skhd->shqk", queries, key_rows, preferred_element_type=f32) * score_scale
    )
    weights_again = jnp.exp(scores_again - log_total)
    d_value = jnp.einsum(
        "shqk,sqhd->skhd", weights_again.astype(bf16), d_context, preferred_element_type=f32
    )
    d_weights = jnp.einsum("sqhd,skhd->shqk", d_context, value_rows, preferred_element_type=f32)
    row_inner = jnp.sum(d_weights * weights_again, -1, keepdims=True)
    d_scores = (weights_again * (d_weights - row_inner)).astype(bf16)
    d_query = (
        jnp.einsum("shqk,skhd->sqhd", d_scores, key_rows, preferred_element_type=f32) * score_scale
    )
    d_key = (
        jnp.einsum("shqk,sqhd->skhd", d_scores, queries, preferred_element_type=f32) * score_scale
    )
    d_joined = jnp.concatenate(
        [
            d_query.reshape(group, heads_width),
            d_key.reshape(group, heads_width),
            d_value.reshape(group, heads_width),
        ],
        1,
    ).astype(bf16)
    grad_wq = dot(d_joined, tokens_all, 0, 0).astype(bf16)
    grad_wq = grad_wq.reshape(3, cols, head_piece, width)
    grad_wq = dp_sum(
        col_reduce([grad_wq[:, d].reshape(3 * head_piece, width) for d in range(cols)])
    )
    grad_wq = row_swap(grad_wq.astype(bf16), 1, 0).reshape(rows, 3, head_piece, width_local)
    grad_w_qkv = jnp.transpose(grad_wq, (1, 3, 0, 2)).reshape(3, width_local, heads_tile)
    grad_w_qkv = grad_w_qkv.astype(f32)

    d_tokens = dot(d_joined, wq_all, 1, 0)
    d_tokens = row_reduce(
        [
            lax.dynamic_slice(d_tokens, (0, (r ^ j) * width_local), (group, width_local))
            for j in range(rows)
        ]
    )
    grad_tokens = d_one_cols + d_tokens

    head_sums = jnp.stack(
        [
            jnp.sum(d_joined[:, :heads_width], 0, dtype=f32),
            jnp.sum(d_joined[:, 2 * heads_width :], 0, dtype=f32),
        ],
    ).reshape(2, cols, head_piece)
    head_sums = from_col(jnp.transpose(head_sums, (1, 0, 2))[:, :, None, :])
    head_sums = jnp.where(jnp.arange(rows)[None, None, :, None] == r, head_sums, 0.0)
    head_sums = lax.psum(head_sums, ("dp", "row", "col"))
    grad_bias_qv = lax.dynamic_slice_in_dim(head_sums, c, 1, 0).reshape(2, heads_tile)

    return (
        output,
        grad_tokens,
        grad_w_qkv,
        grad_bias_qv,
        grad_w_out,
        vector_grads[0],
        vector_grads[1],
        vector_grads[2],
        grad_w_in,
        grad_bias_in,
        grad_w_back,
        vector_grads[3],
        vector_grads[4],
        vector_grads[5],
    )


def solution(mesh):
    in_specs = (
        P(("dp", "col"), "row"),
        P(None, "row", "col"),
        P(None, "col"),
        P("col", "row"),
        P("row"),
        P("row"),
        P("row"),
        P("row", "col"),
        P("col"),
        P("col", "row"),
        P("row"),
        P("row"),
        P("row"),
        P(("dp", "col"), "row"),
    )
    out_specs = (
        P(("dp", "col"), "row"),
        P(("dp", "col"), "row"),
        P(None, "row", "col"),
        P(None, "col"),
        P("col", "row"),
        P("row"),
        P("row"),
        P("row"),
        P("row", "col"),
        P("col"),
        P("col", "row"),
        P("row"),
        P("row"),
        P("row"),
    )
    return jax.shard_map(
        per_device, mesh=mesh, in_specs=in_specs, out_specs=out_specs, check_vma=False
    )
```

```python
import jax
import jax.numpy as jnp
from jax import lax
from jax.sharding import PartitionSpec as P

HEAD_DIM = 64
SEQ_LEN = 512
norm_eps = 1e-12

f32 = jnp.float32
bf16 = jnp.bfloat16

REL = (0, 2, 1, 3)


def swap(values, axis, bit):
    size = lax.axis_size(axis)
    return lax.ppermute(values, axis, [(i, i ^ bit) for i in range(size)])


def dot(left, right, left_dim, right_dim):
    return lax.dot_general(
        left, right, (((left_dim,), (right_dim,)), ((), ())), preferred_element_type=f32
    )


def after(values, earlier):
    return lax.optimization_barrier((values, earlier))[0]


def trade(values, axis):
    return lax.all_to_all(values, axis, 0, 0, tiled=True)


def to_rel(values, dim):
    r = lax.axis_index("row")
    size = values.shape[dim] // 4
    parts = [lax.dynamic_slice_in_dim(values, (r ^ j) * size, size, dim) for j in REL]
    return jnp.concatenate(parts, dim)


def from_rel(values, dim):
    r = lax.axis_index("row")
    size = values.shape[dim] // 4
    parts = []
    for a in range(4):
        j = r ^ a
        place = ((j & 1) << 1) | (j >> 1)
        parts.append(lax.dynamic_slice_in_dim(values, place * size, size, dim))
    return jnp.concatenate(parts, dim)


def row_reduce(own, across, beside, diagonal, dim):
    size = own.shape[dim]
    got = swap(jnp.concatenate([beside, diagonal], dim).astype(bf16), "row", 1)
    far = across + lax.slice_in_dim(got, size, 2 * size, axis=dim).astype(f32)
    far = swap(far.astype(bf16), "row", 2)
    return own + lax.slice_in_dim(got, 0, size, axis=dim).astype(f32) + far.astype(f32)


def line_gather(block):
    size, here = lax.axis_size("col"), lax.axis_index("col")
    up, down = [block], [block]
    for step in range(1, size):
        up.append(lax.ppermute(up[-1], "col", [(i, i - 1) for i in range(1, size - step + 1)]))
        down.append(lax.ppermute(down[-1], "col", [(i, i + 1) for i in range(step - 1, size - 1)]))
    blocks = [block] + [
        jnp.where(here + step < size, up[step], down[size - step]) for step in range(1, size)
    ]
    return blocks


def in_col_order(blocks):
    size, here = lax.axis_size("col"), lax.axis_index("col")
    out = jnp.zeros((size,) + blocks[0].shape, blocks[0].dtype)
    for step, b in enumerate(blocks):
        place = (here + step) % size
        out = lax.dynamic_update_slice_in_dim(out, b[None], place, 0)
    return out


def spread(block, axis):
    return trade(jnp.broadcast_to(block[None], (lax.axis_size(axis),) + block.shape), axis)


def normalize(resid):
    row_mean = jnp.mean(resid, 1, keepdims=True)
    centered = resid - row_mean
    variance = jnp.mean(centered * centered, 1, keepdims=True)
    inv_std = lax.rsqrt(variance + norm_eps)
    return centered * inv_std, inv_std


def norm_backward(incoming, normed, inv_std, gain):
    scaled = incoming * gain
    return inv_std * (
        scaled
        - jnp.mean(scaled, 1, keepdims=True)
        - normed * jnp.mean(scaled * normed, 1, keepdims=True)
    )


def dp_sum(values, first_bit):
    size = lax.axis_size("dp")
    bit = first_bit
    while bit < size:
        low = values.astype(bf16)
        values = low.astype(f32) + swap(low, "dp", bit).astype(f32)
        bit *= 2
    return values


def per_device(
    tokens,
    w_qkv,
    bias_qv,
    w_out,
    bias_out,
    gain_one,
    shift_one,
    w_in,
    bias_in,
    w_back,
    bias_back,
    gain_two,
    shift_two,
    cotangent,
):
    rows, cols = lax.axis_size("row"), lax.axis_size("col")
    r, n = lax.axis_index("row"), lax.axis_index("dp") & 1
    dp_size = lax.axis_size("dp")
    group, width_local = tokens.shape
    block = group // rows
    width = width_local * rows
    heads_tile = w_qkv.shape[2]
    head_piece = heads_tile // rows
    heads_width = cols * head_piece
    hid_tile = w_in.shape[1]
    hid_piece = hid_tile // rows
    half = hid_piece // 2
    hid_half = cols * half
    seq_count = group // SEQ_LEN
    head_count = heads_width // HEAD_DIM
    score_scale = HEAD_DIM ** (-0.5)
    seq_shape = (seq_count, SEQ_LEN, head_count, HEAD_DIM)

    wq = jnp.transpose(w_qkv, (2, 0, 1)).reshape(rows, head_piece, 3, width_local)
    wq = trade(jnp.transpose(wq, (0, 2, 1, 3)).reshape(rows, 3 * head_piece, width_local), "row")
    wq = to_rel(jnp.transpose(wq, (1, 0, 2)).reshape(3 * head_piece, width), 1)
    hid_bias = lax.dynamic_slice(bias_in, (r * hid_piece,), (hid_piece,))
    head_bias = lax.dynamic_slice(bias_qv, (0, r * head_piece), (2, head_piece)).reshape(-1)
    bias_row = jnp.concatenate([hid_bias, head_bias])
    bias_rows = jnp.pad(bias_row[None], ((0, 15), (0, width - bias_row.shape[0])))
    line = line_gather(jnp.concatenate([wq, bias_rows], 0))
    wq_all = in_col_order([b[: 3 * head_piece].reshape(3, head_piece, width) for b in line])
    wq_all = jnp.transpose(wq_all, (1, 0, 2, 3)).reshape(3 * heads_width, width)
    col_bias = in_col_order([b[3 * head_piece, : bias_row.shape[0]] for b in line]).astype(f32)
    bias_q = col_bias[:, hid_piece : hid_piece + head_piece].reshape(-1)
    bias_v = col_bias[:, hid_piece + head_piece :].reshape(-1)

    def own_first(values):
        parts = [
            lax.dynamic_slice_in_dim(values, k * half, half, 1).reshape(hid_half)
            for k in (n, 1 - n)
        ]
        return jnp.concatenate(parts)

    bias_in_f = own_first(col_bias[:, :hid_piece])

    across = swap(tokens, "row", 2)
    beside = swap(tokens, "row", 1)
    diagonal = swap(across, "row", 1)
    tokens_all = jnp.concatenate([tokens, across, beside, diagonal], 1)

    wi = jnp.transpose(w_in).reshape(rows, hid_piece, width_local)
    wi = lax.dynamic_slice_in_dim(wi, n * half, half, 1)
    wb = w_back.reshape(rows, hid_piece, width_local)
    wb = lax.dynamic_slice_in_dim(wb, n * half, half, 1)
    wo = w_out.reshape(rows, head_piece, width_local)
    vectors = jnp.stack([bias_out, gain_one, shift_one, bias_back, gain_two, shift_two])
    vectors = jnp.pad(vectors, ((0, 10), (0, 0)))
    vectors = jnp.broadcast_to(vectors[None], (rows,) + vectors.shape)
    mixed = trade(jnp.concatenate([wi, wb, wo, vectors], 1), "row")
    mixed = jnp.transpose(mixed, (1, 0, 2)).reshape(-1, width)
    wi, wb = mixed[:half], mixed[half : 2 * half]
    wo = mixed[2 * half : 2 * half + head_piece]
    vectors = mixed[2 * half + head_piece :].astype(f32)
    bias_out_f, gain_one_f, shift_one_f, bias_back_f, gain_two_f, shift_two_f = [
        vectors[i] for i in range(6)
    ]
    wi = lax.all_gather(wi, "col", axis=0, tiled=True)
    wo_all = spread(after(wo, line[-1]), "col").reshape(heads_width, width)
    wb = spread(after(wb, line[-1]), "col").reshape(hid_half, width)
    wi_all = jnp.concatenate([wi, swap(wi, "dp", 1)], 0)
    wb_all = jnp.concatenate([wb, swap(wb, "dp", 1)], 0)
    cot = after(cotangent, line[-1]).reshape(rows, block, width_local)
    cot = jnp.transpose(trade(cot, "row"), (1, 0, 2)).reshape(block, width).astype(f32)

    joined = dot(tokens_all, wq_all, 1, 1)
    queries = (joined[:, :heads_width] + bias_q).astype(bf16).reshape(seq_shape)
    key_rows = joined[:, heads_width : 2 * heads_width].astype(bf16).reshape(seq_shape)
    value_rows = (joined[:, 2 * heads_width :] + bias_v).astype(bf16).reshape(seq_shape)
    scores = (
        jnp.einsum("sqhd,skhd->shqk", queries, key_rows, preferred_element_type=f32) * score_scale
    )
    row_peak = jnp.max(scores, -1, keepdims=True)
    expo_scores = jnp.exp(scores - row_peak)
    row_total = jnp.sum(expo_scores, -1, keepdims=True)
    attn_weights = expo_scores / row_total
    log_total = row_peak + jnp.log(row_total)
    context = jnp.einsum(
        "shqk,skhd->sqhd", attn_weights.astype(bf16), value_rows, preferred_element_type=f32
    )
    context = to_rel(context.reshape(group, heads_width).astype(bf16), 0)

    send = dot(context[2 * block :], wo_all, 1, 0).astype(bf16)
    keep = dot(context[: 2 * block], wo_all, 1, 0)
    attended = row_reduce(keep[:block], keep[block:], send[:block], send[block:], 0) + bias_out_f
    tokens_own = lax.dynamic_slice_in_dim(tokens_all, r * block, block, 0)
    tokens_own = from_rel(tokens_own, 1).astype(f32)
    normed_one, inv_one = normalize(tokens_own + attended)
    hidden_one = normed_one * gain_one_f + shift_one_f

    def chips(values):
        over = swap(values, "row", 2)
        near = jnp.concatenate([values, swap(values, "row", 1)], 0)
        return near, jnp.concatenate([over, swap(over, "row", 1)], 0)

    def reduce_chips(near, far):
        return row_reduce(near[:block], far[:block], near[block:], far[block:], 0)

    hidden = chips(hidden_one.astype(bf16))
    pre_act, cdf, activated, mlp = [], [], [], []
    for h in hidden:
        pre = dot(h, wi_all, 1, 1) + bias_in_f
        pre_act.append(pre)
        cdf.append(0.5 * (1.0 + lax.erf(pre * 0.7071067811865476)))
        activated.append((pre * cdf[-1]).astype(bf16))
        mlp.append(dot(activated[-1], wb_all, 1, 0))
    mlp_out = reduce_chips(*mlp) + bias_back_f
    normed_two, inv_two = normalize(hidden_one + mlp_out)
    output = (normed_two * gain_two_f + shift_two_f).astype(bf16)

    d_two = norm_backward(cot, normed_two, inv_two, gain_two_f)
    d_mlp_low = d_two.astype(bf16)
    d_mlp = chips(d_mlp_low)
    d_pre, d_hid = [], []
    for k in range(2):
        d_activated = dot(d_mlp[k], wb_all, 1, 1)
        pdf = jnp.exp(-0.5 * pre_act[k] * pre_act[k]) * 0.3989422804014327
        d_pre.append((d_activated * (cdf[k] + pre_act[k] * pdf)).astype(bf16))
        d_hid.append(dot(d_pre[k], wi_all, 1, 0))
    d_hidden = d_two + reduce_chips(*d_hid)
    output = after(output, d_pre[0])
    output = lax.all_to_all(output, "row", 1, 0, tiled=True)

    def hidden_grad(left, right):
        other = sum(dot(a[:, hid_half:], b, 0, 0) for a, b in zip(left, right))
        own = sum(dot(a[:, :hid_half], b, 0, 0) for a, b in zip(left, right))
        total = own + swap(other.astype(bf16), "dp", 1).astype(f32)
        return trade(total.astype(bf16).reshape(cols, half, width), "col")

    grad_wb = hidden_grad(activated, d_mlp)
    grad_wi = hidden_grad(d_pre, hidden)
    hid_grads = jnp.stack(
        [jnp.sum(grad_wb.astype(f32), 0), jnp.sum(grad_wi.astype(f32), 0)], 0
    )
    hid_grads = dp_sum(hid_grads, 2).astype(bf16)
    others = swap(hid_grads, "dp", 1)
    hid_grads = jnp.concatenate(
        [jnp.where(n == 0, hid_grads, others), jnp.where(n == 0, others, hid_grads)], 1
    )
    hid_grads = lax.all_to_all(hid_grads, "row", 2, 1, tiled=True).astype(f32)
    grad_w_back, grad_w_in = hid_grads[0], jnp.transpose(hid_grads[1])

    d_one = norm_backward(d_hidden, normed_one, inv_one, gain_one_f)
    d_att = d_one.astype(bf16)
    over = swap(d_att, "row", 2)
    d_att_all = jnp.concatenate([d_att, over, swap(d_att, "row", 1), swap(over, "row", 1)], 0)
    d_one_cols = lax.all_to_all(after(d_one, over), "row", 1, 0, tiled=True)

    def by_owner(values):
        each = values.shape[-2]
        parts = values.reshape(cols, each, rows, width_local)
        got = trade(jnp.transpose(parts, (2, 0, 1, 3)).reshape(-1, each, width_local), ("row", "col"))
        got = jnp.sum(got.reshape(rows, cols, each, width_local).astype(f32), 1)
        return dp_sum(got, 1)

    grad_wo = dot(context, d_att_all, 0, 0).astype(bf16).reshape(cols, head_piece, width)
    grad_w_out = by_owner(grad_wo).reshape(heads_tile, width_local)

    d_context = from_rel(dot(d_att_all, wo_all, 1, 1).astype(bf16), 0).reshape(seq_shape)
    scores_again = (
        jnp.einsum("sqhd,skhd->shqk", queries, key_rows, preferred_element_type=f32) * score_scale
    )
    weights_again = jnp.exp(scores_again - log_total)
    d_value = jnp.einsum(
        "shqk,sqhd->skhd", weights_again.astype(bf16), d_context, preferred_element_type=f32
    )
    d_weights = jnp.einsum("sqhd,skhd->shqk", d_context, value_rows, preferred_element_type=f32)
    row_inner = jnp.sum(d_weights * weights_again, -1, keepdims=True)
    d_scores = (weights_again * (d_weights - row_inner)).astype(bf16)
    d_query = (
        jnp.einsum("shqk,skhd->sqhd", d_scores, key_rows, preferred_element_type=f32) * score_scale
    )
    d_key = (
        jnp.einsum("shqk,sqhd->skhd", d_scores, queries, preferred_element_type=f32) * score_scale
    )
    d_joined = jnp.concatenate(
        [
            d_query.reshape(group, heads_width),
            d_key.reshape(group, heads_width),
            d_value.reshape(group, heads_width),
        ],
        1,
    ).astype(bf16)
    grad_wq = dot(d_joined, tokens_all, 0, 0).astype(bf16)
    grad_wq = from_rel(grad_wq, 1).reshape(3, cols, head_piece, width)
    grad_wq = jnp.transpose(grad_wq, (1, 0, 2, 3)).reshape(cols, 3 * head_piece, width)
    grad_wq = by_owner(grad_wq).reshape(rows, 3, head_piece, width_local)
    grad_w_qkv = jnp.transpose(grad_wq, (1, 3, 0, 2)).reshape(3, width_local, heads_tile)

    split = 2 * width_local
    keep = dot(d_joined, wq_all[:, :split], 1, 0)
    send = dot(d_joined, wq_all[:, split:], 1, 0).astype(bf16)
    d_tokens = row_reduce(
        keep[:, :width_local],
        keep[:, width_local:],
        send[:, :width_local],
        send[:, width_local:],
        1,
    )
    grad_tokens = d_one_cols + d_tokens

    vector_grads = jnp.stack(
        [
            jnp.sum(d_att, 0, dtype=f32),
            jnp.sum(d_hidden * normed_one, 0),
            jnp.sum(d_hidden, 0),
            jnp.sum(d_mlp_low, 0, dtype=f32),
            jnp.sum(cot * normed_two, 0),
            jnp.sum(cot, 0),
        ]
    )
    vector_grads = jnp.transpose(vector_grads.reshape(6, rows, width_local), (1, 0, 2))
    hid_sums = sum(jnp.sum(d, 0, dtype=f32) for d in d_pre).reshape(2, cols, 1, half)
    hid_sums = [jnp.where(n == k, hid_sums[0], hid_sums[1]) for k in range(2)]
    hid_sums = jnp.concatenate(hid_sums, 2)
    head_sums = jnp.sum(d_joined.reshape(group, 3, cols, head_piece), 0, dtype=f32)
    head_sums = jnp.concatenate([head_sums[0], head_sums[2]], 1)
    head_sums = jnp.pad(head_sums, ((0, 0), (0, hid_piece - 2 * head_piece)))[:, None]
    col_sums = jnp.concatenate([hid_sums, head_sums], 1)
    small = jnp.concatenate(
        [
            jnp.broadcast_to(vector_grads[:, None], (rows, cols, 6, width_local)),
            jnp.broadcast_to(col_sums[None], (rows, cols, 2, width_local)),
        ],
        2,
    )
    small = jnp.broadcast_to(small[None], (dp_size,) + small.shape)
    small = trade(small.reshape(-1, 8, width_local), ("dp", "row", "col"))
    small = small.reshape(dp_size, rows, cols, 8, width_local)
    vector_grads = jnp.sum(small[:, :, :, :6], (0, 1, 2))
    col_sums = jnp.sum(small[:, :, :, 6:], (0, 2))
    grad_bias_in = col_sums[:, 0].reshape(hid_tile)
    grad_bias_qv = jnp.stack(
        [
            col_sums[:, 1, :head_piece].reshape(heads_tile),
            col_sums[:, 1, head_piece : 2 * head_piece].reshape(heads_tile),
        ]
    )

    return (
        output,
        grad_tokens,
        grad_w_qkv,
        grad_bias_qv,
        grad_w_out,
        vector_grads[0],
        vector_grads[1],
        vector_grads[2],
        grad_w_in,
        grad_bias_in,
        grad_w_back,
        vector_grads[3],
        vector_grads[4],
        vector_grads[5],
    )


def solution(mesh):
    in_specs = (
        P(("dp", "col"), "row"),
        P(None, "row", "col"),
        P(None, "col"),
        P("col", "row"),
        P("row"),
        P("row"),
        P("row"),
        P("row", "col"),
        P("col"),
        P("col", "row"),
        P("row"),
        P("row"),
        P("row"),
        P(("dp", "col"), "row"),
    )
    out_specs = (
        P(("dp", "col"), "row"),
        P(("dp", "col"), "row"),
        P(None, "row", "col"),
        P(None, "col"),
        P("col", "row"),
        P("row"),
        P("row"),
        P("row"),
        P("row", "col"),
        P("col"),
        P("col", "row"),
        P("row"),
        P("row"),
        P("row"),
    )
    return jax.shard_map(
        per_device, mesh=mesh, in_specs=in_specs, out_specs=out_specs, check_vma=False
    )
```

```python
import jax
import jax.numpy as jnp
from jax import lax
from jax.sharding import PartitionSpec as P

HEAD_DIM = 64
SEQ_LEN = 512
norm_eps = 1e-12

f32 = jnp.float32
bf16 = jnp.bfloat16

REL = (0, 2, 1, 3)


def swap(values, axis, bit):
    size = lax.axis_size(axis)
    return lax.ppermute(values, axis, [(i, i ^ bit) for i in range(size)])


def dot(left, right, left_dim, right_dim):
    return lax.dot_general(
        left, right, (((left_dim,), (right_dim,)), ((), ())), preferred_element_type=f32
    )


def after(values, earlier):
    return lax.optimization_barrier((values, earlier))[0]


def trade(values, axis):
    return lax.all_to_all(values, axis, 0, 0, tiled=True)


def to_rel(values, dim):
    r = lax.axis_index("row")
    size = values.shape[dim] // 4
    parts = [lax.dynamic_slice_in_dim(values, (r ^ j) * size, size, dim) for j in REL]
    return jnp.concatenate(parts, dim)


def from_rel(values, dim):
    r = lax.axis_index("row")
    size = values.shape[dim] // 4
    parts = []
    for a in range(4):
        j = r ^ a
        place = ((j & 1) << 1) | (j >> 1)
        parts.append(lax.dynamic_slice_in_dim(values, place * size, size, dim))
    return jnp.concatenate(parts, dim)


def row_reduce(own, across, beside, diagonal, dim):
    size = own.shape[dim]
    got = swap(jnp.concatenate([beside, diagonal], dim).astype(bf16), "row", 1)
    far = across + lax.slice_in_dim(got, size, 2 * size, axis=dim).astype(f32)
    far = swap(far.astype(bf16), "row", 2)
    return own + lax.slice_in_dim(got, 0, size, axis=dim).astype(f32) + far.astype(f32)


def line_gather(block, gate):
    size, here = lax.axis_size("col"), lax.axis_index("col")
    up, down = [block], [block]
    for step in range(1, size):
        up.append(lax.ppermute(up[-1], "col", [(i, i - 1) for i in range(1, size - step + 1)]))
        down.append(lax.ppermute(down[-1], "col", [(i, i + 1) for i in range(step - 1, size - 1)]))
        if step == 1:
            up[1], down[1], _ = lax.optimization_barrier((up[1], down[1], gate))
    blocks = [block] + [
        jnp.where(here + step < size, up[step], down[size - step]) for step in range(1, size)
    ]
    return blocks


def in_col_order(blocks):
    size, here = lax.axis_size("col"), lax.axis_index("col")
    out = jnp.zeros((size,) + blocks[0].shape, blocks[0].dtype)
    for step, b in enumerate(blocks):
        place = (here + step) % size
        out = lax.dynamic_update_slice_in_dim(out, b[None], place, 0)
    return out


def spread(block, axis):
    return trade(jnp.broadcast_to(block[None], (lax.axis_size(axis),) + block.shape), axis)


def normalize(resid):
    row_mean = jnp.mean(resid, 1, keepdims=True)
    centered = resid - row_mean
    variance = jnp.mean(centered * centered, 1, keepdims=True)
    inv_std = lax.rsqrt(variance + norm_eps)
    return centered * inv_std, inv_std


def norm_backward(incoming, normed, inv_std, gain):
    scaled = incoming * gain
    return inv_std * (
        scaled
        - jnp.mean(scaled, 1, keepdims=True)
        - normed * jnp.mean(scaled * normed, 1, keepdims=True)
    )


def dp_sum(values, first_bit):
    size = lax.axis_size("dp")
    bit = first_bit
    while bit < size:
        low = values.astype(bf16)
        values = low.astype(f32) + swap(low, "dp", bit).astype(f32)
        bit *= 2
    return values


def per_device(
    tokens,
    w_qkv,
    bias_qv,
    w_out,
    bias_out,
    gain_one,
    shift_one,
    w_in,
    bias_in,
    w_back,
    bias_back,
    gain_two,
    shift_two,
    cotangent,
):
    rows, cols = lax.axis_size("row"), lax.axis_size("col")
    r, n = lax.axis_index("row"), lax.axis_index("dp") & 1
    dp_size = lax.axis_size("dp")
    group, width_local = tokens.shape
    block = group // rows
    width = width_local * rows
    heads_tile = w_qkv.shape[2]
    head_piece = heads_tile // rows
    heads_width = cols * head_piece
    hid_tile = w_in.shape[1]
    hid_piece = hid_tile // rows
    half = hid_piece // 2
    hid_half = cols * half
    seq_count = group // SEQ_LEN
    head_count = heads_width // HEAD_DIM
    score_scale = HEAD_DIM ** (-0.5)
    seq_shape = (seq_count, SEQ_LEN, head_count, HEAD_DIM)

    heads_rows = 3 * head_piece
    wq = jnp.transpose(w_qkv, (2, 0, 1)).reshape(rows, head_piece, 3, width_local)
    wq = jnp.transpose(wq, (0, 2, 1, 3)).reshape(rows, heads_rows, width_local)
    wo = w_out.reshape(rows, head_piece, width_local)
    first = trade(jnp.concatenate([wq, wo], 1), "row")
    first = jnp.transpose(first, (1, 0, 2)).reshape(-1, width)
    first = jnp.concatenate([to_rel(first[:heads_rows], 1), first[heads_rows:]], 0)
    hid_bias = lax.dynamic_slice(bias_in, (r * hid_piece,), (hid_piece,))
    head_bias = lax.dynamic_slice(bias_qv, (0, r * head_piece), (2, head_piece)).reshape(-1)
    bias_row = jnp.concatenate([hid_bias, head_bias])
    bias_rows = jnp.pad(bias_row[None], ((0, 15), (0, width - bias_row.shape[0])))

    wi = jnp.transpose(w_in).reshape(rows, hid_piece, width_local)
    wi = lax.dynamic_slice_in_dim(wi, n * half, half, 1)
    wb = w_back.reshape(rows, hid_piece, width_local)
    wb = lax.dynamic_slice_in_dim(wb, n * half, half, 1)
    vectors = jnp.stack([bias_out, gain_one, shift_one, bias_back, gain_two, shift_two])
    vectors = jnp.pad(vectors, ((0, 10), (0, 0)))
    vectors = jnp.broadcast_to(vectors[None], (rows,) + vectors.shape)
    mixed = trade(after(jnp.concatenate([wi, wb, vectors], 1), first), "row")
    mixed = jnp.transpose(mixed, (1, 0, 2)).reshape(-1, width)
    wi, wb = mixed[:half], mixed[half : 2 * half]
    vectors = mixed[2 * half :].astype(f32)
    bias_out_f, gain_one_f, shift_one_f, bias_back_f, gain_two_f, shift_two_f = [
        vectors[i] for i in range(6)
    ]

    def both_halves(mine):
        other = swap(mine, "dp", 1)
        return jnp.concatenate([jnp.where(n == 0, mine, other), jnp.where(n == 0, other, mine)], 0)

    line = line_gather(jnp.concatenate([first, bias_rows], 0), wi)
    wi = spread(wi, "col").reshape(hid_half, width)
    wq_all = in_col_order([b[:heads_rows].reshape(3, head_piece, width) for b in line])
    wq_all = jnp.transpose(wq_all, (1, 0, 2, 3)).reshape(3 * heads_width, width)
    bias_at = heads_rows + head_piece
    wo_all = in_col_order([b[heads_rows:bias_at] for b in line]).reshape(heads_width, width)
    col_bias = in_col_order([b[bias_at, : bias_row.shape[0]] for b in line]).astype(f32)
    bias_q = col_bias[:, hid_piece : hid_piece + head_piece].reshape(-1)
    bias_v = col_bias[:, hid_piece + head_piece :].reshape(-1)
    bias_in_f = jnp.transpose(col_bias[:, :hid_piece].reshape(cols, 2, half), (1, 0, 2)).reshape(-1)

    across = swap(tokens, "row", 2)
    beside = swap(tokens, "row", 1)
    diagonal = swap(across, "row", 1)
    tokens_all = jnp.concatenate([tokens, across, beside, diagonal], 1)

    wb = spread(after(wb, line[-1]), "col").reshape(hid_half, width)
    tokens_all, wi = lax.optimization_barrier((tokens_all, wi))
    wi_all = both_halves(wi)
    cot = after(cotangent, wb).reshape(rows, block, width_local)
    cot = jnp.transpose(trade(cot, "row"), (1, 0, 2)).reshape(block, width).astype(f32)

    joined = dot(tokens_all, wq_all, 1, 1)
    queries = (joined[:, :heads_width] + bias_q).astype(bf16).reshape(seq_shape)
    key_rows = joined[:, heads_width : 2 * heads_width].astype(bf16).reshape(seq_shape)
    value_rows = (joined[:, 2 * heads_width :] + bias_v).astype(bf16).reshape(seq_shape)
    scores = (
        jnp.einsum("sqhd,skhd->shqk", queries, key_rows, preferred_element_type=f32) * score_scale
    )
    row_peak = jnp.max(scores, -1, keepdims=True)
    expo_scores = jnp.exp(scores - row_peak)
    row_total = jnp.sum(expo_scores, -1, keepdims=True)
    attn_weights = expo_scores / row_total
    log_total = row_peak + jnp.log(row_total)
    context = jnp.einsum(
        "shqk,skhd->sqhd", attn_weights.astype(bf16), value_rows, preferred_element_type=f32
    )
    context, wb, wi_all = lax.optimization_barrier((context, wb, wi_all))
    wb_all = both_halves(wb)
    context = to_rel(context.reshape(group, heads_width).astype(bf16), 0)

    send = dot(context[2 * block :], wo_all, 1, 0).astype(bf16)
    keep = dot(context[: 2 * block], wo_all, 1, 0)
    attended = row_reduce(keep[:block], keep[block:], send[:block], send[block:], 0) + bias_out_f
    tokens_own = lax.dynamic_slice_in_dim(tokens_all, r * block, block, 0)
    tokens_own = from_rel(tokens_own, 1).astype(f32)
    normed_one, inv_one = normalize(tokens_own + attended)
    hidden_one = normed_one * gain_one_f + shift_one_f

    def chips(values):
        over = swap(values, "row", 2)
        near = jnp.concatenate([values, swap(values, "row", 1)], 0)
        return near, jnp.concatenate([over, swap(over, "row", 1)], 0)

    def reduce_chips(near, far):
        return row_reduce(near[:block], far[:block], near[block:], far[block:], 0)

    hidden = chips(hidden_one.astype(bf16))
    pre_act, cdf, activated, mlp = [], [], [], []
    for h in hidden:
        pre = dot(h, wi_all, 1, 1) + bias_in_f
        pre_act.append(pre)
        cdf.append(0.5 * (1.0 + lax.erf(pre * 0.7071067811865476)))
        activated.append((pre * cdf[-1]).astype(bf16))
        mlp.append(dot(activated[-1], wb_all, 1, 0))
    mlp_out = reduce_chips(*mlp) + bias_back_f
    normed_two, inv_two = normalize(hidden_one + mlp_out)
    output = (normed_two * gain_two_f + shift_two_f).astype(bf16)

    d_two = norm_backward(cot, normed_two, inv_two, gain_two_f)
    d_mlp_low = d_two.astype(bf16)
    d_mlp = chips(d_mlp_low)
    d_pre, d_hid = [], []
    for k in range(2):
        d_activated = dot(d_mlp[k], wb_all, 1, 1)
        pdf = jnp.exp(-0.5 * pre_act[k] * pre_act[k]) * 0.3989422804014327
        d_pre.append((d_activated * (cdf[k] + pre_act[k] * pdf)).astype(bf16))
        d_hid.append(dot(d_pre[k], wi_all, 1, 0))
    d_hidden = d_two + reduce_chips(*d_hid)
    def hidden_grad(left, right):
        def one(k):
            picked = [lax.dynamic_slice_in_dim(a, k * hid_half, hid_half, 1) for a in left]
            return sum(dot(a, b, 0, 0) for a, b in zip(picked, right))

        other = swap(one(1 - n).astype(bf16), "dp", 1)
        return (one(n) + other.astype(f32)).astype(bf16).reshape(cols, half, width)

    grad_wb = hidden_grad(activated, d_mlp)
    grad_wi = hidden_grad(d_pre, hidden)
    hid_grads = jnp.concatenate([grad_wb, grad_wi], 1).reshape(-1, width)
    hid_grads = lax.psum_scatter(hid_grads, "col", scatter_dimension=0, tiled=True)
    hid_grads = dp_sum(hid_grads, 2).astype(bf16)
    hid_grads = both_halves(hid_grads.reshape(1, 2, half, width))
    hid_grads = jnp.transpose(hid_grads, (1, 0, 2, 3)).reshape(2 * hid_piece, width)
    hid_grads = jnp.concatenate([hid_grads, output], 0).reshape(-1, rows, width_local)
    hid_grads = trade(jnp.transpose(hid_grads, (1, 0, 2)), "row")
    output = hid_grads[:, 2 * hid_piece :].reshape(group, width_local)
    grad_w_back = hid_grads[:, :hid_piece].reshape(hid_tile, width_local).astype(f32)
    grad_w_in = hid_grads[:, hid_piece : 2 * hid_piece].reshape(hid_tile, width_local)
    grad_w_in = jnp.transpose(grad_w_in).astype(f32)

    d_one = norm_backward(d_hidden, normed_one, inv_one, gain_one_f)
    d_att = d_one.astype(bf16)
    over = swap(d_att, "row", 2)
    d_att_all = jnp.concatenate([d_att, over, swap(d_att, "row", 1), swap(over, "row", 1)], 0)

    def by_owner(values):
        each = values.shape[1]
        got = jnp.transpose(values, (2, 0, 1, 3)).reshape(-1, each, width_local)
        got = trade(got, ("row", "col"))
        got = jnp.sum(got.reshape(rows, cols, each, width_local).astype(f32), 1)
        return dp_sum(got, 1)

    grad_wo = dot(context, d_att_all, 0, 0).astype(bf16).reshape(cols, head_piece, rows, width_local)
    grad_w_out = by_owner(grad_wo).reshape(heads_tile, width_local)

    d_context = from_rel(dot(d_att_all, wo_all, 1, 1).astype(bf16), 0).reshape(seq_shape)
    scores_again = (
        jnp.einsum("sqhd,skhd->shqk", queries, key_rows, preferred_element_type=f32) * score_scale
    )
    weights_again = jnp.exp(scores_again - log_total)
    d_value = jnp.einsum(
        "shqk,sqhd->skhd", weights_again.astype(bf16), d_context, preferred_element_type=f32
    )
    d_weights = jnp.einsum("sqhd,skhd->shqk", d_context, value_rows, preferred_element_type=f32)
    row_inner = jnp.sum(d_weights * weights_again, -1, keepdims=True)
    d_scores = (weights_again * (d_weights - row_inner)).astype(bf16)
    d_query = (
        jnp.einsum("shqk,skhd->sqhd", d_scores, key_rows, preferred_element_type=f32) * score_scale
    )
    d_key = (
        jnp.einsum("shqk,sqhd->skhd", d_scores, queries, preferred_element_type=f32) * score_scale
    )
    d_joined = jnp.concatenate(
        [
            d_query.reshape(group, heads_width),
            d_key.reshape(group, heads_width),
            d_value.reshape(group, heads_width),
        ],
        1,
    ).astype(bf16)
    grad_wq = dot(d_joined, tokens_all, 0, 0).astype(bf16)
    grad_wq = from_rel(grad_wq, 1).reshape(3, cols, head_piece, width)
    grad_wq = jnp.transpose(grad_wq, (1, 0, 2, 3)).reshape(cols, heads_rows, rows, width_local)
    head_sums = jnp.sum(d_joined.reshape(group, 3, cols, head_piece), 0, dtype=f32)
    head_sums = jnp.concatenate([head_sums[0], head_sums[2]], 1).astype(bf16)
    head_sums = jnp.pad(head_sums, ((0, 0), (0, width_local - 2 * head_piece)))
    head_sums = jnp.broadcast_to(head_sums[:, None, None], (cols, 16, rows, width_local))
    grad_wq = by_owner(jnp.concatenate([grad_wq, head_sums], 1))
    head_sums = grad_wq[:, heads_rows, : 2 * head_piece].reshape(rows, 2, head_piece)
    grad_bias_qv = jnp.transpose(head_sums, (1, 0, 2)).reshape(2, heads_tile)
    grad_wq = grad_wq[:, :heads_rows].reshape(rows, 3, head_piece, width_local)
    grad_w_qkv = jnp.transpose(grad_wq, (1, 3, 0, 2)).reshape(3, width_local, heads_tile)

    split = 2 * width_local
    d_one_rel = to_rel(d_one, 1)
    own_rows = (jnp.arange(rows) == r)[:, None, None]

    def with_own(values, own):
        values = values.reshape(rows, block, split)
        return (values + jnp.where(own_rows, own[None], 0.0)).reshape(group, split)

    keep = with_own(dot(d_joined, wq_all[:, :split], 1, 0), d_one_rel[:, :split])
    send = with_own(dot(d_joined, wq_all[:, split:], 1, 0), d_one_rel[:, split:]).astype(bf16)
    grad_tokens = row_reduce(
        keep[:, :width_local],
        keep[:, width_local:],
        send[:, :width_local],
        send[:, width_local:],
        1,
    )

    vector_grads = jnp.stack(
        [
            jnp.sum(d_att, 0, dtype=f32),
            jnp.sum(d_hidden * normed_one, 0),
            jnp.sum(d_hidden, 0),
            jnp.sum(d_mlp_low, 0, dtype=f32),
            jnp.sum(cot * normed_two, 0),
            jnp.sum(cot, 0),
        ]
    )
    vector_grads = jnp.transpose(vector_grads.reshape(6, rows, width_local), (1, 0, 2))
    hid_sums = sum(jnp.sum(d, 0, dtype=f32) for d in d_pre).reshape(2, cols, half)
    hid_sums = jnp.transpose(hid_sums, (1, 0, 2)).reshape(1, cols, 1, hid_piece)
    small = jnp.concatenate(
        [
            jnp.broadcast_to(vector_grads[:, None], (rows, cols, 6, width_local)),
            jnp.broadcast_to(hid_sums, (rows, cols, 2, width_local)),
        ],
        2,
    )
    small = jnp.broadcast_to(small[None], (dp_size,) + small.shape)
    small = trade(small.reshape(-1, 8, width_local), ("dp", "row", "col"))
    small = small.reshape(dp_size, rows, cols, 8, width_local)
    vector_grads = jnp.sum(small[:, :, :, :6], (0, 1, 2))
    grad_bias_in = jnp.sum(small[:, :, :, 6], (0, 2)).reshape(hid_tile)

    return (
        output,
        grad_tokens,
        grad_w_qkv,
        grad_bias_qv,
        grad_w_out,
        vector_grads[0],
        vector_grads[1],
        vector_grads[2],
        grad_w_in,
        grad_bias_in,
        grad_w_back,
        vector_grads[3],
        vector_grads[4],
        vector_grads[5],
    )


def solution(mesh):
    in_specs = (
        P(("dp", "col"), "row"),
        P(None, "row", "col"),
        P(None, "col"),
        P("col", "row"),
        P("row"),
        P("row"),
        P("row"),
        P("row", "col"),
        P("col"),
        P("col", "row"),
        P("row"),
        P("row"),
        P("row"),
        P(("dp", "col"), "row"),
    )
    out_specs = (
        P(("dp", "col"), "row"),
        P(("dp", "col"), "row"),
        P(None, "row", "col"),
        P(None, "col"),
        P("col", "row"),
        P("row"),
        P("row"),
        P("row"),
        P("row", "col"),
        P("col"),
        P("col", "row"),
        P("row"),
        P("row"),
        P("row"),
    )
    return jax.shard_map(
        per_device, mesh=mesh, in_specs=in_specs, out_specs=out_specs, check_vma=False
    )
```

```python
import jax
import jax.numpy as jnp
from jax import lax
from jax.sharding import PartitionSpec as P

HEAD_DIM = 64
SEQ_LEN = 512
norm_eps = 1e-12

f32 = jnp.float32
bf16 = jnp.bfloat16

REL = (0, 2, 1, 3)


def swap(values, axis, bit):
    size = lax.axis_size(axis)
    return lax.ppermute(values, axis, [(i, i ^ bit) for i in range(size)])


def dot(left, right, left_dim, right_dim):
    return lax.dot_general(
        left, right, (((left_dim,), (right_dim,)), ((), ())), preferred_element_type=f32
    )


def after(values, earlier):
    return lax.optimization_barrier((values, earlier))[0]


def trade(values, axis):
    return lax.all_to_all(values, axis, 0, 0, tiled=True)


def to_rel(values, dim):
    r = lax.axis_index("row")
    size = values.shape[dim] // 4
    parts = [lax.dynamic_slice_in_dim(values, (r ^ j) * size, size, dim) for j in REL]
    return jnp.concatenate(parts, dim)


def from_rel(values, dim):
    r = lax.axis_index("row")
    size = values.shape[dim] // 4
    parts = []
    for a in range(4):
        j = r ^ a
        place = ((j & 1) << 1) | (j >> 1)
        parts.append(lax.dynamic_slice_in_dim(values, place * size, size, dim))
    return jnp.concatenate(parts, dim)


def row_reduce(own, across, beside, diagonal, dim, gates=(None, None)):
    size = own.shape[dim]
    got = swap(jnp.concatenate([beside, diagonal], dim).astype(bf16), "row", 1)
    first = second = None
    if gates[0] is not None:
        got, first = lax.optimization_barrier((got, gates[0]))
    far = across + lax.slice_in_dim(got, size, 2 * size, axis=dim).astype(f32)
    far = swap(far.astype(bf16), "row", 2)
    if gates[1] is not None:
        second = gates[1](first)
        far, second = lax.optimization_barrier((far, second))
    total = own + lax.slice_in_dim(got, 0, size, axis=dim).astype(f32) + far.astype(f32)
    return total if gates[1] is None else (total, second)


def line_step(up, down, step):
    size = lax.axis_size("col")
    return (
        lax.ppermute(up, "col", [(i, i - 1) for i in range(1, size - step + 1)]),
        lax.ppermute(down, "col", [(i, i + 1) for i in range(step - 1, size - 1)]),
    )


def line_blocks(steps):
    size, here = lax.axis_size("col"), lax.axis_index("col")
    return [
        jnp.where(here + k < size, steps[k][0], steps[size - k][1]) for k in range(1, size)
    ]


def col_rolled(values, sign):
    size, here = lax.axis_size("col"), lax.axis_index("col")
    parts = [
        lax.dynamic_slice_in_dim(values, (k + sign * here + size) % size, 1, 0)
        for k in range(size)
    ]
    return jnp.concatenate(parts, 0)


def in_col_order(blocks):
    size, here = lax.axis_size("col"), lax.axis_index("col")
    out = jnp.zeros((size,) + blocks[0].shape, blocks[0].dtype)
    for step, b in enumerate(blocks):
        place = (here + step) % size
        out = lax.dynamic_update_slice_in_dim(out, b[None], place, 0)
    return out


def spread(block, axis):
    return trade(jnp.broadcast_to(block[None], (lax.axis_size(axis),) + block.shape), axis)


def normalize(resid):
    row_mean = jnp.mean(resid, 1, keepdims=True)
    centered = resid - row_mean
    variance = jnp.mean(centered * centered, 1, keepdims=True)
    inv_std = lax.rsqrt(variance + norm_eps)
    return centered * inv_std, inv_std


def norm_backward(incoming, normed, inv_std, gain):
    scaled = incoming * gain
    return inv_std * (
        scaled
        - jnp.mean(scaled, 1, keepdims=True)
        - normed * jnp.mean(scaled * normed, 1, keepdims=True)
    )


def dp_sum(values, first_bit):
    size = lax.axis_size("dp")
    bit = first_bit
    while bit < size:
        low = values.astype(bf16)
        values = low.astype(f32) + swap(low, "dp", bit).astype(f32)
        bit *= 2
    return values


def per_device(
    tokens,
    w_qkv,
    bias_qv,
    w_out,
    bias_out,
    gain_one,
    shift_one,
    w_in,
    bias_in,
    w_back,
    bias_back,
    gain_two,
    shift_two,
    cotangent,
):
    rows, cols = lax.axis_size("row"), lax.axis_size("col")
    r, n = lax.axis_index("row"), lax.axis_index("dp") & 1
    dp_size = lax.axis_size("dp")
    group, width_local = tokens.shape
    block = group // rows
    width = width_local * rows
    heads_tile = w_qkv.shape[2]
    head_piece = heads_tile // rows
    heads_width = cols * head_piece
    hid_tile = w_in.shape[1]
    hid_piece = hid_tile // rows
    half = hid_piece // 2
    hid_half = cols * half
    seq_count = group // SEQ_LEN
    head_count = heads_width // HEAD_DIM
    score_scale = HEAD_DIM ** (-0.5)
    seq_shape = (seq_count, SEQ_LEN, head_count, HEAD_DIM)

    heads_rows = 3 * head_piece
    wq = jnp.transpose(w_qkv, (2, 0, 1)).reshape(rows, head_piece, 3, width_local)
    wq = jnp.transpose(wq, (0, 2, 1, 3)).reshape(rows, heads_rows, width_local)
    wo = w_out.reshape(rows, head_piece, width_local)
    first = trade(jnp.concatenate([wq, wo], 1), "row")
    first = jnp.transpose(first, (1, 0, 2)).reshape(-1, width)
    first = jnp.concatenate([to_rel(first[:heads_rows], 1), first[heads_rows:]], 0)
    hid_bias = lax.dynamic_slice(bias_in, (r * hid_piece,), (hid_piece,))
    head_bias = lax.dynamic_slice(bias_qv, (0, r * head_piece), (2, head_piece)).reshape(-1)
    bias_row = jnp.concatenate([hid_bias, head_bias])
    bias_rows = jnp.pad(bias_row[None], ((0, 15), (0, width - bias_row.shape[0])))

    wi = jnp.transpose(w_in).reshape(rows, hid_piece, width_local)
    wi = lax.dynamic_slice_in_dim(wi, n * half, half, 1)
    wb = w_back.reshape(rows, hid_piece, width_local)
    wb = lax.dynamic_slice_in_dim(wb, n * half, half, 1)
    vectors = jnp.stack([bias_out, gain_one, shift_one, bias_back, gain_two, shift_two])
    vectors = jnp.pad(vectors, ((0, 10), (0, 0)))
    vectors = jnp.broadcast_to(vectors[None], (rows,) + vectors.shape)
    mixed = trade(after(jnp.concatenate([wi, wb, vectors], 1), first), "row")
    mixed = jnp.transpose(mixed, (1, 0, 2)).reshape(-1, width)
    vectors = mixed[2 * half :].astype(f32)
    bias_out_f, gain_one_f, shift_one_f, bias_back_f, gain_two_f, shift_two_f = [
        vectors[i] for i in range(6)
    ]

    def both_halves(mine):
        other = swap(mine, "dp", 1)
        return jnp.concatenate([jnp.where(n == 0, mine, other), jnp.where(n == 0, other, mine)], 0)

    begin = jnp.concatenate([first, bias_rows], 0)
    steps = [(begin, begin)]
    steps.append(line_step(*steps[0], 1))
    steps[1], mixed = lax.optimization_barrier((steps[1], mixed))
    steps.append(line_step(*steps[1], 2))
    steps.append(line_step(*steps[2], 3))
    line = [begin] + line_blocks(steps)
    wq_all = in_col_order([b[:heads_rows].reshape(3, head_piece, width) for b in line])
    wq_all = jnp.transpose(wq_all, (1, 0, 2, 3)).reshape(3 * heads_width, width)
    bias_at = heads_rows + head_piece
    wo_all = in_col_order([b[heads_rows:bias_at] for b in line]).reshape(heads_width, width)
    col_bias = in_col_order([b[bias_at, : bias_row.shape[0]] for b in line]).astype(f32)
    bias_q = col_bias[:, hid_piece : hid_piece + head_piece].reshape(-1)
    bias_v = col_bias[:, hid_piece + head_piece :].reshape(-1)
    bias_in_f = col_rolled(col_bias[:, :hid_piece], 1).reshape(cols, 2, half)
    bias_in_f = jnp.where(n == 0, bias_in_f, bias_in_f[:, ::-1])
    bias_in_f = jnp.transpose(bias_in_f, (1, 0, 2)).reshape(-1)

    across = swap(tokens, "row", 2)
    beside = swap(tokens, "row", 1)
    diagonal = swap(across, "row", 1)
    tokens_all = jnp.concatenate([tokens, across, beside, diagonal], 1)

    wide, _ = lax.optimization_barrier((mixed[: 2 * half], steps[3]))
    wide_own = swap(wide, "dp", 1)
    wide_steps = [(wide, wide), line_step(wide, wide, 1)]
    cot = after(cotangent, wide_own).reshape(rows, block, width_local)
    cot = jnp.transpose(trade(cot, "row"), (1, 0, 2)).reshape(block, width).astype(f32)

    joined = dot(tokens_all, wq_all, 1, 1)
    queries = (joined[:, :heads_width] + bias_q).astype(bf16).reshape(seq_shape)
    key_rows = joined[:, heads_width : 2 * heads_width].astype(bf16).reshape(seq_shape)
    value_rows = (joined[:, 2 * heads_width :] + bias_v).astype(bf16).reshape(seq_shape)
    scores = (
        jnp.einsum("sqhd,skhd->shqk", queries, key_rows, preferred_element_type=f32) * score_scale
    )
    row_peak = jnp.max(scores, -1, keepdims=True)
    expo_scores = jnp.exp(scores - row_peak)
    row_total = jnp.sum(expo_scores, -1, keepdims=True)
    attn_weights = expo_scores / row_total
    log_total = row_peak + jnp.log(row_total)
    context = jnp.einsum(
        "shqk,skhd->sqhd", attn_weights.astype(bf16), value_rows, preferred_element_type=f32
    )
    context, wide_own, wide_steps[1] = lax.optimization_barrier(
        (context, wide_own, wide_steps[1])
    )
    wide_steps.append(line_step(*wide_steps[1], 2))
    context = to_rel(context.reshape(group, heads_width).astype(bf16), 0)

    send = dot(context[2 * block :], wo_all, 1, 0).astype(bf16)
    keep = dot(context[: 2 * block], wo_all, 1, 0)
    attended, (wide_second, wide_third) = row_reduce(
        keep[:block],
        keep[block:],
        send[:block],
        send[block:],
        0,
        (wide_steps[2], lambda second: (second, line_step(*second, 3))),
    )
    attended = attended + bias_out_f
    wide_steps = [wide_steps[0], wide_steps[1], wide_second, wide_third]
    wide_blocks = line_blocks(wide_steps)
    second_other = swap(wide_blocks[1], "dp", 1)
    ends = jnp.stack([wide_blocks[0], wide_blocks[2]])
    ends_in = swap(ends[:, :half], "dp", 1)
    ends_back = swap(after(ends[:, half:], ends_in), "dp", 1)
    wi_all = jnp.concatenate(
        [wide[:half]]
        + [b[:half] for b in wide_blocks]
        + [wide_own[:half], ends_in[0], second_other[:half], ends_in[1]]
    )
    wb_all = jnp.concatenate(
        [wide[half:]]
        + [b[half:] for b in wide_blocks]
        + [wide_own[half:], ends_back[0], second_other[half:], ends_back[1]]
    )
    tokens_own = lax.dynamic_slice_in_dim(tokens_all, r * block, block, 0)
    tokens_own = from_rel(tokens_own, 1).astype(f32)
    normed_one, inv_one = normalize(tokens_own + attended)
    hidden_one = normed_one * gain_one_f + shift_one_f

    def chips(values):
        over = swap(values, "row", 2)
        near = jnp.concatenate([values, swap(values, "row", 1)], 0)
        return near, jnp.concatenate([over, swap(over, "row", 1)], 0)

    def reduce_chips(near, far):
        return row_reduce(near[:block], far[:block], near[block:], far[block:], 0)

    hidden = chips(hidden_one.astype(bf16))
    pre_act, cdf, activated, mlp = [], [], [], []
    for h in hidden:
        pre = dot(h, wi_all, 1, 1) + bias_in_f
        pre_act.append(pre)
        cdf.append(0.5 * (1.0 + lax.erf(pre * 0.7071067811865476)))
        activated.append((pre * cdf[-1]).astype(bf16))
        mlp.append(dot(activated[-1], wb_all, 1, 0))
    mlp_out = reduce_chips(*mlp) + bias_back_f
    normed_two, inv_two = normalize(hidden_one + mlp_out)
    output = (normed_two * gain_two_f + shift_two_f).astype(bf16)

    d_two = norm_backward(cot, normed_two, inv_two, gain_two_f)
    d_mlp_low = d_two.astype(bf16)
    d_mlp = chips(d_mlp_low)
    d_pre, d_hid = [], []
    for k in range(2):
        d_activated = dot(d_mlp[k], wb_all, 1, 1)
        pdf = jnp.exp(-0.5 * pre_act[k] * pre_act[k]) * 0.3989422804014327
        d_pre.append((d_activated * (cdf[k] + pre_act[k] * pdf)).astype(bf16))
        d_hid.append(dot(d_pre[k], wi_all, 1, 0))
    d_hidden = d_two + reduce_chips(*d_hid)
    def hidden_grad(left, right):
        total = sum(dot(a, b, 0, 0) for a, b in zip(left, right)).astype(bf16)
        total = total.reshape(2, cols, half, width)
        parts = [lax.dynamic_slice_in_dim(total, k, 1, 0)[0] for k in (n, 1 - n)]
        return jnp.stack([col_rolled(p, -1) for p in parts])

    grad_wb = hidden_grad(activated, d_mlp)
    grad_wi = hidden_grad(d_pre, hidden)
    hid_grads = jnp.concatenate([grad_wb, grad_wi], 2)
    if dp_size == 2:
        hid_grads = lax.psum_scatter(
            hid_grads.reshape(-1, width), ("dp", "col"), scatter_dimension=0, tiled=True
        )
        hid_grads = both_halves(hid_grads.reshape(1, 2, half, width))
    else:
        hid_grads = jnp.transpose(hid_grads, (1, 0, 2, 3)).reshape(-1, width)
        hid_grads = lax.psum_scatter(hid_grads, "col", scatter_dimension=0, tiled=True)
        hid_grads = lax.psum(hid_grads.astype(f32), "dp").astype(bf16).reshape(2, 2, half, width)
    hid_grads = jnp.transpose(hid_grads, (1, 0, 2, 3)).reshape(2 * hid_piece, width)
    hid_grads = jnp.concatenate([hid_grads, output], 0).reshape(-1, rows, width_local)
    hid_grads = jnp.transpose(hid_grads, (1, 0, 2))
    pieces = [lax.dynamic_slice_in_dim(hid_grads, r ^ j, 1, 0) for j in range(rows)]
    pieces = jnp.concatenate(
        [pieces[0]] + [swap(pieces[j], "row", j) for j in range(1, rows)], 0
    )
    hid_grads = jnp.concatenate(
        [lax.dynamic_slice_in_dim(pieces, r ^ a, 1, 0) for a in range(rows)], 0
    )
    output = hid_grads[:, 2 * hid_piece :].reshape(group, width_local)
    grad_w_back = hid_grads[:, :hid_piece].reshape(hid_tile, width_local).astype(f32)
    grad_w_in = hid_grads[:, hid_piece : 2 * hid_piece].reshape(hid_tile, width_local)
    grad_w_in = jnp.transpose(grad_w_in).astype(f32)

    d_one = norm_backward(d_hidden, normed_one, inv_one, gain_one_f)
    d_att = d_one.astype(bf16)
    over = swap(d_att, "row", 2)
    d_att_all = jnp.concatenate([d_att, over, swap(d_att, "row", 1), swap(over, "row", 1)], 0)

    def by_owner(values):
        each = values.shape[1]
        got = jnp.transpose(values, (2, 0, 1, 3)).reshape(-1, each, width_local)
        got = trade(got, ("row", "col"))
        got = jnp.sum(got.reshape(rows, cols, each, width_local).astype(f32), 1)
        return dp_sum(got, 1)

    vector_grads = jnp.stack(
        [
            jnp.sum(d_att, 0, dtype=f32),
            jnp.sum(d_hidden * normed_one, 0),
            jnp.sum(d_hidden, 0),
            jnp.sum(d_mlp_low, 0, dtype=f32),
            jnp.sum(cot * normed_two, 0),
            jnp.sum(cot, 0),
        ]
    )
    vector_grads = jnp.transpose(vector_grads.reshape(6, rows, width_local), (1, 0, 2))
    hid_sums = sum(jnp.sum(d, 0, dtype=f32) for d in d_pre).reshape(2, cols, half)
    hid_sums = jnp.where(n == 0, hid_sums, hid_sums[::-1])
    hid_sums = col_rolled(jnp.transpose(hid_sums, (1, 0, 2)), -1).reshape(1, cols, 1, hid_piece)
    small = jnp.concatenate(
        [
            jnp.broadcast_to(vector_grads[:, None], (rows, cols, 6, width_local)),
            jnp.broadcast_to(hid_sums, (rows, cols, 2, width_local)),
        ],
        2,
    )
    small = jnp.broadcast_to(small[None], (dp_size,) + small.shape)
    small = trade(small.reshape(-1, 8, width_local), ("dp", "row", "col"))
    small = small.reshape(dp_size, rows, cols, 8, width_local)
    vector_grads = jnp.sum(small[:, :, :, :6], (0, 1, 2))
    grad_bias_in = jnp.sum(small[:, :, :, 6], (0, 2)).reshape(hid_tile)

    grad_wo = dot(context, d_att_all, 0, 0).astype(bf16).reshape(cols, head_piece, rows, width_local)
    grad_w_out = by_owner(after(grad_wo, small)).reshape(heads_tile, width_local)

    d_context = from_rel(dot(d_att_all, wo_all, 1, 1).astype(bf16), 0).reshape(seq_shape)
    scores_again = (
        jnp.einsum("sqhd,skhd->shqk", queries, key_rows, preferred_element_type=f32) * score_scale
    )
    weights_again = jnp.exp(scores_again - log_total)
    d_value = jnp.einsum(
        "shqk,sqhd->skhd", weights_again.astype(bf16), d_context, preferred_element_type=f32
    )
    d_weights = jnp.einsum("sqhd,skhd->shqk", d_context, value_rows, preferred_element_type=f32)
    row_inner = jnp.sum(d_weights * weights_again, -1, keepdims=True)
    d_scores = (weights_again * (d_weights - row_inner)).astype(bf16)
    d_query = (
        jnp.einsum("shqk,skhd->sqhd", d_scores, key_rows, preferred_element_type=f32) * score_scale
    )
    d_key = (
        jnp.einsum("shqk,sqhd->skhd", d_scores, queries, preferred_element_type=f32) * score_scale
    )
    d_joined = jnp.concatenate(
        [
            d_query.reshape(group, heads_width),
            d_key.reshape(group, heads_width),
            d_value.reshape(group, heads_width),
        ],
        1,
    ).astype(bf16)
    grad_wq = dot(d_joined, tokens_all, 0, 0).astype(bf16)
    grad_wq = from_rel(grad_wq, 1).reshape(3, cols, head_piece, width)
    grad_wq = jnp.transpose(grad_wq, (1, 0, 2, 3)).reshape(cols, heads_rows, rows, width_local)
    head_sums = jnp.sum(d_joined.reshape(group, 3, cols, head_piece), 0, dtype=f32)
    head_sums = jnp.concatenate([head_sums[0], head_sums[2]], 1).astype(bf16)
    head_sums = jnp.pad(head_sums, ((0, 0), (0, width_local - 2 * head_piece)))
    head_sums = jnp.broadcast_to(head_sums[:, None, None], (cols, 16, rows, width_local))
    grad_wq = by_owner(jnp.concatenate([grad_wq, head_sums], 1))
    head_sums = grad_wq[:, heads_rows, : 2 * head_piece].reshape(rows, 2, head_piece)
    grad_bias_qv = jnp.transpose(head_sums, (1, 0, 2)).reshape(2, heads_tile)
    grad_wq = grad_wq[:, :heads_rows].reshape(rows, 3, head_piece, width_local)
    grad_w_qkv = jnp.transpose(grad_wq, (1, 3, 0, 2)).reshape(3, width_local, heads_tile)

    split = 2 * width_local
    d_one_rel = to_rel(d_one, 1)
    own_rows = (jnp.arange(rows) == r)[:, None, None]

    def with_own(values, own):
        values = values.reshape(rows, block, split)
        return (values + jnp.where(own_rows, own[None], 0.0)).reshape(group, split)

    keep = with_own(dot(d_joined, wq_all[:, :split], 1, 0), d_one_rel[:, :split])
    send = with_own(dot(d_joined, wq_all[:, split:], 1, 0), d_one_rel[:, split:]).astype(bf16)
    grad_tokens = row_reduce(
        keep[:, :width_local],
        keep[:, width_local:],
        send[:, :width_local],
        send[:, width_local:],
        1,
    )

    return (
        output,
        grad_tokens,
        grad_w_qkv,
        grad_bias_qv,
        grad_w_out,
        vector_grads[0],
        vector_grads[1],
        vector_grads[2],
        grad_w_in,
        grad_bias_in,
        grad_w_back,
        vector_grads[3],
        vector_grads[4],
        vector_grads[5],
    )


def solution(mesh):
    in_specs = (
        P(("dp", "col"), "row"),
        P(None, "row", "col"),
        P(None, "col"),
        P("col", "row"),
        P("row"),
        P("row"),
        P("row"),
        P("row", "col"),
        P("col"),
        P("col", "row"),
        P("row"),
        P("row"),
        P("row"),
        P(("dp", "col"), "row"),
    )
    out_specs = (
        P(("dp", "col"), "row"),
        P(("dp", "col"), "row"),
        P(None, "row", "col"),
        P(None, "col"),
        P("col", "row"),
        P("row"),
        P("row"),
        P("row"),
        P("row", "col"),
        P("col"),
        P("col", "row"),
        P("row"),
        P("row"),
        P("row"),
    )
    return jax.shard_map(
        per_device, mesh=mesh, in_specs=in_specs, out_specs=out_specs, check_vma=False
    )
```

```python
import jax
import jax.numpy as jnp
from jax import lax
from jax.sharding import PartitionSpec as P

HEAD_DIM = 64
SEQ_LEN = 512
norm_eps = 1e-12

f32 = jnp.float32
bf16 = jnp.bfloat16

REL = (0, 2, 1, 3)


def swap(values, axis, bit):
    size = lax.axis_size(axis)
    return lax.ppermute(values, axis, [(i, i ^ bit) for i in range(size)])


def dot(left, right, left_dim, right_dim):
    return lax.dot_general(
        left, right, (((left_dim,), (right_dim,)), ((), ())), preferred_element_type=f32
    )


def after(values, earlier):
    return lax.optimization_barrier((values, earlier))[0]


def trade(values, axis):
    return lax.all_to_all(values, axis, 0, 0, tiled=True)


def to_rel(values, dim):
    r = lax.axis_index("row")
    size = values.shape[dim] // 4
    parts = [lax.dynamic_slice_in_dim(values, (r ^ j) * size, size, dim) for j in REL]
    return jnp.concatenate(parts, dim)


def from_rel(values, dim):
    r = lax.axis_index("row")
    size = values.shape[dim] // 4
    parts = []
    for a in range(4):
        j = r ^ a
        place = ((j & 1) << 1) | (j >> 1)
        parts.append(lax.dynamic_slice_in_dim(values, place * size, size, dim))
    return jnp.concatenate(parts, dim)


def row_reduce(own, across, beside, diagonal, dim):
    size = own.shape[dim]
    got = swap(jnp.concatenate([beside, diagonal], dim).astype(bf16), "row", 1)
    far = across + lax.slice_in_dim(got, size, 2 * size, axis=dim).astype(f32)
    far = swap(far.astype(bf16), "row", 2)
    return own + lax.slice_in_dim(got, 0, size, axis=dim).astype(f32) + far.astype(f32)


def line_step(up, down, step):
    size = lax.axis_size("col")
    return (
        lax.ppermute(up, "col", [(i, i - 1) for i in range(1, size - step + 1)]),
        lax.ppermute(down, "col", [(i, i + 1) for i in range(step - 1, size - 1)]),
    )


def line_blocks(steps):
    size, here = lax.axis_size("col"), lax.axis_index("col")
    return [
        jnp.where(here + k < size, steps[k][0], steps[size - k][1]) for k in range(1, size)
    ]


def in_col_order(blocks):
    size, here = lax.axis_size("col"), lax.axis_index("col")
    out = jnp.zeros((size,) + blocks[0].shape, blocks[0].dtype)
    for step, b in enumerate(blocks):
        place = (here + step) % size
        out = lax.dynamic_update_slice_in_dim(out, b[None], place, 0)
    return out


def spread(block, axis):
    return trade(jnp.broadcast_to(block[None], (lax.axis_size(axis),) + block.shape), axis)


def normalize(resid):
    row_mean = jnp.mean(resid, 1, keepdims=True)
    centered = resid - row_mean
    variance = jnp.mean(centered * centered, 1, keepdims=True)
    inv_std = lax.rsqrt(variance + norm_eps)
    return centered * inv_std, inv_std


def norm_backward(incoming, normed, inv_std, gain):
    scaled = incoming * gain
    return inv_std * (
        scaled
        - jnp.mean(scaled, 1, keepdims=True)
        - normed * jnp.mean(scaled * normed, 1, keepdims=True)
    )


def dp_sum(values, first_bit):
    size = lax.axis_size("dp")
    bit = first_bit
    while bit < size:
        low = values.astype(bf16)
        values = low.astype(f32) + swap(low, "dp", bit).astype(f32)
        bit *= 2
    return values


def per_device(
    tokens,
    w_qkv,
    bias_qv,
    w_out,
    bias_out,
    gain_one,
    shift_one,
    w_in,
    bias_in,
    w_back,
    bias_back,
    gain_two,
    shift_two,
    cotangent,
):
    rows, cols = lax.axis_size("row"), lax.axis_size("col")
    r, n = lax.axis_index("row"), lax.axis_index("dp") & 1
    dp_size = lax.axis_size("dp")
    group, width_local = tokens.shape
    block = group // rows
    width = width_local * rows
    heads_tile = w_qkv.shape[2]
    head_piece = heads_tile // rows
    heads_width = cols * head_piece
    hid_tile = w_in.shape[1]
    hid_piece = hid_tile // rows
    half = hid_piece // 2
    hid_half = cols * half
    seq_count = group // SEQ_LEN
    head_count = heads_width // HEAD_DIM
    score_scale = HEAD_DIM ** (-0.5)
    seq_shape = (seq_count, SEQ_LEN, head_count, HEAD_DIM)

    heads_rows = 3 * head_piece
    wq = jnp.transpose(w_qkv, (2, 0, 1)).reshape(rows, head_piece, 3, width_local)
    wq = jnp.transpose(wq, (0, 2, 1, 3)).reshape(rows, heads_rows, width_local)
    wo = w_out.reshape(rows, head_piece, width_local)
    first = trade(jnp.concatenate([wq, wo], 1), "row")
    first = jnp.transpose(first, (1, 0, 2)).reshape(-1, width)
    first = jnp.concatenate([to_rel(first[:heads_rows], 1), first[heads_rows:]], 0)
    hid_bias = lax.dynamic_slice(bias_in, (r * hid_piece,), (hid_piece,))
    head_bias = lax.dynamic_slice(bias_qv, (0, r * head_piece), (2, head_piece)).reshape(-1)
    bias_row = jnp.concatenate([hid_bias, head_bias])
    bias_rows = jnp.pad(bias_row[None], ((0, 31), (0, width - bias_row.shape[0])))

    wi = jnp.transpose(w_in).reshape(rows, hid_piece, width_local)
    wi = lax.dynamic_slice_in_dim(wi, n * half, half, 1)
    wb = w_back.reshape(rows, hid_piece, width_local)
    wb = lax.dynamic_slice_in_dim(wb, n * half, half, 1)
    vectors = jnp.stack([bias_out, gain_one, shift_one, bias_back, gain_two, shift_two])
    vectors = jnp.pad(vectors, ((0, 10), (0, 0)))
    vectors = jnp.broadcast_to(vectors[None], (rows,) + vectors.shape)
    mixed = trade(after(jnp.concatenate([wi, wb, vectors], 1), first), "row")
    mixed = jnp.transpose(mixed, (1, 0, 2)).reshape(-1, width)
    wi, wb = mixed[:half], mixed[half : 2 * half]
    vectors = mixed[2 * half :].astype(f32)
    bias_out_f, gain_one_f, shift_one_f, bias_back_f, gain_two_f, shift_two_f = [
        vectors[i] for i in range(6)
    ]

    def both_halves(mine):
        other = swap(mine, "dp", 1)
        return jnp.concatenate([jnp.where(n == 0, mine, other), jnp.where(n == 0, other, mine)], 0)

    begin = jnp.concatenate([first, bias_rows], 0)
    line_half = begin.shape[0] // 2
    mine = lax.dynamic_slice_in_dim(begin, n * line_half, line_half, 0)
    steps = [(mine, mine)]
    steps.append(line_step(mine, mine, 1))
    steps[1], wi = lax.optimization_barrier((steps[1], wi))
    steps.append(line_step(*steps[1], 2))
    steps.append(line_step(*steps[2], 3))
    wi = spread(wi, "col").reshape(hid_half, width)
    steps[3], wi = lax.optimization_barrier((steps[3], wi))
    ours = line_blocks(steps)
    middle = swap(ours[1], "dp", 1)
    ends = swap(jnp.stack([ours[0], ours[2]]), "dp", 1)
    line = [begin]
    for our, their in zip(ours, [ends[0], middle, ends[1]]):
        both = [jnp.where(n == 0, our, their), jnp.where(n == 0, their, our)]
        line.append(jnp.concatenate(both, 0))
    wq_all = in_col_order([b[:heads_rows].reshape(3, head_piece, width) for b in line])
    wq_all = jnp.transpose(wq_all, (1, 0, 2, 3)).reshape(3 * heads_width, width)
    bias_at = heads_rows + head_piece
    wo_all = in_col_order([b[heads_rows:bias_at] for b in line]).reshape(heads_width, width)
    col_bias = in_col_order([b[bias_at, : bias_row.shape[0]] for b in line]).astype(f32)
    bias_q = col_bias[:, hid_piece : hid_piece + head_piece].reshape(-1)
    bias_v = col_bias[:, hid_piece + head_piece :].reshape(-1)
    bias_in_f = jnp.transpose(col_bias[:, :hid_piece].reshape(cols, 2, half), (1, 0, 2)).reshape(-1)

    across = swap(tokens, "row", 2)
    beside = swap(tokens, "row", 1)
    diagonal = swap(across, "row", 1)
    tokens_all = jnp.concatenate([tokens, across, beside, diagonal], 1)

    wb = spread(after(wb, steps[3]), "col").reshape(hid_half, width)
    wi_all = both_halves(wi)
    cot = after(cotangent, wb).reshape(rows, block, width_local)
    cot = jnp.transpose(trade(cot, "row"), (1, 0, 2)).reshape(block, width).astype(f32)

    joined = dot(tokens_all, wq_all, 1, 1)
    queries = (joined[:, :heads_width] + bias_q).astype(bf16).reshape(seq_shape)
    key_rows = joined[:, heads_width : 2 * heads_width].astype(bf16).reshape(seq_shape)
    value_rows = (joined[:, 2 * heads_width :] + bias_v).astype(bf16).reshape(seq_shape)
    scores = (
        jnp.einsum("sqhd,skhd->shqk", queries, key_rows, preferred_element_type=f32) * score_scale
    )
    row_peak = jnp.max(scores, -1, keepdims=True)
    expo_scores = jnp.exp(scores - row_peak)
    row_total = jnp.sum(expo_scores, -1, keepdims=True)
    attn_weights = expo_scores / row_total
    log_total = row_peak + jnp.log(row_total)
    context = jnp.einsum(
        "shqk,skhd->sqhd", attn_weights.astype(bf16), value_rows, preferred_element_type=f32
    )
    context, wb, wi_all = lax.optimization_barrier((context, wb, wi_all))
    wb_all = both_halves(wb)
    context = to_rel(context.reshape(group, heads_width).astype(bf16), 0)

    send = dot(context[2 * block :], wo_all, 1, 0).astype(bf16)
    keep = dot(context[: 2 * block], wo_all, 1, 0)
    attended = row_reduce(keep[:block], keep[block:], send[:block], send[block:], 0) + bias_out_f
    tokens_own = lax.dynamic_slice_in_dim(tokens_all, r * block, block, 0)
    tokens_own = from_rel(tokens_own, 1).astype(f32)
    normed_one, inv_one = normalize(tokens_own + attended)
    hidden_one = normed_one * gain_one_f + shift_one_f

    def chips(values):
        over = swap(values, "row", 2)
        near = jnp.concatenate([values, swap(values, "row", 1)], 0)
        return near, jnp.concatenate([over, swap(over, "row", 1)], 0)

    def reduce_chips(near, far):
        return row_reduce(near[:block], far[:block], near[block:], far[block:], 0)

    hidden = chips(hidden_one.astype(bf16))
    pre_act, cdf, activated, mlp = [], [], [], []
    for h in hidden:
        pre = dot(h, wi_all, 1, 1) + bias_in_f
        pre_act.append(pre)
        cdf.append(0.5 * (1.0 + lax.erf(pre * 0.7071067811865476)))
        activated.append((pre * cdf[-1]).astype(bf16))
        mlp.append(dot(activated[-1], wb_all, 1, 0))
    mlp_out = reduce_chips(*mlp) + bias_back_f
    normed_two, inv_two = normalize(hidden_one + mlp_out)
    output = (normed_two * gain_two_f + shift_two_f).astype(bf16)

    d_two = norm_backward(cot, normed_two, inv_two, gain_two_f)
    d_mlp_low = d_two.astype(bf16)
    d_mlp = chips(d_mlp_low)
    d_pre, d_hid = [], []
    for k in range(2):
        d_activated = dot(d_mlp[k], wb_all, 1, 1)
        pdf = jnp.exp(-0.5 * pre_act[k] * pre_act[k]) * 0.3989422804014327
        d_pre.append((d_activated * (cdf[k] + pre_act[k] * pdf)).astype(bf16))
        d_hid.append(dot(d_pre[k], wi_all, 1, 0))
    d_hidden = d_two + reduce_chips(*d_hid)
    def hidden_grad(left, right):
        return sum(dot(a, b, 0, 0) for a, b in zip(left, right)).astype(bf16)

    grad_wb = hidden_grad(activated, d_mlp)
    grad_wi = hidden_grad(d_pre, hidden)
    hid_grads_gate = None
    if dp_size == 2:
        grad_wb = trade(grad_wb.reshape(2 * cols, half, width), ("dp", "col"))
        hid_grads_gate = grad_wb
        grad_wb = jnp.sum(grad_wb.astype(f32), 0).astype(bf16)
        grad_wi = lax.psum_scatter(grad_wi, ("dp", "col"), scatter_dimension=0, tiled=True)
        hid_grads = both_halves(jnp.stack([grad_wb, grad_wi])[None])
    else:
        hid_grads = jnp.stack([grad_wb, grad_wi]).reshape(2, 2, cols, half, width)
        hid_grads = jnp.transpose(hid_grads, (2, 1, 0, 3, 4)).reshape(-1, width)
        hid_grads = lax.psum_scatter(hid_grads, "col", scatter_dimension=0, tiled=True)
        hid_grads = lax.psum(hid_grads.astype(f32), "dp").astype(bf16).reshape(2, 2, half, width)
    hid_grads = jnp.transpose(hid_grads, (1, 0, 2, 3)).reshape(2 * hid_piece, width)
    hid_grads = jnp.concatenate([hid_grads, output], 0).reshape(-1, rows, width_local)
    hid_grads = jnp.transpose(hid_grads, (1, 0, 2))
    pieces = [lax.dynamic_slice_in_dim(hid_grads, r ^ j, 1, 0) for j in range(rows)]
    pieces = jnp.concatenate(
        [pieces[0]] + [swap(pieces[j], "row", j) for j in range(1, rows)], 0
    )
    hid_grads = jnp.concatenate(
        [lax.dynamic_slice_in_dim(pieces, r ^ a, 1, 0) for a in range(rows)], 0
    )
    output = hid_grads[:, 2 * hid_piece :].reshape(group, width_local)
    grad_w_back = hid_grads[:, :hid_piece].reshape(hid_tile, width_local).astype(f32)
    grad_w_in = hid_grads[:, hid_piece : 2 * hid_piece].reshape(hid_tile, width_local)
    grad_w_in = jnp.transpose(grad_w_in).astype(f32)

    d_one = norm_backward(d_hidden, normed_one, inv_one, gain_one_f)
    d_att = d_one.astype(bf16)
    over = swap(d_att, "row", 2)
    d_att_all = jnp.concatenate([d_att, over, swap(d_att, "row", 1), swap(over, "row", 1)], 0)
    d_att_all, _ = lax.optimization_barrier((d_att_all, hid_grads_gate))

    def by_owner(values):
        each = values.shape[1]
        got = jnp.transpose(values, (2, 0, 1, 3)).reshape(-1, each, width_local)
        raw = trade(got, ("row", "col"))
        got = jnp.sum(raw.reshape(rows, cols, each, width_local).astype(f32), 1)
        return dp_sum(got, 1), raw

    grad_wo = dot(context, d_att_all, 0, 0).astype(bf16).reshape(cols, head_piece, rows, width_local)
    grad_w_out = by_owner(grad_wo)[0].reshape(heads_tile, width_local)

    d_context = from_rel(dot(d_att_all, wo_all, 1, 1).astype(bf16), 0).reshape(seq_shape)
    scores_again = (
        jnp.einsum("sqhd,skhd->shqk", queries, key_rows, preferred_element_type=f32) * score_scale
    )
    weights_again = jnp.exp(scores_again - log_total)
    d_value = jnp.einsum(
        "shqk,sqhd->skhd", weights_again.astype(bf16), d_context, preferred_element_type=f32
    )
    d_weights = jnp.einsum("sqhd,skhd->shqk", d_context, value_rows, preferred_element_type=f32)
    row_inner = jnp.sum(d_weights * weights_again, -1, keepdims=True)
    d_scores = (weights_again * (d_weights - row_inner)).astype(bf16)
    d_query = (
        jnp.einsum("shqk,skhd->sqhd", d_scores, key_rows, preferred_element_type=f32) * score_scale
    )
    d_key = (
        jnp.einsum("shqk,sqhd->skhd", d_scores, queries, preferred_element_type=f32) * score_scale
    )
    d_joined = jnp.concatenate(
        [
            d_query.reshape(group, heads_width),
            d_key.reshape(group, heads_width),
            d_value.reshape(group, heads_width),
        ],
        1,
    ).astype(bf16)
    grad_wq = dot(d_joined, tokens_all, 0, 0).astype(bf16)
    grad_wq = from_rel(grad_wq, 1).reshape(3, cols, head_piece, width)
    grad_wq = jnp.transpose(grad_wq, (1, 0, 2, 3)).reshape(cols, heads_rows, rows, width_local)
    head_sums = jnp.sum(d_joined.reshape(group, 3, cols, head_piece), 0, dtype=f32)
    head_sums = jnp.concatenate([head_sums[0], head_sums[2]], 1).astype(bf16)
    head_sums = jnp.pad(head_sums, ((0, 0), (0, width_local - 2 * head_piece)))
    head_sums = jnp.broadcast_to(head_sums[:, None, None], (cols, 16, rows, width_local))
    grad_wq, arrived = by_owner(jnp.concatenate([grad_wq, head_sums], 1))
    head_sums = grad_wq[:, heads_rows, : 2 * head_piece].reshape(rows, 2, head_piece)
    grad_bias_qv = jnp.transpose(head_sums, (1, 0, 2)).reshape(2, heads_tile)
    grad_wq = grad_wq[:, :heads_rows].reshape(rows, 3, head_piece, width_local)
    grad_w_qkv = jnp.transpose(grad_wq, (1, 3, 0, 2)).reshape(3, width_local, heads_tile)

    split = 2 * width_local
    d_one_rel = to_rel(d_one, 1)
    own_rows = (jnp.arange(rows) == r)[:, None, None]

    def with_own(values, own):
        values = values.reshape(rows, block, split)
        return (values + jnp.where(own_rows, own[None], 0.0)).reshape(group, split)

    keep = with_own(dot(d_joined, wq_all[:, :split], 1, 0), d_one_rel[:, :split])
    send = with_own(dot(d_joined, wq_all[:, split:], 1, 0), d_one_rel[:, split:]).astype(bf16)
    grad_tokens = row_reduce(
        keep[:, :width_local],
        keep[:, width_local:],
        send[:, :width_local],
        send[:, width_local:],
        1,
    )

    vector_grads = jnp.stack(
        [
            jnp.sum(d_att, 0, dtype=f32),
            jnp.sum(d_hidden * normed_one, 0),
            jnp.sum(d_hidden, 0),
            jnp.sum(d_mlp_low, 0, dtype=f32),
            jnp.sum(cot * normed_two, 0),
            jnp.sum(cot, 0),
        ]
    )
    vector_grads = jnp.transpose(vector_grads.reshape(6, rows, width_local), (1, 0, 2))
    hid_sums = sum(jnp.sum(d, 0, dtype=f32) for d in d_pre).reshape(2, cols, half)
    hid_sums = jnp.transpose(hid_sums, (1, 0, 2)).reshape(1, cols, 1, hid_piece)
    small = jnp.concatenate(
        [
            jnp.broadcast_to(vector_grads[:, None], (rows, cols, 6, width_local)),
            jnp.broadcast_to(hid_sums, (rows, cols, 2, width_local)),
        ],
        2,
    )
    small = jnp.broadcast_to(small[None], (dp_size,) + small.shape)
    small = after(small, arrived)
    small = trade(small.reshape(-1, 8, width_local), ("dp", "row", "col"))
    small = small.reshape(dp_size, rows, cols, 8, width_local)
    vector_grads = jnp.sum(small[:, :, :, :6], (0, 1, 2))
    grad_bias_in = jnp.sum(small[:, :, :, 6], (0, 2)).reshape(hid_tile)

    return (
        output,
        grad_tokens,
        grad_w_qkv,
        grad_bias_qv,
        grad_w_out,
        vector_grads[0],
        vector_grads[1],
        vector_grads[2],
        grad_w_in,
        grad_bias_in,
        grad_w_back,
        vector_grads[3],
        vector_grads[4],
        vector_grads[5],
    )


def solution(mesh):
    in_specs = (
        P(("dp", "col"), "row"),
        P(None, "row", "col"),
        P(None, "col"),
        P("col", "row"),
        P("row"),
        P("row"),
        P("row"),
        P("row", "col"),
        P("col"),
        P("col", "row"),
        P("row"),
        P("row"),
        P("row"),
        P(("dp", "col"), "row"),
    )
    out_specs = (
        P(("dp", "col"), "row"),
        P(("dp", "col"), "row"),
        P(None, "row", "col"),
        P(None, "col"),
        P("col", "row"),
        P("row"),
        P("row"),
        P("row"),
        P("row", "col"),
        P("col"),
        P("col", "row"),
        P("row"),
        P("row"),
        P("row"),
    )
    return jax.shard_map(
        per_device, mesh=mesh, in_specs=in_specs, out_specs=out_specs, check_vma=False
    )
```

```python
import jax
import jax.numpy as jnp
from jax import lax
from jax.experimental import pallas as pl
from jax.experimental.pallas import tpu as pltpu
from jax.sharding import PartitionSpec as P

HEAD_DIM = 64
SEQ_LEN = 512
norm_eps = 1e-12

f32 = jnp.float32
bf16 = jnp.bfloat16

REL = (0, 2, 1, 3)


def swap(values, axis, bit):
    size = lax.axis_size(axis)
    return lax.ppermute(values, axis, [(i, i ^ bit) for i in range(size)])


def dot(left, right, left_dim, right_dim):
    return lax.dot_general(
        left, right, (((left_dim,), (right_dim,)), ((), ())), preferred_element_type=f32
    )


def after(values, earlier):
    return lax.optimization_barrier((values, earlier))[0]


def trade(values, axis):
    return lax.all_to_all(values, axis, 0, 0, tiled=True)


def to_rel(values, dim):
    r = lax.axis_index("row")
    size = values.shape[dim] // 4
    parts = [lax.dynamic_slice_in_dim(values, (r ^ j) * size, size, dim) for j in REL]
    return jnp.concatenate(parts, dim)


def from_rel(values, dim):
    r = lax.axis_index("row")
    size = values.shape[dim] // 4
    parts = []
    for a in range(4):
        j = r ^ a
        place = ((j & 1) << 1) | (j >> 1)
        parts.append(lax.dynamic_slice_in_dim(values, place * size, size, dim))
    return jnp.concatenate(parts, dim)


def row_reduce(own, across, beside, diagonal, dim):
    size = own.shape[dim]
    got = swap(jnp.concatenate([beside, diagonal], dim).astype(bf16), "row", 1)
    far = across + lax.slice_in_dim(got, size, 2 * size, axis=dim).astype(f32)
    far = swap(far.astype(bf16), "row", 2)
    return own + lax.slice_in_dim(got, 0, size, axis=dim).astype(f32) + far.astype(f32)


def line_step(up, down, step):
    size = lax.axis_size("col")
    return (
        lax.ppermute(up, "col", [(i, i - 1) for i in range(1, size - step + 1)]),
        lax.ppermute(down, "col", [(i, i + 1) for i in range(step - 1, size - 1)]),
    )


def line_blocks(steps):
    size, here = lax.axis_size("col"), lax.axis_index("col")
    return [
        jnp.where(here + k < size, steps[k][0], steps[size - k][1]) for k in range(1, size)
    ]


def in_col_order(blocks):
    size, here = lax.axis_size("col"), lax.axis_index("col")
    out = jnp.zeros((size,) + blocks[0].shape, blocks[0].dtype)
    for step, b in enumerate(blocks):
        place = (here + step) % size
        out = lax.dynamic_update_slice_in_dim(out, b[None], place, 0)
    return out


def spread(block, axis):
    return trade(jnp.broadcast_to(block[None], (lax.axis_size(axis),) + block.shape), axis)


def normalize(resid):
    row_mean = jnp.mean(resid, 1, keepdims=True)
    centered = resid - row_mean
    variance = jnp.mean(centered * centered, 1, keepdims=True)
    inv_std = lax.rsqrt(variance + norm_eps)
    return centered * inv_std, inv_std


def norm_backward(incoming, normed, inv_std, gain):
    scaled = incoming * gain
    return inv_std * (
        scaled
        - jnp.mean(scaled, 1, keepdims=True)
        - normed * jnp.mean(scaled * normed, 1, keepdims=True)
    )


def dp_sum(values, first_bit):
    size = lax.axis_size("dp")
    bit = first_bit
    while bit < size:
        low = values.astype(bf16)
        values = low.astype(f32) + swap(low, "dp", bit).astype(f32)
        bit *= 2
    return values


def head_part(values, head, part):
    start = (3 * head + part) * HEAD_DIM
    return values[:, start : start + HEAD_DIM]


def attend_kernel(qkv_ref, out_ref):
    qkv = qkv_ref[...]
    for head in range(out_ref.shape[1] // HEAD_DIM):
        queries, keys, vals = [head_part(qkv, head, part) for part in range(3)]
        scores = dot(queries, keys, 1, 1) * HEAD_DIM ** (-0.5)
        expo = jnp.exp(scores - jnp.max(scores, 1, keepdims=True))
        weights = expo / jnp.sum(expo, 1, keepdims=True)
        context = dot(weights.astype(bf16), vals, 1, 0).astype(bf16)
        out_ref[:, head * HEAD_DIM : (head + 1) * HEAD_DIM] = context


def attend_back_kernel(qkv_ref, d_context_ref, out_ref):
    qkv = qkv_ref[...]
    scale = HEAD_DIM ** (-0.5)
    for head in range(d_context_ref.shape[1] // HEAD_DIM):
        queries, keys, vals = [head_part(qkv, head, part) for part in range(3)]
        d_context = d_context_ref[:, head * HEAD_DIM : (head + 1) * HEAD_DIM]
        scores = dot(keys, queries, 1, 1) * scale
        expo = jnp.exp(scores - jnp.max(scores, 0, keepdims=True))
        weights = expo / jnp.sum(expo, 0, keepdims=True)
        d_value = dot(weights.astype(bf16), d_context, 1, 0)
        d_weights = dot(vals, d_context, 1, 1)
        inner = jnp.sum(d_weights * weights, 0, keepdims=True)
        d_scores = (weights * (d_weights - inner)).astype(bf16)
        d_key = dot(d_scores, queries, 1, 0) * scale
        d_query = dot(d_scores, keys, 0, 0) * scale
        for part, grad in enumerate((d_query, d_key, d_value)):
            start = (3 * head + part) * HEAD_DIM
            out_ref[:, start : start + HEAD_DIM] = grad.astype(bf16)


def by_sequence(kernel, operands, width, flops):
    tokens = operands[0].shape[0]
    heads = operands[0].shape[1] // (3 * HEAD_DIM)
    return pl.pallas_call(
        kernel,
        grid=(tokens // SEQ_LEN,),
        in_specs=[pl.BlockSpec((SEQ_LEN, v.shape[1]), lambda i: (i, 0)) for v in operands],
        out_specs=pl.BlockSpec((SEQ_LEN, width), lambda i: (i, 0)),
        out_shape=jax.ShapeDtypeStruct((tokens, width), bf16),
        compiler_params=pltpu.CompilerParams(vmem_limit_bytes=40 * 2**20),
        cost_estimate=pl.CostEstimate(
            flops=flops * tokens * SEQ_LEN * heads * HEAD_DIM,
            bytes_accessed=2 * tokens * (width + sum(v.shape[1] for v in operands)),
            transcendentals=tokens * SEQ_LEN * heads,
        ),
    )(*operands)


def per_device(
    tokens,
    w_qkv,
    bias_qv,
    w_out,
    bias_out,
    gain_one,
    shift_one,
    w_in,
    bias_in,
    w_back,
    bias_back,
    gain_two,
    shift_two,
    cotangent,
):
    rows, cols = lax.axis_size("row"), lax.axis_size("col")
    r, n = lax.axis_index("row"), lax.axis_index("dp") & 1
    dp_size = lax.axis_size("dp")
    group, width_local = tokens.shape
    block = group // rows
    width = width_local * rows
    heads_tile = w_qkv.shape[2]
    head_piece = heads_tile // rows
    heads_width = cols * head_piece
    hid_tile = w_in.shape[1]
    hid_piece = hid_tile // rows
    half = hid_piece // 2
    hid_half = cols * half

    heads_rows = 3 * head_piece
    wq = jnp.transpose(w_qkv, (2, 0, 1)).reshape(rows, head_piece, 3, width_local)
    wq = jnp.transpose(wq, (0, 2, 1, 3)).reshape(rows, heads_rows, width_local)
    wo = w_out.reshape(rows, head_piece, width_local)
    first = trade(jnp.concatenate([wq, wo], 1), "row")
    first = jnp.transpose(first, (1, 0, 2)).reshape(-1, width)
    first = jnp.concatenate([to_rel(first[:heads_rows], 1), first[heads_rows:]], 0)
    hid_bias = lax.dynamic_slice(bias_in, (r * hid_piece,), (hid_piece,))
    head_bias = lax.dynamic_slice(bias_qv, (0, r * head_piece), (2, head_piece)).reshape(-1)
    bias_row = jnp.concatenate([hid_bias, head_bias])
    bias_rows = jnp.pad(bias_row[None], ((0, 31), (0, width - bias_row.shape[0])))

    wi = jnp.transpose(w_in).reshape(rows, hid_piece, width_local)
    wi = lax.dynamic_slice_in_dim(wi, n * half, half, 1)
    wb = w_back.reshape(rows, hid_piece, width_local)
    wb = lax.dynamic_slice_in_dim(wb, n * half, half, 1)
    vectors = jnp.stack([bias_out, gain_one, shift_one, bias_back, gain_two, shift_two])
    vectors = jnp.pad(vectors, ((0, 10), (0, 0)))
    vectors = jnp.broadcast_to(vectors[None], (rows,) + vectors.shape)
    mixed = trade(after(jnp.concatenate([wi, wb, vectors], 1), first), "row")
    mixed = jnp.transpose(mixed, (1, 0, 2)).reshape(-1, width)
    wi, wb = mixed[:half], mixed[half : 2 * half]
    vectors = mixed[2 * half :].astype(f32)
    bias_out_f, gain_one_f, shift_one_f, bias_back_f, gain_two_f, shift_two_f = [
        vectors[i] for i in range(6)
    ]

    def both_halves(mine):
        other = swap(mine, "dp", 1)
        return jnp.concatenate([jnp.where(n == 0, mine, other), jnp.where(n == 0, other, mine)], 0)

    begin = jnp.concatenate([first, bias_rows], 0)
    line_half = begin.shape[0] // 2
    mine = lax.dynamic_slice_in_dim(begin, n * line_half, line_half, 0)
    steps = [(mine, mine)]
    steps.append(line_step(mine, mine, 1))
    steps[1], wi = lax.optimization_barrier((steps[1], wi))
    steps.append(line_step(*steps[1], 2))
    wi = spread(wi, "col").reshape(hid_half, width)
    steps[2], wi = lax.optimization_barrier((steps[2], wi))
    steps.append(line_step(*steps[2], 3))
    wb = spread(after(wb, wi), "col").reshape(hid_half, width)
    steps[3], wb = lax.optimization_barrier((steps[3], wb))
    ours = line_blocks(steps)
    middle = swap(ours[1], "dp", 1)
    ends = swap(jnp.stack([ours[0], ours[2]]), "dp", 1)
    line = [begin]
    for our, their in zip(ours, [ends[0], middle, ends[1]]):
        both = [jnp.where(n == 0, our, their), jnp.where(n == 0, their, our)]
        line.append(jnp.concatenate(both, 0))
    wq_all = in_col_order([b[:heads_rows] for b in line]).reshape(3 * heads_width, width)
    bias_at = heads_rows + head_piece
    wo_all = in_col_order([b[heads_rows:bias_at] for b in line]).reshape(heads_width, width)
    col_bias = in_col_order([b[bias_at, : bias_row.shape[0]] for b in line]).astype(f32)
    bias_q = col_bias[:, hid_piece : hid_piece + head_piece]
    bias_v = col_bias[:, hid_piece + head_piece :]
    bias_qkv = jnp.concatenate([bias_q, jnp.zeros_like(bias_q), bias_v], 1).reshape(-1)
    bias_in_f = jnp.transpose(col_bias[:, :hid_piece].reshape(cols, 2, half), (1, 0, 2)).reshape(-1)

    across = swap(tokens, "row", 2)
    beside = swap(tokens, "row", 1)
    diagonal = swap(across, "row", 1)
    tokens_all = jnp.concatenate([tokens, across, beside, diagonal], 1)

    wi_all = both_halves(wi)
    cot = after(cotangent, wb).reshape(rows, block, width_local)
    cot = jnp.transpose(trade(cot, "row"), (1, 0, 2)).reshape(block, width).astype(f32)

    joined = (dot(tokens_all, wq_all, 1, 1) + bias_qkv).astype(bf16)
    context = by_sequence(attend_kernel, [joined], heads_width, 4)
    context, wb, wi_all = lax.optimization_barrier((context, wb, wi_all))
    wb_all = both_halves(wb)
    context = to_rel(context, 0)

    send = dot(context[2 * block :], wo_all, 1, 0).astype(bf16)
    keep = dot(context[: 2 * block], wo_all, 1, 0)
    attended = row_reduce(keep[:block], keep[block:], send[:block], send[block:], 0) + bias_out_f
    tokens_own = lax.dynamic_slice_in_dim(tokens_all, r * block, block, 0)
    tokens_own = from_rel(tokens_own, 1).astype(f32)
    normed_one, inv_one = normalize(tokens_own + attended)
    hidden_one = normed_one * gain_one_f + shift_one_f

    def chips(values):
        over = swap(values, "row", 2)
        near = jnp.concatenate([values, swap(values, "row", 1)], 0)
        return near, jnp.concatenate([over, swap(over, "row", 1)], 0)

    def reduce_chips(near, far):
        return row_reduce(near[:block], far[:block], near[block:], far[block:], 0)

    hidden = chips(hidden_one.astype(bf16))
    pre_act, cdf, activated, mlp = [], [], [], []
    for h in hidden:
        pre = dot(h, wi_all, 1, 1) + bias_in_f
        pre_act.append(pre)
        cdf.append(0.5 * (1.0 + lax.erf(pre * 0.7071067811865476)))
        activated.append((pre * cdf[-1]).astype(bf16))
        mlp.append(dot(activated[-1], wb_all, 1, 0))
    mlp_out = reduce_chips(*mlp) + bias_back_f
    normed_two, inv_two = normalize(hidden_one + mlp_out)
    output = (normed_two * gain_two_f + shift_two_f).astype(bf16)

    d_two = norm_backward(cot, normed_two, inv_two, gain_two_f)
    d_mlp_low = d_two.astype(bf16)
    d_mlp = chips(d_mlp_low)
    d_pre, d_hid = [], []
    for k in range(2):
        d_activated = dot(d_mlp[k], wb_all, 1, 1)
        pdf = jnp.exp(-0.5 * pre_act[k] * pre_act[k]) * 0.3989422804014327
        d_pre.append((d_activated * (cdf[k] + pre_act[k] * pdf)).astype(bf16))
        d_hid.append(dot(d_pre[k], wi_all, 1, 0))
    grad_wb = sum(dot(a, b, 0, 0) for a, b in zip(activated, d_mlp)).astype(bf16)
    d_hidden = d_two + reduce_chips(*d_hid)
    d_hidden, _ = lax.optimization_barrier((d_hidden, grad_wb))
    grad_wi = sum(dot(a, b, 0, 0) for a, b in zip(d_pre, hidden)).astype(bf16)
    grad_wi_ready, hid_grads_gate = grad_wi, None
    if dp_size == 2:
        grad_wb = trade(grad_wb.reshape(2 * cols, half, width), ("dp", "col"))
        hid_grads_gate = grad_wb
        grad_wi = lax.psum_scatter(grad_wi, ("dp", "col"), scatter_dimension=0, tiled=True)

    d_one = norm_backward(d_hidden, normed_one, inv_one, gain_one_f)
    d_att = d_one.astype(bf16)
    over = swap(d_att, "row", 2)
    over, _ = lax.optimization_barrier((over, grad_wi_ready))
    d_att_all = jnp.concatenate([d_att, over, swap(d_att, "row", 1), swap(over, "row", 1)], 0)

    def by_owner(values):
        each = values.shape[2]
        raw = trade(values.reshape(-1, each, width_local), ("row", "col"))
        got = jnp.sum(raw.reshape(rows, cols, each, width_local).astype(f32), 1)
        return dp_sum(got, 1), raw

    grad_wo = dot(context, d_att_all, 0, 0).astype(bf16).reshape(cols, head_piece, rows, width_local)
    grad_wo = jnp.transpose(grad_wo, (2, 0, 1, 3))

    d_context = from_rel(dot(d_att_all, wo_all, 1, 1).astype(bf16), 0)
    d_joined = by_sequence(attend_back_kernel, [joined, d_context], 3 * heads_width, 10)
    d_joined, _ = lax.optimization_barrier((d_joined, hid_grads_gate))
    grad_wq = []
    for a in range(rows):
        j = r ^ a
        place = (((j & 1) << 1) | (j >> 1)) * width_local
        owned = lax.dynamic_slice_in_dim(tokens_all, place, width_local, 1)
        grad_wq.append(dot(d_joined, owned, 0, 0).astype(bf16).reshape(cols, heads_rows, -1))
    grad_wq = jnp.concatenate([jnp.stack(grad_wq), grad_wo], 2)
    d_joined_late = after(d_joined, grad_wq)
    grad_wq, arrived = by_owner(grad_wq)
    grad_w_out = grad_wq[:, heads_rows:].reshape(heads_tile, width_local)
    grad_wq = grad_wq[:, :heads_rows].reshape(rows, 3, head_piece, width_local)
    grad_w_qkv = jnp.transpose(grad_wq, (1, 3, 0, 2)).reshape(3, width_local, heads_tile)

    split = 2 * width_local
    d_one_rel = to_rel(d_one, 1)
    own_rows = (jnp.arange(rows) == r)[:, None, None]

    def with_own(values, own):
        values = values.reshape(rows, block, split)
        return (values + jnp.where(own_rows, own[None], 0.0)).reshape(group, split)

    keep = with_own(dot(d_joined_late, wq_all[:, :split], 1, 0), d_one_rel[:, :split])
    send = with_own(dot(d_joined_late, wq_all[:, split:], 1, 0), d_one_rel[:, split:]).astype(bf16)
    grad_tokens = row_reduce(
        keep[:, :width_local],
        keep[:, width_local:],
        send[:, :width_local],
        send[:, width_local:],
        1,
    )

    vector_grads = jnp.stack(
        [
            jnp.sum(d_att, 0, dtype=f32),
            jnp.sum(d_hidden * normed_one, 0),
            jnp.sum(d_hidden, 0),
            jnp.sum(d_mlp_low, 0, dtype=f32),
            jnp.sum(cot * normed_two, 0),
            jnp.sum(cot, 0),
        ]
    )
    vector_grads = jnp.transpose(vector_grads.reshape(6, rows, width_local), (1, 0, 2))
    hid_sums = sum(jnp.sum(d, 0, dtype=f32) for d in d_pre).reshape(2, cols, half)
    hid_sums = jnp.transpose(hid_sums, (1, 0, 2)).reshape(1, cols, 1, hid_piece)
    head_sums = jnp.sum(d_joined, 0, dtype=f32).reshape(cols, 3, head_piece)
    head_sums = jnp.concatenate([head_sums[:, 0], head_sums[:, 2]], 1)
    head_sums = jnp.pad(head_sums, ((0, 0), (0, width_local - 2 * head_piece)))
    col_sums = jnp.concatenate([hid_sums, head_sums[None, :, None]], 2)
    small = jnp.concatenate(
        [
            jnp.broadcast_to(vector_grads[:, None], (rows, cols, 6, width_local)),
            jnp.broadcast_to(col_sums, (rows, cols, 2, width_local)),
        ],
        2,
    )
    small = jnp.broadcast_to(small[None], (dp_size,) + small.shape)
    small = after(small, arrived)
    small = trade(small.reshape(-1, 8, width_local), ("dp", "row", "col"))
    small = small.reshape(dp_size, rows, cols, 8, width_local)
    vector_grads = jnp.sum(small[:, :, :, :6], (0, 1, 2))
    grad_bias_in = jnp.sum(small[:, :, :, 6], (0, 2)).reshape(hid_tile)
    head_sums = jnp.sum(small[:, :, :, 7, : 2 * head_piece], (0, 2)).reshape(rows, 2, head_piece)
    grad_bias_qv = jnp.transpose(head_sums, (1, 0, 2)).reshape(2, heads_tile)

    if dp_size == 2:
        grad_wb = jnp.sum(grad_wb.astype(f32), 0).astype(bf16)
        grad_wi = after(grad_wi, send)
        hid_grads = both_halves(jnp.stack([grad_wb, grad_wi])[None])
    else:
        hid_grads = jnp.stack([grad_wb, grad_wi]).reshape(2, 2, cols, half, width)
        hid_grads = jnp.transpose(hid_grads, (2, 1, 0, 3, 4)).reshape(-1, width)
        hid_grads = lax.psum_scatter(hid_grads, "col", scatter_dimension=0, tiled=True)
        hid_grads = lax.psum(hid_grads.astype(f32), "dp").astype(bf16).reshape(2, 2, half, width)
    hid_grads = jnp.transpose(hid_grads, (1, 0, 2, 3)).reshape(2 * hid_piece, width)
    hid_grads = jnp.concatenate([hid_grads, output], 0).reshape(-1, rows, width_local)
    hid_grads = jnp.transpose(hid_grads, (1, 0, 2))
    pieces = [lax.dynamic_slice_in_dim(hid_grads, r ^ j, 1, 0) for j in range(rows)]
    pieces = jnp.concatenate(
        [pieces[0]] + [swap(pieces[j], "row", j) for j in range(1, rows)], 0
    )
    hid_grads = jnp.concatenate(
        [lax.dynamic_slice_in_dim(pieces, r ^ a, 1, 0) for a in range(rows)], 0
    )
    output = hid_grads[:, 2 * hid_piece :].reshape(group, width_local)
    grad_w_back = hid_grads[:, :hid_piece].reshape(hid_tile, width_local).astype(f32)
    grad_w_in = hid_grads[:, hid_piece : 2 * hid_piece].reshape(hid_tile, width_local)
    grad_w_in = jnp.transpose(grad_w_in).astype(f32)

    return (
        output,
        grad_tokens,
        grad_w_qkv,
        grad_bias_qv,
        grad_w_out,
        vector_grads[0],
        vector_grads[1],
        vector_grads[2],
        grad_w_in,
        grad_bias_in,
        grad_w_back,
        vector_grads[3],
        vector_grads[4],
        vector_grads[5],
    )


def solution(mesh):
    in_specs = (
        P(("dp", "col"), "row"),
        P(None, "row", "col"),
        P(None, "col"),
        P("col", "row"),
        P("row"),
        P("row"),
        P("row"),
        P("row", "col"),
        P("col"),
        P("col", "row"),
        P("row"),
        P("row"),
        P("row"),
        P(("dp", "col"), "row"),
    )
    out_specs = (
        P(("dp", "col"), "row"),
        P(("dp", "col"), "row"),
        P(None, "row", "col"),
        P(None, "col"),
        P("col", "row"),
        P("row"),
        P("row"),
        P("row"),
        P("row", "col"),
        P("col"),
        P("col", "row"),
        P("row"),
        P("row"),
        P("row"),
    )
    return jax.shard_map(
        per_device, mesh=mesh, in_specs=in_specs, out_specs=out_specs, check_vma=False
    )
```

```python
import jax
import jax.numpy as jnp
from jax import lax
from jax.experimental import pallas as pl
from jax.experimental.pallas import tpu as pltpu
from jax.sharding import PartitionSpec as P

HEAD_DIM = 64
SEQ_LEN = 512
norm_eps = 1e-12

f32 = jnp.float32
bf16 = jnp.bfloat16

REL = (0, 2, 1, 3)


def swap(values, axis, bit):
    size = lax.axis_size(axis)
    return lax.ppermute(values, axis, [(i, i ^ bit) for i in range(size)])


def dot(left, right, left_dim, right_dim):
    return lax.dot_general(
        left, right, (((left_dim,), (right_dim,)), ((), ())), preferred_element_type=f32
    )


def after(values, earlier):
    return lax.optimization_barrier((values, earlier))[0]


def trade(values, axis):
    return lax.all_to_all(values, axis, 0, 0, tiled=True)


def to_rel(values, dim):
    r = lax.axis_index("row")
    size = values.shape[dim] // 4
    parts = [lax.dynamic_slice_in_dim(values, (r ^ j) * size, size, dim) for j in REL]
    return jnp.concatenate(parts, dim)


def from_rel(values, dim):
    r = lax.axis_index("row")
    size = values.shape[dim] // 4
    parts = []
    for a in range(4):
        j = r ^ a
        place = ((j & 1) << 1) | (j >> 1)
        parts.append(lax.dynamic_slice_in_dim(values, place * size, size, dim))
    return jnp.concatenate(parts, dim)


def row_reduce(own, across, beside, diagonal, dim):
    size = own.shape[dim]
    got = swap(jnp.concatenate([beside, diagonal], dim).astype(bf16), "row", 1)
    far = across + lax.slice_in_dim(got, size, 2 * size, axis=dim).astype(f32)
    far = swap(far.astype(bf16), "row", 2)
    return own + lax.slice_in_dim(got, 0, size, axis=dim).astype(f32) + far.astype(f32)


def line_step(up, down, step):
    size = lax.axis_size("col")
    return (
        lax.ppermute(up, "col", [(i, i - 1) for i in range(1, size - step + 1)]),
        lax.ppermute(down, "col", [(i, i + 1) for i in range(step - 1, size - 1)]),
    )


def line_blocks(steps):
    size, here = lax.axis_size("col"), lax.axis_index("col")
    return [
        jnp.where(here + k < size, steps[k][0], steps[size - k][1]) for k in range(1, size)
    ]


def in_col_order(blocks):
    size, here = lax.axis_size("col"), lax.axis_index("col")
    out = jnp.zeros((size,) + blocks[0].shape, blocks[0].dtype)
    for step, b in enumerate(blocks):
        place = (here + step) % size
        out = lax.dynamic_update_slice_in_dim(out, b[None], place, 0)
    return out


def spread(block, axis):
    return trade(jnp.broadcast_to(block[None], (lax.axis_size(axis),) + block.shape), axis)


def normalize(resid):
    row_mean = jnp.mean(resid, 1, keepdims=True)
    centered = resid - row_mean
    variance = jnp.mean(centered * centered, 1, keepdims=True)
    inv_std = lax.rsqrt(variance + norm_eps)
    return centered * inv_std, inv_std


def norm_backward(incoming, normed, inv_std, gain):
    scaled = incoming * gain
    return inv_std * (
        scaled
        - jnp.mean(scaled, 1, keepdims=True)
        - normed * jnp.mean(scaled * normed, 1, keepdims=True)
    )


def dp_sum(values, first_bit):
    size = lax.axis_size("dp")
    bit = first_bit
    while bit < size:
        low = values.astype(bf16)
        values = low.astype(f32) + swap(low, "dp", bit).astype(f32)
        bit *= 2
    return values


def head_part(values, head, part):
    start = (3 * head + part) * HEAD_DIM
    return values[:, start : start + HEAD_DIM]


def attend_kernel(qkv_ref, out_ref):
    qkv = qkv_ref[...]
    for head in range(out_ref.shape[1] // HEAD_DIM):
        queries, keys, vals = [head_part(qkv, head, part) for part in range(3)]
        scores = dot(queries, keys, 1, 1) * HEAD_DIM ** (-0.5)
        expo = jnp.exp(scores - jnp.max(scores, 1, keepdims=True))
        weights = expo / jnp.sum(expo, 1, keepdims=True)
        context = dot(weights.astype(bf16), vals, 1, 0).astype(bf16)
        out_ref[:, head * HEAD_DIM : (head + 1) * HEAD_DIM] = context


def attend_back_kernel(qkv_ref, d_context_ref, out_ref):
    qkv = qkv_ref[...]
    scale = HEAD_DIM ** (-0.5)
    for head in range(d_context_ref.shape[1] // HEAD_DIM):
        queries, keys, vals = [head_part(qkv, head, part) for part in range(3)]
        d_context = d_context_ref[:, head * HEAD_DIM : (head + 1) * HEAD_DIM]
        scores = dot(keys, queries, 1, 1) * scale
        expo = jnp.exp(scores - jnp.max(scores, 0, keepdims=True))
        weights = expo / jnp.sum(expo, 0, keepdims=True)
        d_value = dot(weights.astype(bf16), d_context, 1, 0)
        d_weights = dot(vals, d_context, 1, 1)
        inner = jnp.sum(d_weights * weights, 0, keepdims=True)
        d_scores = (weights * (d_weights - inner)).astype(bf16)
        d_key = dot(d_scores, queries, 1, 0) * scale
        d_query = dot(d_scores, keys, 0, 0) * scale
        for part, grad in enumerate((d_query, d_key, d_value)):
            start = (3 * head + part) * HEAD_DIM
            out_ref[:, start : start + HEAD_DIM] = grad.astype(bf16)


def by_sequence(kernel, operands, width, flops):
    tokens = operands[0].shape[0]
    heads = operands[0].shape[1] // (3 * HEAD_DIM)
    return pl.pallas_call(
        kernel,
        grid=(tokens // SEQ_LEN,),
        in_specs=[pl.BlockSpec((SEQ_LEN, v.shape[1]), lambda i: (i, 0)) for v in operands],
        out_specs=pl.BlockSpec((SEQ_LEN, width), lambda i: (i, 0)),
        out_shape=jax.ShapeDtypeStruct((tokens, width), bf16),
        compiler_params=pltpu.CompilerParams(vmem_limit_bytes=40 * 2**20),
        cost_estimate=pl.CostEstimate(
            flops=flops * tokens * SEQ_LEN * heads * HEAD_DIM,
            bytes_accessed=2 * tokens * (width + sum(v.shape[1] for v in operands)),
            transcendentals=tokens * SEQ_LEN * heads,
        ),
    )(*operands)


def per_device(
    tokens,
    w_qkv,
    bias_qv,
    w_out,
    bias_out,
    gain_one,
    shift_one,
    w_in,
    bias_in,
    w_back,
    bias_back,
    gain_two,
    shift_two,
    cotangent,
):
    rows, cols = lax.axis_size("row"), lax.axis_size("col")
    r, n = lax.axis_index("row"), lax.axis_index("dp") & 1
    dp_size = lax.axis_size("dp")
    group, width_local = tokens.shape
    block = group // rows
    width = width_local * rows
    heads_tile = w_qkv.shape[2]
    head_piece = heads_tile // rows
    heads_width = cols * head_piece
    hid_tile = w_in.shape[1]
    hid_piece = hid_tile // rows
    half = hid_piece // 2
    hid_half = cols * half

    heads_rows = 3 * head_piece
    wq = jnp.transpose(w_qkv, (2, 0, 1)).reshape(rows, head_piece, 3, width_local)
    wq = jnp.transpose(wq, (0, 2, 1, 3)).reshape(rows, heads_rows, width_local)
    wo = w_out.reshape(rows, head_piece, width_local)
    first = trade(jnp.concatenate([wq, wo], 1), "row")
    first = jnp.transpose(first, (1, 0, 2)).reshape(-1, width)
    first = jnp.concatenate([to_rel(first[:heads_rows], 1), first[heads_rows:]], 0)
    hid_bias = lax.dynamic_slice(bias_in, (r * hid_piece,), (hid_piece,))
    head_bias = lax.dynamic_slice(bias_qv, (0, r * head_piece), (2, head_piece)).reshape(-1)
    bias_row = jnp.concatenate([hid_bias, head_bias])
    bias_rows = jnp.pad(bias_row[None], ((0, 15), (0, width - bias_row.shape[0])))

    wi = jnp.transpose(w_in).reshape(rows, hid_piece, width_local)
    wi = lax.dynamic_slice_in_dim(wi, n * half, half, 1)
    wb = w_back.reshape(rows, hid_piece, width_local)
    wb = lax.dynamic_slice_in_dim(wb, n * half, half, 1)
    vectors = jnp.stack([bias_out, gain_one, shift_one, bias_back, gain_two, shift_two])
    vectors = jnp.pad(vectors, ((0, 10), (0, 0)))
    vectors = jnp.broadcast_to(vectors[None], (rows,) + vectors.shape)
    mixed = trade(after(jnp.concatenate([wi, wb, vectors], 1), first), "row")
    mixed = jnp.transpose(mixed, (1, 0, 2)).reshape(-1, width)
    wi, wb = mixed[:half], mixed[half : 2 * half]
    vectors = mixed[2 * half :].astype(f32)
    bias_out_f, gain_one_f, shift_one_f, bias_back_f, gain_two_f, shift_two_f = [
        vectors[i] for i in range(6)
    ]

    def both_halves(mine):
        other = swap(mine, "dp", 1)
        return jnp.concatenate([jnp.where(n == 0, mine, other), jnp.where(n == 0, other, mine)], 0)

    begin = jnp.concatenate([first, bias_rows], 0)
    steps = [(begin, begin)]
    steps.append(line_step(begin, begin, 1))
    steps[1], _ = lax.optimization_barrier((steps[1], wi))
    wi = spread(wi, "col").reshape(hid_half, width)
    steps.append(line_step(*steps[1], 2))
    steps.append(line_step(*steps[2], 3))
    line = [begin] + line_blocks(steps)
    wq_all = in_col_order([b[:heads_rows] for b in line]).reshape(3 * heads_width, width)
    bias_at = heads_rows + head_piece
    wo_all = in_col_order([b[heads_rows:bias_at] for b in line]).reshape(heads_width, width)
    col_bias = in_col_order([b[bias_at, : bias_row.shape[0]] for b in line]).astype(f32)
    bias_q = col_bias[:, hid_piece : hid_piece + head_piece]
    bias_v = col_bias[:, hid_piece + head_piece :]
    bias_qkv = jnp.concatenate([bias_q, jnp.zeros_like(bias_q), bias_v], 1).reshape(-1)
    bias_in_f = jnp.transpose(col_bias[:, :hid_piece].reshape(cols, 2, half), (1, 0, 2)).reshape(-1)

    across = swap(tokens, "row", 2)
    beside = swap(tokens, "row", 1)
    diagonal = swap(across, "row", 1)
    tokens_all = jnp.concatenate([tokens, across, beside, diagonal], 1)

    wb = spread(after(wb, line[-1]), "col").reshape(hid_half, width)
    tokens_all, wi = lax.optimization_barrier((tokens_all, wi))
    wi_all = both_halves(wi)
    cot = after(cotangent, wb).reshape(rows, block, width_local)
    cot = jnp.transpose(trade(cot, "row"), (1, 0, 2)).reshape(block, width).astype(f32)

    joined = (dot(tokens_all, wq_all, 1, 1) + bias_qkv).astype(bf16)
    context = by_sequence(attend_kernel, [joined], heads_width, 4)
    context, wb, wi_all = lax.optimization_barrier((context, wb, wi_all))
    wb_all = both_halves(wb)
    context = to_rel(context, 0)

    send = dot(context[2 * block :], wo_all, 1, 0).astype(bf16)
    keep = dot(context[: 2 * block], wo_all, 1, 0)
    attended = row_reduce(keep[:block], keep[block:], send[:block], send[block:], 0) + bias_out_f
    tokens_own = lax.dynamic_slice_in_dim(tokens_all, r * block, block, 0)
    tokens_own = from_rel(tokens_own, 1).astype(f32)
    normed_one, inv_one = normalize(tokens_own + attended)
    hidden_one = normed_one * gain_one_f + shift_one_f

    def chips(values):
        over = swap(values, "row", 2)
        near = jnp.concatenate([values, swap(values, "row", 1)], 0)
        return near, jnp.concatenate([over, swap(over, "row", 1)], 0)

    def reduce_chips(near, far):
        return row_reduce(near[:block], far[:block], near[block:], far[block:], 0)

    hidden = chips(hidden_one.astype(bf16))
    pre_act, cdf, activated, mlp = [], [], [], []
    for h in hidden:
        pre = dot(h, wi_all, 1, 1) + bias_in_f
        pre_act.append(pre)
        cdf.append(0.5 * (1.0 + lax.erf(pre * 0.7071067811865476)))
        activated.append((pre * cdf[-1]).astype(bf16))
        mlp.append(dot(activated[-1], wb_all, 1, 0))
    mlp_out = reduce_chips(*mlp) + bias_back_f
    normed_two, inv_two = normalize(hidden_one + mlp_out)
    output = (normed_two * gain_two_f + shift_two_f).astype(bf16)

    d_two = norm_backward(cot, normed_two, inv_two, gain_two_f)
    d_mlp_low = d_two.astype(bf16)
    d_mlp = chips(d_mlp_low)
    d_pre, d_hid = [], []
    for k in range(2):
        d_activated = dot(d_mlp[k], wb_all, 1, 1)
        pdf = jnp.exp(-0.5 * pre_act[k] * pre_act[k]) * 0.3989422804014327
        d_pre.append((d_activated * (cdf[k] + pre_act[k] * pdf)).astype(bf16))
        d_hid.append(dot(d_pre[k], wi_all, 1, 0))
    grad_wb = sum(dot(a, b, 0, 0) for a, b in zip(activated, d_mlp)).astype(bf16)
    d_hidden = d_two + reduce_chips(*d_hid)
    d_hidden, _ = lax.optimization_barrier((d_hidden, grad_wb))

    def row_trade(values):
        sent = [lax.dynamic_slice_in_dim(values, r ^ j, 1, 0) for j in range(rows)]
        got = jnp.concatenate([sent[0]] + [swap(sent[j], "row", j) for j in range(1, rows)], 0)
        return jnp.concatenate(
            [lax.dynamic_slice_in_dim(got, r ^ a, 1, 0) for a in range(rows)], 0
        )

    output = jnp.transpose(output.reshape(block, rows, width_local), (1, 0, 2))
    output = row_trade(output).reshape(group, width_local)
    grad_wi = sum(dot(a, b, 0, 0) for a, b in zip(d_pre, hidden)).astype(bf16)
    grad_wi_ready = grad_wi

    def half_of(grad, k):
        return lax.dynamic_slice_in_dim(grad, k * hid_half, hid_half, 0)

    wb_other = swap(half_of(grad_wb, 1 - n), "dp", 1)
    wi_other = swap(half_of(grad_wi, 1 - n), "dp", 1)

    d_one = norm_backward(d_hidden, normed_one, inv_one, gain_one_f)
    d_att = d_one.astype(bf16)
    over = swap(d_att, "row", 2)
    over, _ = lax.optimization_barrier((over, grad_wi_ready))
    d_att_all = jnp.concatenate([d_att, over, swap(d_att, "row", 1), swap(over, "row", 1)], 0)
    d_att_all, wb_other = lax.optimization_barrier((d_att_all, wb_other))

    def by_owner(values):
        each = values.shape[2]
        got = trade(values.reshape(-1, each, width_local), ("row", "col"))
        got = jnp.sum(got.reshape(rows, cols, each, width_local).astype(f32), 1)
        return dp_sum(got, 1)

    grad_wo = dot(context, d_att_all, 0, 0).astype(bf16).reshape(cols, head_piece, rows, width_local)
    grad_wo = jnp.transpose(grad_wo, (2, 0, 1, 3))

    d_context = from_rel(dot(d_att_all, wo_all, 1, 1).astype(bf16), 0)
    d_joined = by_sequence(attend_back_kernel, [joined, d_context], 3 * heads_width, 10)
    d_joined, wi_other = lax.optimization_barrier((d_joined, wi_other))
    hid_grads = [
        (half_of(grad, n).astype(f32) + other.astype(f32)).astype(bf16).reshape(cols, half, width)
        for grad, other in ((grad_wb, wb_other), (grad_wi, wi_other))
    ]
    hid_grads = jnp.concatenate(hid_grads, 1).reshape(-1, width)
    hid_grads = lax.psum_scatter(hid_grads, "col", scatter_dimension=0, tiled=True)
    grad_wq = []
    for a in range(rows):
        j = r ^ a
        place = (((j & 1) << 1) | (j >> 1)) * width_local
        owned = lax.dynamic_slice_in_dim(tokens_all, place, width_local, 1)
        grad_wq.append(dot(d_joined, owned, 0, 0).astype(bf16).reshape(cols, heads_rows, -1))
    grad_wq = jnp.concatenate([jnp.stack(grad_wq), grad_wo], 2)
    d_joined_late = after(d_joined, grad_wq)
    grad_wq = by_owner(grad_wq)
    grad_w_out = grad_wq[:, heads_rows:].reshape(heads_tile, width_local)
    grad_wq = grad_wq[:, :heads_rows].reshape(rows, 3, head_piece, width_local)
    grad_w_qkv = jnp.transpose(grad_wq, (1, 3, 0, 2)).reshape(3, width_local, heads_tile)

    split = 2 * width_local
    d_one_rel = to_rel(d_one, 1)
    own_rows = (jnp.arange(rows) == r)[:, None, None]

    def with_own(values, own):
        values = values.reshape(rows, block, split)
        return (values + jnp.where(own_rows, own[None], 0.0)).reshape(group, split)

    keep = with_own(dot(d_joined_late, wq_all[:, :split], 1, 0), d_one_rel[:, :split])
    send = with_own(dot(d_joined_late, wq_all[:, split:], 1, 0), d_one_rel[:, split:]).astype(bf16)
    grad_tokens = row_reduce(
        keep[:, :width_local],
        keep[:, width_local:],
        send[:, :width_local],
        send[:, width_local:],
        1,
    )

    vector_grads = jnp.stack(
        [
            jnp.sum(d_att, 0, dtype=f32),
            jnp.sum(d_hidden * normed_one, 0),
            jnp.sum(d_hidden, 0),
            jnp.sum(d_mlp_low, 0, dtype=f32),
            jnp.sum(cot * normed_two, 0),
            jnp.sum(cot, 0),
        ]
    )
    hid_sums = sum(jnp.sum(d, 0, dtype=f32) for d in d_pre).reshape(2, cols, half)
    hid_sums = jnp.transpose(hid_sums, (1, 0, 2)).reshape(cols, hid_piece)
    head_sums = jnp.sum(d_joined, 0, dtype=f32).reshape(cols, 3 * head_piece)
    col_sums = jnp.concatenate(
        [hid_sums, head_sums[:, :head_piece], head_sums[:, 2 * head_piece :]], 1
    )
    col_sums = jnp.where((jnp.arange(rows) == r)[None, :, None], col_sums[:, None], 0.0)
    small = jnp.concatenate([vector_grads, col_sums.reshape(-1, width)], 0)
    for axis in ("row", "col", "dp"):
        bit = 1
        while bit < lax.axis_size(axis):
            small = small + swap(small, axis, bit)
            bit *= 2
    vector_grads = lax.dynamic_slice_in_dim(small[:6], r * width_local, width_local, 1)
    col_sums = small[6:].reshape(cols, rows, hid_piece + 2 * head_piece)
    col_sums = lax.dynamic_slice_in_dim(col_sums, lax.axis_index("col"), 1, 0)[0]
    grad_bias_in = col_sums[:, :hid_piece].reshape(hid_tile)
    head_sums = col_sums[:, hid_piece:].reshape(rows, 2, head_piece)
    grad_bias_qv = jnp.transpose(head_sums, (1, 0, 2)).reshape(2, heads_tile)

    hid_grads = dp_sum(after(hid_grads, send), 2).astype(bf16)
    if dp_size == 2:
        hid_grads = jnp.transpose(hid_grads.reshape(2 * half, rows, width_local), (1, 0, 2))
        hid_grads = jnp.broadcast_to(hid_grads[None], (2,) + hid_grads.shape)
        hid_grads = trade(hid_grads.reshape(2 * rows, 2 * half, width_local), ("dp", "row"))
        hid_grads = hid_grads.reshape(2, rows, 2, half, width_local)
    else:
        hid_grads = both_halves(hid_grads.reshape(1, 2 * half, width))
        hid_grads = jnp.transpose(hid_grads.reshape(4 * half, rows, width_local), (1, 0, 2))
        hid_grads = trade(hid_grads, "row").reshape(rows, 2, 2, half, width_local)
        hid_grads = jnp.transpose(hid_grads, (1, 0, 2, 3, 4))
    hid_grads = jnp.transpose(hid_grads, (2, 1, 0, 3, 4)).reshape(2, hid_tile, width_local)
    grad_w_back = hid_grads[0].astype(f32)
    grad_w_in = jnp.transpose(hid_grads[1]).astype(f32)

    return (
        output,
        grad_tokens,
        grad_w_qkv,
        grad_bias_qv,
        grad_w_out,
        vector_grads[0],
        vector_grads[1],
        vector_grads[2],
        grad_w_in,
        grad_bias_in,
        grad_w_back,
        vector_grads[3],
        vector_grads[4],
        vector_grads[5],
    )


def solution(mesh):
    in_specs = (
        P(("dp", "col"), "row"),
        P(None, "row", "col"),
        P(None, "col"),
        P("col", "row"),
        P("row"),
        P("row"),
        P("row"),
        P("row", "col"),
        P("col"),
        P("col", "row"),
        P("row"),
        P("row"),
        P("row"),
        P(("dp", "col"), "row"),
    )
    out_specs = (
        P(("dp", "col"), "row"),
        P(("dp", "col"), "row"),
        P(None, "row", "col"),
        P(None, "col"),
        P("col", "row"),
        P("row"),
        P("row"),
        P("row"),
        P("row", "col"),
        P("col"),
        P("col", "row"),
        P("row"),
        P("row"),
        P("row"),
    )
    return jax.shard_map(
        per_device, mesh=mesh, in_specs=in_specs, out_specs=out_specs, check_vma=False
    )
```

```python
import jax
import jax.numpy as jnp
from jax import lax
from jax.experimental import pallas as pl
from jax.experimental.pallas import tpu as pltpu
from jax.sharding import PartitionSpec as P

HEAD_DIM = 64
SEQ_LEN = 512
norm_eps = 1e-12

f32 = jnp.float32
bf16 = jnp.bfloat16

REL = (0, 2, 1, 3)


def swap(values, axis, bit):
    size = lax.axis_size(axis)
    return lax.ppermute(values, axis, [(i, i ^ bit) for i in range(size)])


def dot(left, right, left_dim, right_dim):
    return lax.dot_general(
        left, right, (((left_dim,), (right_dim,)), ((), ())), preferred_element_type=f32
    )


def after(values, earlier):
    return lax.optimization_barrier((values, earlier))[0]


def trade(values, axis):
    return lax.all_to_all(values, axis, 0, 0, tiled=True)


def to_rel(values, dim):
    r = lax.axis_index("row")
    size = values.shape[dim] // 4
    parts = [lax.dynamic_slice_in_dim(values, (r ^ j) * size, size, dim) for j in REL]
    return jnp.concatenate(parts, dim)


def from_rel(values, dim):
    r = lax.axis_index("row")
    size = values.shape[dim] // 4
    parts = []
    for a in range(4):
        j = r ^ a
        place = ((j & 1) << 1) | (j >> 1)
        parts.append(lax.dynamic_slice_in_dim(values, place * size, size, dim))
    return jnp.concatenate(parts, dim)


def row_reduce(own, across, beside, diagonal, dim):
    size = own.shape[dim]
    got = swap(jnp.concatenate([beside, diagonal], dim).astype(bf16), "row", 1)
    far = across + lax.slice_in_dim(got, size, 2 * size, axis=dim).astype(f32)
    far = swap(far.astype(bf16), "row", 2)
    return own + lax.slice_in_dim(got, 0, size, axis=dim).astype(f32) + far.astype(f32)


def line_step(up, down, step):
    size = lax.axis_size("col")
    return (
        lax.ppermute(up, "col", [(i, i - 1) for i in range(1, size - step + 1)]),
        lax.ppermute(down, "col", [(i, i + 1) for i in range(step - 1, size - 1)]),
    )


def line_blocks(steps):
    size, here = lax.axis_size("col"), lax.axis_index("col")
    return [
        jnp.where(here + k < size, steps[k][0], steps[size - k][1]) for k in range(1, size)
    ]


def in_col_order(blocks):
    size, here = lax.axis_size("col"), lax.axis_index("col")
    out = jnp.zeros((size,) + blocks[0].shape, blocks[0].dtype)
    for step, b in enumerate(blocks):
        place = (here + step) % size
        out = lax.dynamic_update_slice_in_dim(out, b[None], place, 0)
    return out


def spread(block, axis):
    return trade(jnp.broadcast_to(block[None], (lax.axis_size(axis),) + block.shape), axis)


def normalize(resid):
    row_mean = jnp.mean(resid, 1, keepdims=True)
    centered = resid - row_mean
    variance = jnp.mean(centered * centered, 1, keepdims=True)
    inv_std = lax.rsqrt(variance + norm_eps)
    return centered * inv_std, inv_std


def norm_backward(incoming, normed, inv_std, gain):
    scaled = incoming * gain
    return inv_std * (
        scaled
        - jnp.mean(scaled, 1, keepdims=True)
        - normed * jnp.mean(scaled * normed, 1, keepdims=True)
    )


def dp_sum(values, first_bit):
    size = lax.axis_size("dp")
    bit = first_bit
    while bit < size:
        low = values.astype(bf16)
        values = low.astype(f32) + swap(low, "dp", bit).astype(f32)
        bit *= 2
    return values


def head_part(values, head, part):
    start = (3 * head + part) * HEAD_DIM
    return values[:, start : start + HEAD_DIM]


def attend_kernel(qkv_ref, out_ref):
    qkv = qkv_ref[...]
    for head in range(out_ref.shape[1] // HEAD_DIM):
        queries, keys, vals = [head_part(qkv, head, part) for part in range(3)]
        scores = dot(queries, keys, 1, 1) * HEAD_DIM ** (-0.5)
        expo = jnp.exp(scores - jnp.max(scores, 1, keepdims=True))
        weights = expo / jnp.sum(expo, 1, keepdims=True)
        context = dot(weights.astype(bf16), vals, 1, 0).astype(bf16)
        out_ref[:, head * HEAD_DIM : (head + 1) * HEAD_DIM] = context


def attend_back_kernel(qkv_ref, d_context_ref, out_ref):
    qkv = qkv_ref[...]
    scale = HEAD_DIM ** (-0.5)
    for head in range(d_context_ref.shape[1] // HEAD_DIM):
        queries, keys, vals = [head_part(qkv, head, part) for part in range(3)]
        d_context = d_context_ref[:, head * HEAD_DIM : (head + 1) * HEAD_DIM]
        scores = dot(keys, queries, 1, 1) * scale
        expo = jnp.exp(scores - jnp.max(scores, 0, keepdims=True))
        weights = expo / jnp.sum(expo, 0, keepdims=True)
        d_value = dot(weights.astype(bf16), d_context, 1, 0)
        d_weights = dot(vals, d_context, 1, 1)
        inner = jnp.sum(d_weights * weights, 0, keepdims=True)
        d_scores = (weights * (d_weights - inner)).astype(bf16)
        d_key = dot(d_scores, queries, 1, 0) * scale
        d_query = dot(d_scores, keys, 0, 0) * scale
        for part, grad in enumerate((d_query, d_key, d_value)):
            start = (3 * head + part) * HEAD_DIM
            out_ref[:, start : start + HEAD_DIM] = grad.astype(bf16)


def by_sequence(kernel, operands, width, flops):
    tokens = operands[0].shape[0]
    heads = operands[0].shape[1] // (3 * HEAD_DIM)
    return pl.pallas_call(
        kernel,
        grid=(tokens // SEQ_LEN,),
        in_specs=[pl.BlockSpec((SEQ_LEN, v.shape[1]), lambda i: (i, 0)) for v in operands],
        out_specs=pl.BlockSpec((SEQ_LEN, width), lambda i: (i, 0)),
        out_shape=jax.ShapeDtypeStruct((tokens, width), bf16),
        compiler_params=pltpu.CompilerParams(vmem_limit_bytes=40 * 2**20),
        cost_estimate=pl.CostEstimate(
            flops=flops * tokens * SEQ_LEN * heads * HEAD_DIM,
            bytes_accessed=2 * tokens * (width + sum(v.shape[1] for v in operands)),
            transcendentals=tokens * SEQ_LEN * heads,
        ),
    )(*operands)


def per_device(
    tokens,
    w_qkv,
    bias_qv,
    w_out,
    bias_out,
    gain_one,
    shift_one,
    w_in,
    bias_in,
    w_back,
    bias_back,
    gain_two,
    shift_two,
    cotangent,
):
    rows, cols = lax.axis_size("row"), lax.axis_size("col")
    r, n = lax.axis_index("row"), lax.axis_index("dp") & 1
    dp_size = lax.axis_size("dp")
    group, width_local = tokens.shape
    block = group // rows
    width = width_local * rows
    heads_tile = w_qkv.shape[2]
    head_piece = heads_tile // rows
    heads_width = cols * head_piece
    hid_tile = w_in.shape[1]
    hid_piece = hid_tile // rows
    half = hid_piece // 2
    hid_half = cols * half

    heads_rows = 3 * head_piece
    wq = jnp.transpose(w_qkv, (2, 0, 1)).reshape(rows, head_piece, 3, width_local)
    wq = jnp.transpose(wq, (0, 2, 1, 3)).reshape(rows, heads_rows, width_local)
    wo = w_out.reshape(rows, head_piece, width_local)
    first = trade(jnp.concatenate([wq, wo], 1), "row")
    first = jnp.transpose(first, (1, 0, 2)).reshape(-1, width)
    first = jnp.concatenate([to_rel(first[:heads_rows], 1), first[heads_rows:]], 0)
    hid_bias = lax.dynamic_slice(bias_in, (r * hid_piece,), (hid_piece,))
    head_bias = lax.dynamic_slice(bias_qv, (0, r * head_piece), (2, head_piece)).reshape(-1)
    bias_row = jnp.concatenate([hid_bias, head_bias])
    bias_rows = jnp.pad(bias_row[None], ((0, 15), (0, width - bias_row.shape[0])))

    wi = jnp.transpose(w_in).reshape(rows, hid_piece, width_local)
    wi = lax.dynamic_slice_in_dim(wi, n * half, half, 1)
    wb = w_back.reshape(rows, hid_piece, width_local)
    wb = lax.dynamic_slice_in_dim(wb, n * half, half, 1)
    vectors = jnp.stack([bias_out, gain_one, shift_one, bias_back, gain_two, shift_two])
    vectors = jnp.pad(vectors, ((0, 10), (0, 0)))
    vectors = jnp.broadcast_to(vectors[None], (rows,) + vectors.shape)
    mixed = trade(after(jnp.concatenate([wi, wb, vectors], 1), first), "row")
    mixed = jnp.transpose(mixed, (1, 0, 2)).reshape(-1, width)
    wi, wb = mixed[:half], mixed[half : 2 * half]
    vectors = mixed[2 * half :].astype(f32)
    bias_out_f, gain_one_f, shift_one_f, bias_back_f, gain_two_f, shift_two_f = [
        vectors[i] for i in range(6)
    ]

    def both_halves(mine):
        other = swap(mine, "dp", 1)
        return jnp.concatenate([jnp.where(n == 0, mine, other), jnp.where(n == 0, other, mine)], 0)

    begin = jnp.concatenate([first, bias_rows], 0)
    steps = [(begin, begin)]
    steps.append(line_step(begin, begin, 1))
    steps[1], _ = lax.optimization_barrier((steps[1], wi))
    wi = spread(wi, "col").reshape(hid_half, width)
    steps.append(line_step(*steps[1], 2))
    steps.append(line_step(*steps[2], 3))
    line = [begin] + line_blocks(steps)
    wq_all = in_col_order([b[:heads_rows] for b in line]).reshape(3 * heads_width, width)
    bias_at = heads_rows + head_piece
    wo_all = in_col_order([b[heads_rows:bias_at] for b in line]).reshape(heads_width, width)
    col_bias = in_col_order([b[bias_at, : bias_row.shape[0]] for b in line]).astype(f32)
    bias_q = col_bias[:, hid_piece : hid_piece + head_piece]
    bias_v = col_bias[:, hid_piece + head_piece :]
    bias_qkv = jnp.concatenate([bias_q, jnp.zeros_like(bias_q), bias_v], 1).reshape(-1)
    bias_in_f = jnp.transpose(col_bias[:, :hid_piece].reshape(cols, 2, half), (1, 0, 2)).reshape(-1)

    across = swap(tokens, "row", 2)
    beside = swap(tokens, "row", 1)
    diagonal = swap(across, "row", 1)
    tokens_all = jnp.concatenate([tokens, across, beside, diagonal], 1)

    wb = spread(after(wb, line[-1]), "col").reshape(hid_half, width)
    tokens_all, wi = lax.optimization_barrier((tokens_all, wi))
    wi_all = both_halves(wi)
    cot = after(cotangent, wb).reshape(rows, block, width_local)
    cot = jnp.transpose(trade(cot, "row"), (1, 0, 2)).reshape(block, width).astype(f32)

    joined = (dot(tokens_all, wq_all, 1, 1) + bias_qkv).astype(bf16)
    context = by_sequence(attend_kernel, [joined], heads_width, 4)
    context, wb, wi_all = lax.optimization_barrier((context, wb, wi_all))
    wb_all = both_halves(wb)
    context = to_rel(context, 0)

    send = dot(context[2 * block :], wo_all, 1, 0).astype(bf16)
    keep = dot(context[: 2 * block], wo_all, 1, 0)
    attended = row_reduce(keep[:block], keep[block:], send[:block], send[block:], 0) + bias_out_f
    tokens_own = lax.dynamic_slice_in_dim(tokens_all, r * block, block, 0)
    tokens_own = from_rel(tokens_own, 1).astype(f32)
    normed_one, inv_one = normalize(tokens_own + attended)
    hidden_one = normed_one * gain_one_f + shift_one_f

    def chips(values):
        over = swap(values, "row", 2)
        near = jnp.concatenate([values, swap(values, "row", 1)], 0)
        return near, jnp.concatenate([over, swap(over, "row", 1)], 0)

    def reduce_chips(near, far):
        return row_reduce(near[:block], far[:block], near[block:], far[block:], 0)

    hidden = chips(hidden_one.astype(bf16))
    pre_act, cdf, activated, mlp = [], [], [], []
    for h in hidden:
        pre = dot(h, wi_all, 1, 1) + bias_in_f
        pre_act.append(pre)
        cdf.append(0.5 * (1.0 + lax.erf(pre * 0.7071067811865476)))
        activated.append((pre * cdf[-1]).astype(bf16))
        mlp.append(dot(activated[-1], wb_all, 1, 0))
    mlp_out = reduce_chips(*mlp) + bias_back_f
    normed_two, inv_two = normalize(hidden_one + mlp_out)
    output = (normed_two * gain_two_f + shift_two_f).astype(bf16)

    d_two = norm_backward(cot, normed_two, inv_two, gain_two_f)
    d_mlp_low = d_two.astype(bf16)
    d_mlp = chips(d_mlp_low)
    d_pre, d_hid = [], []
    for k in range(2):
        d_activated = dot(d_mlp[k], wb_all, 1, 1)
        pdf = jnp.exp(-0.5 * pre_act[k] * pre_act[k]) * 0.3989422804014327
        d_pre.append((d_activated * (cdf[k] + pre_act[k] * pdf)).astype(bf16))
        d_hid.append(dot(d_pre[k], wi_all, 1, 0))
    grad_wb = sum(dot(a, b, 0, 0) for a, b in zip(activated, d_mlp)).astype(bf16)
    d_hidden = d_two + reduce_chips(*d_hid)
    d_hidden, _ = lax.optimization_barrier((d_hidden, grad_wb))

    def row_trade(values):
        sent = [lax.dynamic_slice_in_dim(values, r ^ j, 1, 0) for j in range(rows)]
        got = jnp.concatenate([sent[0]] + [swap(sent[j], "row", j) for j in range(1, rows)], 0)
        return jnp.concatenate(
            [lax.dynamic_slice_in_dim(got, r ^ a, 1, 0) for a in range(rows)], 0
        )

    output = jnp.transpose(output.reshape(block, rows, width_local), (1, 0, 2))
    output = row_trade(output).reshape(group, width_local)
    grad_wi = sum(dot(a, b, 0, 0) for a, b in zip(d_pre, hidden)).astype(bf16)
    grad_wi_ready = grad_wi

    def half_of(grad, k):
        return lax.dynamic_slice_in_dim(grad, k * hid_half, hid_half, 0)

    wb_other = swap(half_of(grad_wb, 1 - n), "dp", 1)
    wi_other = swap(half_of(grad_wi, 1 - n), "dp", 1)

    d_one = norm_backward(d_hidden, normed_one, inv_one, gain_one_f)
    d_att = d_one.astype(bf16)
    over = swap(d_att, "row", 2)
    over, _ = lax.optimization_barrier((over, grad_wi_ready))
    d_att_all = jnp.concatenate([d_att, over, swap(d_att, "row", 1), swap(over, "row", 1)], 0)
    d_att_all, wb_other = lax.optimization_barrier((d_att_all, wb_other))

    def by_owner(values):
        each = values.shape[2]
        raw = trade(values.reshape(-1, each, width_local), ("row", "col"))
        got = jnp.sum(raw.reshape(rows, cols, each, width_local).astype(f32), 1)
        return dp_sum(got, 1), raw

    grad_wo = dot(context, d_att_all, 0, 0).astype(bf16).reshape(cols, head_piece, rows, width_local)
    grad_wo = jnp.transpose(grad_wo, (2, 0, 1, 3))

    d_context = from_rel(dot(d_att_all, wo_all, 1, 1).astype(bf16), 0)
    d_joined = by_sequence(attend_back_kernel, [joined, d_context], 3 * heads_width, 10)
    wi_other = after(wi_other, d_joined)
    hid_grads = [
        (half_of(grad, n).astype(f32) + other.astype(f32)).astype(bf16).reshape(cols, half, width)
        for grad, other in ((grad_wb, wb_other), (grad_wi, wi_other))
    ]
    hid_grads = jnp.concatenate(hid_grads, 1).reshape(-1, width)
    hid_grads = lax.psum_scatter(hid_grads, "col", scatter_dimension=0, tiled=True)
    grad_wq = []
    for a in range(rows):
        j = r ^ a
        place = (((j & 1) << 1) | (j >> 1)) * width_local
        owned = lax.dynamic_slice_in_dim(tokens_all, place, width_local, 1)
        grad_wq.append(dot(d_joined, owned, 0, 0).astype(bf16).reshape(cols, heads_rows, -1))
    grad_wq = jnp.concatenate([jnp.stack(grad_wq), grad_wo], 2)
    d_joined_late = after(d_joined, grad_wq)
    grad_wq, arrived = by_owner(grad_wq)
    grad_w_out = grad_wq[:, heads_rows:].reshape(heads_tile, width_local)
    grad_wq = grad_wq[:, :heads_rows].reshape(rows, 3, head_piece, width_local)
    grad_w_qkv = jnp.transpose(grad_wq, (1, 3, 0, 2)).reshape(3, width_local, heads_tile)

    split = 2 * width_local
    d_one_rel = to_rel(d_one, 1)
    own_rows = (jnp.arange(rows) == r)[:, None, None]

    def with_own(values, own):
        values = values.reshape(rows, block, split)
        return (values + jnp.where(own_rows, own[None], 0.0)).reshape(group, split)

    keep = with_own(dot(d_joined_late, wq_all[:, :split], 1, 0), d_one_rel[:, :split])
    send = with_own(dot(d_joined_late, wq_all[:, split:], 1, 0), d_one_rel[:, split:]).astype(bf16)
    grad_tokens = row_reduce(
        keep[:, :width_local],
        keep[:, width_local:],
        send[:, :width_local],
        send[:, width_local:],
        1,
    )

    vector_grads = jnp.stack(
        [
            jnp.sum(d_att, 0, dtype=f32),
            jnp.sum(d_hidden * normed_one, 0),
            jnp.sum(d_hidden, 0),
            jnp.sum(d_mlp_low, 0, dtype=f32),
            jnp.sum(cot * normed_two, 0),
            jnp.sum(cot, 0),
        ]
    )
    hid_sums = sum(jnp.sum(d, 0, dtype=f32) for d in d_pre).reshape(2, cols, half)
    hid_sums = jnp.transpose(hid_sums, (1, 0, 2)).reshape(cols, hid_piece)
    head_sums = jnp.sum(d_joined, 0, dtype=f32).reshape(cols, 3 * head_piece)
    col_sums = jnp.concatenate(
        [hid_sums, head_sums[:, :head_piece], head_sums[:, 2 * head_piece :]], 1
    )
    col_sums = jnp.where((jnp.arange(rows) == r)[None, :, None], col_sums[:, None], 0.0)
    small = jnp.concatenate([vector_grads, col_sums.reshape(-1, width)], 0)
    for axis in ("row", "dp", "col"):
        bit = 1
        small = after(small, arrived) if axis == "col" else small
        while bit < lax.axis_size(axis):
            small = small + swap(small, axis, bit)
            bit *= 2
    vector_grads = lax.dynamic_slice_in_dim(small[:6], r * width_local, width_local, 1)
    col_sums = small[6:].reshape(cols, rows, hid_piece + 2 * head_piece)
    col_sums = lax.dynamic_slice_in_dim(col_sums, lax.axis_index("col"), 1, 0)[0]
    grad_bias_in = col_sums[:, :hid_piece].reshape(hid_tile)
    head_sums = col_sums[:, hid_piece:].reshape(rows, 2, head_piece)
    grad_bias_qv = jnp.transpose(head_sums, (1, 0, 2)).reshape(2, heads_tile)

    hid_grads = dp_sum(after(hid_grads, send), 2).astype(bf16)
    if dp_size == 2:
        hid_grads = jnp.transpose(hid_grads.reshape(2 * half, rows, width_local), (1, 0, 2))
        hid_grads = jnp.broadcast_to(hid_grads[None], (2,) + hid_grads.shape)
        hid_grads = trade(hid_grads.reshape(2 * rows, 2 * half, width_local), ("dp", "row"))
        hid_grads = hid_grads.reshape(2, rows, 2, half, width_local)
    else:
        hid_grads = both_halves(hid_grads.reshape(1, 2 * half, width))
        hid_grads = jnp.transpose(hid_grads.reshape(4 * half, rows, width_local), (1, 0, 2))
        hid_grads = trade(hid_grads, "row").reshape(rows, 2, 2, half, width_local)
        hid_grads = jnp.transpose(hid_grads, (1, 0, 2, 3, 4))
    hid_grads = jnp.transpose(hid_grads, (2, 1, 0, 3, 4)).reshape(2, hid_tile, width_local)
    grad_w_back = hid_grads[0].astype(f32)
    grad_w_in = jnp.transpose(hid_grads[1]).astype(f32)

    return (
        output,
        grad_tokens,
        grad_w_qkv,
        grad_bias_qv,
        grad_w_out,
        vector_grads[0],
        vector_grads[1],
        vector_grads[2],
        grad_w_in,
        grad_bias_in,
        grad_w_back,
        vector_grads[3],
        vector_grads[4],
        vector_grads[5],
    )


def solution(mesh):
    in_specs = (
        P(("dp", "col"), "row"),
        P(None, "row", "col"),
        P(None, "col"),
        P("col", "row"),
        P("row"),
        P("row"),
        P("row"),
        P("row", "col"),
        P("col"),
        P("col", "row"),
        P("row"),
        P("row"),
        P("row"),
        P(("dp", "col"), "row"),
    )
    out_specs = (
        P(("dp", "col"), "row"),
        P(("dp", "col"), "row"),
        P(None, "row", "col"),
        P(None, "col"),
        P("col", "row"),
        P("row"),
        P("row"),
        P("row"),
        P("row", "col"),
        P("col"),
        P("col", "row"),
        P("row"),
        P("row"),
        P("row"),
    )
    return jax.shard_map(
        per_device, mesh=mesh, in_specs=in_specs, out_specs=out_specs, check_vma=False
    )
```

```python
import jax
import jax.numpy as jnp
from jax import lax
from jax.experimental import pallas as pl
from jax.experimental.pallas import tpu as pltpu
from jax.sharding import PartitionSpec as P

HEAD_DIM = 64
SEQ_LEN = 512
norm_eps = 1e-12

f32 = jnp.float32
bf16 = jnp.bfloat16

REL = (0, 2, 1, 3)


def swap(values, axis, bit):
    size = lax.axis_size(axis)
    return lax.ppermute(values, axis, [(i, i ^ bit) for i in range(size)])


def dot(left, right, left_dim, right_dim):
    return lax.dot_general(
        left, right, (((left_dim,), (right_dim,)), ((), ())), preferred_element_type=f32
    )


def after(values, earlier):
    return lax.optimization_barrier((values, earlier))[0]


def trade(values, axis):
    return lax.all_to_all(values, axis, 0, 0, tiled=True)


def to_rel(values, dim):
    r = lax.axis_index("row")
    size = values.shape[dim] // 4
    parts = [lax.dynamic_slice_in_dim(values, (r ^ j) * size, size, dim) for j in REL]
    return jnp.concatenate(parts, dim)


def from_rel(values, dim):
    r = lax.axis_index("row")
    size = values.shape[dim] // 4
    parts = []
    for a in range(4):
        j = r ^ a
        place = ((j & 1) << 1) | (j >> 1)
        parts.append(lax.dynamic_slice_in_dim(values, place * size, size, dim))
    return jnp.concatenate(parts, dim)


def row_reduce(own, across, beside, diagonal, dim):
    size = own.shape[dim]
    got = swap(jnp.concatenate([beside, diagonal], dim).astype(bf16), "row", 1)
    far = across + lax.slice_in_dim(got, size, 2 * size, axis=dim).astype(f32)
    far = swap(far.astype(bf16), "row", 2)
    return own + lax.slice_in_dim(got, 0, size, axis=dim).astype(f32) + far.astype(f32)


def line_step(up, down, step):
    size = lax.axis_size("col")
    return (
        lax.ppermute(up, "col", [(i, i - 1) for i in range(1, size - step + 1)]),
        lax.ppermute(down, "col", [(i, i + 1) for i in range(step - 1, size - 1)]),
    )


def line_blocks(steps):
    size, here = lax.axis_size("col"), lax.axis_index("col")
    return [
        jnp.where(here + k < size, steps[k][0], steps[size - k][1]) for k in range(1, size)
    ]


def in_col_order(blocks):
    size, here = lax.axis_size("col"), lax.axis_index("col")
    out = jnp.zeros((size,) + blocks[0].shape, blocks[0].dtype)
    for step, b in enumerate(blocks):
        place = (here + step) % size
        out = lax.dynamic_update_slice_in_dim(out, b[None], place, 0)
    return out


def spread(block, axis):
    return trade(jnp.broadcast_to(block[None], (lax.axis_size(axis),) + block.shape), axis)


def normalize(resid):
    row_mean = jnp.mean(resid, 1, keepdims=True)
    centered = resid - row_mean
    variance = jnp.mean(centered * centered, 1, keepdims=True)
    inv_std = lax.rsqrt(variance + norm_eps)
    return centered * inv_std, inv_std


def norm_backward(incoming, normed, inv_std, gain):
    scaled = incoming * gain
    return inv_std * (
        scaled
        - jnp.mean(scaled, 1, keepdims=True)
        - normed * jnp.mean(scaled * normed, 1, keepdims=True)
    )


def dp_sum(values, first_bit):
    size = lax.axis_size("dp")
    bit = first_bit
    while bit < size:
        low = values.astype(bf16)
        values = low.astype(f32) + swap(low, "dp", bit).astype(f32)
        bit *= 2
    return values


def head_part(values, head, part):
    start = (3 * head + part) * HEAD_DIM
    return values[:, start : start + HEAD_DIM]


def attend_kernel(qkv_ref, out_ref):
    qkv = qkv_ref[...]
    for head in range(out_ref.shape[1] // HEAD_DIM):
        queries, keys, vals = [head_part(qkv, head, part) for part in range(3)]
        scores = dot(queries, keys, 1, 1) * HEAD_DIM ** (-0.5)
        expo = jnp.exp(scores - jnp.max(scores, 1, keepdims=True))
        weights = expo / jnp.sum(expo, 1, keepdims=True)
        context = dot(weights.astype(bf16), vals, 1, 0).astype(bf16)
        out_ref[:, head * HEAD_DIM : (head + 1) * HEAD_DIM] = context


def attend_back_kernel(qkv_ref, d_context_ref, out_ref):
    qkv = qkv_ref[...]
    scale = HEAD_DIM ** (-0.5)
    for head in range(d_context_ref.shape[1] // HEAD_DIM):
        queries, keys, vals = [head_part(qkv, head, part) for part in range(3)]
        d_context = d_context_ref[:, head * HEAD_DIM : (head + 1) * HEAD_DIM]
        scores = dot(keys, queries, 1, 1) * scale
        expo = jnp.exp(scores - jnp.max(scores, 0, keepdims=True))
        weights = expo / jnp.sum(expo, 0, keepdims=True)
        d_value = dot(weights.astype(bf16), d_context, 1, 0)
        d_weights = dot(vals, d_context, 1, 1)
        inner = jnp.sum(d_weights * weights, 0, keepdims=True)
        d_scores = (weights * (d_weights - inner)).astype(bf16)
        d_key = dot(d_scores, queries, 1, 0) * scale
        d_query = dot(d_scores, keys, 0, 0) * scale
        for part, grad in enumerate((d_query, d_key, d_value)):
            start = (3 * head + part) * HEAD_DIM
            out_ref[:, start : start + HEAD_DIM] = grad.astype(bf16)


def by_sequence(kernel, operands, width, flops):
    tokens = operands[0].shape[0]
    heads = operands[0].shape[1] // (3 * HEAD_DIM)
    return pl.pallas_call(
        kernel,
        grid=(tokens // SEQ_LEN,),
        in_specs=[pl.BlockSpec((SEQ_LEN, v.shape[1]), lambda i: (i, 0)) for v in operands],
        out_specs=pl.BlockSpec((SEQ_LEN, width), lambda i: (i, 0)),
        out_shape=jax.ShapeDtypeStruct((tokens, width), bf16),
        compiler_params=pltpu.CompilerParams(vmem_limit_bytes=40 * 2**20),
        cost_estimate=pl.CostEstimate(
            flops=flops * tokens * SEQ_LEN * heads * HEAD_DIM,
            bytes_accessed=2 * tokens * (width + sum(v.shape[1] for v in operands)),
            transcendentals=tokens * SEQ_LEN * heads,
        ),
    )(*operands)


def per_device(
    tokens,
    w_qkv,
    bias_qv,
    w_out,
    bias_out,
    gain_one,
    shift_one,
    w_in,
    bias_in,
    w_back,
    bias_back,
    gain_two,
    shift_two,
    cotangent,
):
    rows, cols = lax.axis_size("row"), lax.axis_size("col")
    r, n = lax.axis_index("row"), lax.axis_index("dp") & 1
    dp_size = lax.axis_size("dp")
    group, width_local = tokens.shape
    block = group // rows
    width = width_local * rows
    heads_tile = w_qkv.shape[2]
    head_piece = heads_tile // rows
    heads_width = cols * head_piece
    hid_tile = w_in.shape[1]
    hid_piece = hid_tile // rows
    half = hid_piece // 2
    hid_half = cols * half

    heads_rows = 3 * head_piece
    wq = jnp.transpose(w_qkv, (2, 0, 1)).reshape(rows, head_piece, 3, width_local)
    wq = jnp.transpose(wq, (0, 2, 1, 3)).reshape(rows, heads_rows, width_local)
    wo = w_out.reshape(rows, head_piece, width_local)
    first = trade(jnp.concatenate([wq, wo], 1), "row")
    first = jnp.transpose(first, (1, 0, 2)).reshape(-1, width)
    first = jnp.concatenate([to_rel(first[:heads_rows], 1), first[heads_rows:]], 0)
    hid_bias = lax.dynamic_slice(bias_in, (r * hid_piece,), (hid_piece,))
    head_bias = lax.dynamic_slice(bias_qv, (0, r * head_piece), (2, head_piece)).reshape(-1)
    bias_row = jnp.concatenate([hid_bias, head_bias])
    bias_rows = jnp.pad(bias_row[None], ((0, 15), (0, width - bias_row.shape[0])))

    wi = jnp.transpose(w_in).reshape(rows, hid_piece, width_local)
    wi = lax.dynamic_slice_in_dim(wi, n * half, half, 1)
    wb = w_back.reshape(rows, hid_piece, width_local)
    wb = lax.dynamic_slice_in_dim(wb, n * half, half, 1)
    vectors = jnp.stack([bias_out, gain_one, shift_one, bias_back, gain_two, shift_two])
    vectors = jnp.pad(vectors, ((0, 10), (0, 0)))
    vectors = jnp.broadcast_to(vectors[None], (rows,) + vectors.shape)
    mixed = trade(after(jnp.concatenate([wi, wb, vectors], 1), first), "row")
    mixed = jnp.transpose(mixed, (1, 0, 2)).reshape(-1, width)
    wi, wb = mixed[:half], mixed[half : 2 * half]
    vectors = mixed[2 * half :].astype(f32)
    bias_out_f, gain_one_f, shift_one_f, bias_back_f, gain_two_f, shift_two_f = [
        vectors[i] for i in range(6)
    ]

    def both_halves(mine):
        other = swap(mine, "dp", 1)
        return jnp.concatenate([jnp.where(n == 0, mine, other), jnp.where(n == 0, other, mine)], 0)

    begin = jnp.concatenate([first, bias_rows], 0)
    steps = [(begin, begin)]
    steps.append(line_step(begin, begin, 1))
    steps[1], _ = lax.optimization_barrier((steps[1], wi))
    wi = spread(wi, "col").reshape(hid_half, width)
    steps.append(line_step(*steps[1], 2))
    steps.append(line_step(*steps[2], 3))
    line = [begin] + line_blocks(steps)
    wq_all = in_col_order([b[:heads_rows] for b in line]).reshape(3 * heads_width, width)
    bias_at = heads_rows + head_piece
    wo_all = in_col_order([b[heads_rows:bias_at] for b in line]).reshape(heads_width, width)
    col_bias = in_col_order([b[bias_at, : bias_row.shape[0]] for b in line]).astype(f32)
    bias_q = col_bias[:, hid_piece : hid_piece + head_piece]
    bias_v = col_bias[:, hid_piece + head_piece :]
    bias_qkv = jnp.concatenate([bias_q, jnp.zeros_like(bias_q), bias_v], 1).reshape(-1)
    bias_in_f = jnp.transpose(col_bias[:, :hid_piece].reshape(cols, 2, half), (1, 0, 2)).reshape(-1)

    across = swap(tokens, "row", 2)
    beside = swap(tokens, "row", 1)
    diagonal = swap(across, "row", 1)
    tokens_all = jnp.concatenate([tokens, across, beside, diagonal], 1)

    wb = spread(after(wb, line[-1]), "col").reshape(hid_half, width)
    tokens_all, wi = lax.optimization_barrier((tokens_all, wi))
    wi_all = both_halves(wi)
    cot = after(cotangent, wb).reshape(rows, block, width_local)
    cot = jnp.transpose(trade(cot, "row"), (1, 0, 2)).reshape(block, width).astype(f32)

    joined = (dot(tokens_all, wq_all, 1, 1) + bias_qkv).astype(bf16)
    context = by_sequence(attend_kernel, [joined], heads_width, 4)
    context, wb, wi_all = lax.optimization_barrier((context, wb, wi_all))
    wb_all = both_halves(wb)
    context = to_rel(context, 0)

    send = dot(context[2 * block :], wo_all, 1, 0).astype(bf16)
    keep = dot(context[: 2 * block], wo_all, 1, 0)
    attended = row_reduce(keep[:block], keep[block:], send[:block], send[block:], 0) + bias_out_f
    tokens_own = lax.dynamic_slice_in_dim(tokens_all, r * block, block, 0)
    tokens_own = from_rel(tokens_own, 1).astype(f32)
    normed_one, inv_one = normalize(tokens_own + attended)
    hidden_one = normed_one * gain_one_f + shift_one_f

    def chips(values):
        over = swap(values, "row", 2)
        near = jnp.concatenate([values, swap(values, "row", 1)], 0)
        return near, jnp.concatenate([over, swap(over, "row", 1)], 0)

    def reduce_chips(near, far):
        return row_reduce(near[:block], far[:block], near[block:], far[block:], 0)

    hidden = chips(hidden_one.astype(bf16))
    pre_act, cdf, activated, mlp = [], [], [], []
    for h in hidden:
        pre = dot(h, wi_all, 1, 1) + bias_in_f
        pre_act.append(pre)
        cdf.append(0.5 * (1.0 + lax.erf(pre * 0.7071067811865476)))
        activated.append((pre * cdf[-1]).astype(bf16))
        mlp.append(dot(activated[-1], wb_all, 1, 0))
    mlp_out = reduce_chips(*mlp) + bias_back_f
    normed_two, inv_two = normalize(hidden_one + mlp_out)
    output = (normed_two * gain_two_f + shift_two_f).astype(bf16)

    d_two = norm_backward(cot, normed_two, inv_two, gain_two_f)
    d_mlp_low = d_two.astype(bf16)
    d_mlp = chips(d_mlp_low)
    d_pre, d_hid = [], []
    for k in range(2):
        d_activated = dot(d_mlp[k], wb_all, 1, 1)
        pdf = jnp.exp(-0.5 * pre_act[k] * pre_act[k]) * 0.3989422804014327
        d_pre.append((d_activated * (cdf[k] + pre_act[k] * pdf)).astype(bf16))
        d_hid.append(dot(d_pre[k], wi_all, 1, 0))
    grad_wb = sum(dot(a, b, 0, 0) for a, b in zip(activated, d_mlp)).astype(bf16)
    d_hidden = d_two + reduce_chips(*d_hid)
    d_hidden, _ = lax.optimization_barrier((d_hidden, grad_wb))

    def row_trade(values):
        sent = [lax.dynamic_slice_in_dim(values, r ^ j, 1, 0) for j in range(rows)]
        got = jnp.concatenate([sent[0]] + [swap(sent[j], "row", j) for j in range(1, rows)], 0)
        return jnp.concatenate(
            [lax.dynamic_slice_in_dim(got, r ^ a, 1, 0) for a in range(rows)], 0
        )

    output = jnp.transpose(output.reshape(block, rows, width_local), (1, 0, 2))
    output = row_trade(output).reshape(group, width_local)
    grad_wi = sum(dot(a, b, 0, 0) for a, b in zip(d_pre, hidden)).astype(bf16)
    grad_wi_ready = grad_wi

    def half_of(grad, k):
        return lax.dynamic_slice_in_dim(grad, k * hid_half, hid_half, 0)

    wb_other = swap(half_of(grad_wb, 1 - n), "dp", 1)
    wi_other = swap(half_of(grad_wi, 1 - n), "dp", 1)

    d_one = norm_backward(d_hidden, normed_one, inv_one, gain_one_f)
    d_att = d_one.astype(bf16)
    over = swap(d_att, "row", 2)
    over, _ = lax.optimization_barrier((over, grad_wi_ready))
    d_att_all = jnp.concatenate([d_att, over, swap(d_att, "row", 1), swap(over, "row", 1)], 0)
    d_att_all, wb_other = lax.optimization_barrier((d_att_all, wb_other))

    def by_owner(values):
        each = values.shape[2] // 2
        own, other = [
            lax.dynamic_slice_in_dim(values, k * each, each, 2) for k in (n, 1 - n)
        ]
        paired = (own.astype(f32) + swap(other, "dp", 1).astype(f32)).astype(bf16)
        raw = trade(paired.reshape(-1, each, width_local), ("row", "col"))
        got = jnp.sum(raw.reshape(rows, cols, each, width_local).astype(f32), 1)
        low = dp_sum(got, 2).astype(bf16)
        back = swap(low, "dp", 1)
        both = [jnp.where(n == 0, low, back), jnp.where(n == 0, back, low)]
        return jnp.concatenate(both, 1).astype(f32), raw

    grad_wo = dot(context, d_att_all, 0, 0).astype(bf16).reshape(cols, head_piece, rows, width_local)
    grad_wo = jnp.transpose(grad_wo, (2, 0, 1, 3))

    d_context = from_rel(dot(d_att_all, wo_all, 1, 1).astype(bf16), 0)
    d_joined = by_sequence(attend_back_kernel, [joined, d_context], 3 * heads_width, 10)
    wi_other = after(wi_other, d_joined)
    hid_grads = [
        (half_of(grad, n).astype(f32) + other.astype(f32)).astype(bf16).reshape(cols, half, width)
        for grad, other in ((grad_wb, wb_other), (grad_wi, wi_other))
    ]
    hid_grads = jnp.concatenate(hid_grads, 1).reshape(-1, width)
    hid_grads = lax.psum_scatter(hid_grads, "col", scatter_dimension=0, tiled=True)
    grad_wq = []
    for a in range(rows):
        j = r ^ a
        place = (((j & 1) << 1) | (j >> 1)) * width_local
        owned = lax.dynamic_slice_in_dim(tokens_all, place, width_local, 1)
        grad_wq.append(dot(d_joined, owned, 0, 0).astype(bf16).reshape(cols, heads_rows, -1))
    grad_wq = jnp.concatenate([jnp.stack(grad_wq), grad_wo], 2)
    d_joined_late = after(d_joined, grad_wq)
    grad_wq, arrived = by_owner(grad_wq)
    grad_w_out = grad_wq[:, heads_rows:].reshape(heads_tile, width_local)
    grad_wq = grad_wq[:, :heads_rows].reshape(rows, 3, head_piece, width_local)
    grad_w_qkv = jnp.transpose(grad_wq, (1, 3, 0, 2)).reshape(3, width_local, heads_tile)

    split = 2 * width_local
    d_one_rel = to_rel(d_one, 1)
    own_rows = (jnp.arange(rows) == r)[:, None, None]

    def with_own(values, own):
        values = values.reshape(rows, block, split)
        return (values + jnp.where(own_rows, own[None], 0.0)).reshape(group, split)

    keep = with_own(dot(d_joined_late, wq_all[:, :split], 1, 0), d_one_rel[:, :split])
    send = with_own(dot(d_joined_late, wq_all[:, split:], 1, 0), d_one_rel[:, split:]).astype(bf16)
    grad_tokens = row_reduce(
        keep[:, :width_local],
        keep[:, width_local:],
        send[:, :width_local],
        send[:, width_local:],
        1,
    )

    vector_grads = jnp.stack(
        [
            jnp.sum(d_att, 0, dtype=f32),
            jnp.sum(d_hidden * normed_one, 0),
            jnp.sum(d_hidden, 0),
            jnp.sum(d_mlp_low, 0, dtype=f32),
            jnp.sum(cot * normed_two, 0),
            jnp.sum(cot, 0),
        ]
    )
    hid_sums = sum(jnp.sum(d, 0, dtype=f32) for d in d_pre).reshape(2, cols, half)
    hid_sums = jnp.transpose(hid_sums, (1, 0, 2)).reshape(cols, hid_piece)
    head_sums = jnp.sum(d_joined, 0, dtype=f32).reshape(cols, 3 * head_piece)
    col_sums = jnp.concatenate(
        [hid_sums, head_sums[:, :head_piece], head_sums[:, 2 * head_piece :]], 1
    )
    col_sums = jnp.where((jnp.arange(rows) == r)[None, :, None], col_sums[:, None], 0.0)
    small = jnp.concatenate([vector_grads, col_sums.reshape(-1, width)], 0)
    for axis in ("row", "dp", "col"):
        bit = 1
        small = after(small, arrived) if axis == "col" else small
        while bit < lax.axis_size(axis):
            small = small + swap(small, axis, bit)
            bit *= 2
    vector_grads = lax.dynamic_slice_in_dim(small[:6], r * width_local, width_local, 1)
    col_sums = small[6:].reshape(cols, rows, hid_piece + 2 * head_piece)
    col_sums = lax.dynamic_slice_in_dim(col_sums, lax.axis_index("col"), 1, 0)[0]
    grad_bias_in = col_sums[:, :hid_piece].reshape(hid_tile)
    head_sums = col_sums[:, hid_piece:].reshape(rows, 2, head_piece)
    grad_bias_qv = jnp.transpose(head_sums, (1, 0, 2)).reshape(2, heads_tile)

    hid_grads = dp_sum(after(hid_grads, send), 2).astype(bf16)
    if dp_size == 2:
        hid_grads = jnp.transpose(hid_grads.reshape(2 * half, rows, width_local), (1, 0, 2))
        hid_grads = jnp.broadcast_to(hid_grads[None], (2,) + hid_grads.shape)
        hid_grads = trade(hid_grads.reshape(2 * rows, 2 * half, width_local), ("dp", "row"))
        hid_grads = hid_grads.reshape(2, rows, 2, half, width_local)
    else:
        hid_grads = both_halves(hid_grads.reshape(1, 2 * half, width))
        hid_grads = jnp.transpose(hid_grads.reshape(4 * half, rows, width_local), (1, 0, 2))
        hid_grads = trade(hid_grads, "row").reshape(rows, 2, 2, half, width_local)
        hid_grads = jnp.transpose(hid_grads, (1, 0, 2, 3, 4))
    hid_grads = jnp.transpose(hid_grads, (2, 1, 0, 3, 4)).reshape(2, hid_tile, width_local)
    grad_w_back = hid_grads[0].astype(f32)
    grad_w_in = jnp.transpose(hid_grads[1]).astype(f32)

    return (
        output,
        grad_tokens,
        grad_w_qkv,
        grad_bias_qv,
        grad_w_out,
        vector_grads[0],
        vector_grads[1],
        vector_grads[2],
        grad_w_in,
        grad_bias_in,
        grad_w_back,
        vector_grads[3],
        vector_grads[4],
        vector_grads[5],
    )


def solution(mesh):
    in_specs = (
        P(("dp", "col"), "row"),
        P(None, "row", "col"),
        P(None, "col"),
        P("col", "row"),
        P("row"),
        P("row"),
        P("row"),
        P("row", "col"),
        P("col"),
        P("col", "row"),
        P("row"),
        P("row"),
        P("row"),
        P(("dp", "col"), "row"),
    )
    out_specs = (
        P(("dp", "col"), "row"),
        P(("dp", "col"), "row"),
        P(None, "row", "col"),
        P(None, "col"),
        P("col", "row"),
        P("row"),
        P("row"),
        P("row"),
        P("row", "col"),
        P("col"),
        P("col", "row"),
        P("row"),
        P("row"),
        P("row"),
    )
    return jax.shard_map(
        per_device, mesh=mesh, in_specs=in_specs, out_specs=out_specs, check_vma=False
    )
```

```python
import jax
import jax.numpy as jnp
from jax import lax
from jax.experimental import pallas as pl
from jax.experimental.pallas import tpu as pltpu
from jax.sharding import PartitionSpec as P

HEAD_DIM = 64
SEQ_LEN = 512
norm_eps = 1e-12

f32 = jnp.float32
bf16 = jnp.bfloat16

REL = (0, 2, 1, 3)


def swap(values, axis, bit):
    size = lax.axis_size(axis)
    return lax.ppermute(values, axis, [(i, i ^ bit) for i in range(size)])


def dot(left, right, left_dim, right_dim):
    return lax.dot_general(
        left, right, (((left_dim,), (right_dim,)), ((), ())), preferred_element_type=f32
    )


def after(values, earlier):
    return lax.optimization_barrier((values, earlier))[0]


def trade(values, axis):
    return lax.all_to_all(values, axis, 0, 0, tiled=True)


def to_rel(values, dim):
    r = lax.axis_index("row")
    size = values.shape[dim] // 4
    parts = [lax.dynamic_slice_in_dim(values, (r ^ j) * size, size, dim) for j in REL]
    return jnp.concatenate(parts, dim)


def from_rel(values, dim):
    r = lax.axis_index("row")
    size = values.shape[dim] // 4
    parts = []
    for a in range(4):
        j = r ^ a
        place = ((j & 1) << 1) | (j >> 1)
        parts.append(lax.dynamic_slice_in_dim(values, place * size, size, dim))
    return jnp.concatenate(parts, dim)


def row_reduce(own, across, beside, diagonal, dim):
    size = own.shape[dim]
    got = swap(jnp.concatenate([beside, diagonal], dim).astype(bf16), "row", 1)
    far = across + lax.slice_in_dim(got, size, 2 * size, axis=dim).astype(f32)
    far = swap(far.astype(bf16), "row", 2)
    return own + lax.slice_in_dim(got, 0, size, axis=dim).astype(f32) + far.astype(f32)


def line_step(up, down, step):
    size = lax.axis_size("col")
    return (
        lax.ppermute(up, "col", [(i, i - 1) for i in range(1, size - step + 1)]),
        lax.ppermute(down, "col", [(i, i + 1) for i in range(step - 1, size - 1)]),
    )


def line_blocks(steps):
    size, here = lax.axis_size("col"), lax.axis_index("col")
    return [
        jnp.where(here + k < size, steps[k][0], steps[size - k][1]) for k in range(1, size)
    ]


def in_col_order(blocks):
    size, here = lax.axis_size("col"), lax.axis_index("col")
    out = jnp.zeros((size,) + blocks[0].shape, blocks[0].dtype)
    for step, b in enumerate(blocks):
        place = (here + step) % size
        out = lax.dynamic_update_slice_in_dim(out, b[None], place, 0)
    return out


def spread(block, axis):
    return trade(jnp.broadcast_to(block[None], (lax.axis_size(axis),) + block.shape), axis)


def butterfly(values, axis):
    bit = 1
    while bit < lax.axis_size(axis):
        values = values + swap(values, axis, bit)
        bit *= 2
    return values


def normalize(resid):
    row_mean = jnp.mean(resid, 1, keepdims=True)
    centered = resid - row_mean
    variance = jnp.mean(centered * centered, 1, keepdims=True)
    inv_std = lax.rsqrt(variance + norm_eps)
    return centered * inv_std, inv_std


def norm_backward(incoming, normed, inv_std, gain):
    scaled = incoming * gain
    return inv_std * (
        scaled
        - jnp.mean(scaled, 1, keepdims=True)
        - normed * jnp.mean(scaled * normed, 1, keepdims=True)
    )


def dp_sum(values, first_bit):
    size = lax.axis_size("dp")
    bit = first_bit
    while bit < size:
        low = values.astype(bf16)
        values = low.astype(f32) + swap(low, "dp", bit).astype(f32)
        bit *= 2
    return values


def head_part(values, head, part):
    start = (3 * head + part) * HEAD_DIM
    return values[:, start : start + HEAD_DIM]


def attend_kernel(qkv_ref, out_ref):
    qkv = qkv_ref[...]
    for head in range(out_ref.shape[1] // HEAD_DIM):
        queries, keys, vals = [head_part(qkv, head, part) for part in range(3)]
        scores = dot(queries, keys, 1, 1) * HEAD_DIM ** (-0.5)
        expo = jnp.exp(scores - jnp.max(scores, 1, keepdims=True))
        weights = expo / jnp.sum(expo, 1, keepdims=True)
        context = dot(weights.astype(bf16), vals, 1, 0).astype(bf16)
        out_ref[:, head * HEAD_DIM : (head + 1) * HEAD_DIM] = context


def attend_back_kernel(qkv_ref, d_context_ref, out_ref):
    qkv = qkv_ref[...]
    scale = HEAD_DIM ** (-0.5)
    for head in range(d_context_ref.shape[1] // HEAD_DIM):
        queries, keys, vals = [head_part(qkv, head, part) for part in range(3)]
        d_context = d_context_ref[:, head * HEAD_DIM : (head + 1) * HEAD_DIM]
        scores = dot(keys, queries, 1, 1) * scale
        expo = jnp.exp(scores - jnp.max(scores, 0, keepdims=True))
        weights = expo / jnp.sum(expo, 0, keepdims=True)
        d_value = dot(weights.astype(bf16), d_context, 1, 0)
        d_weights = dot(vals, d_context, 1, 1)
        inner = jnp.sum(d_weights * weights, 0, keepdims=True)
        d_scores = (weights * (d_weights - inner)).astype(bf16)
        d_key = dot(d_scores, queries, 1, 0) * scale
        d_query = dot(d_scores, keys, 0, 0) * scale
        for part, grad in enumerate((d_query, d_key, d_value)):
            start = (3 * head + part) * HEAD_DIM
            out_ref[:, start : start + HEAD_DIM] = grad.astype(bf16)


def by_sequence(kernel, operands, width, flops):
    tokens = operands[0].shape[0]
    heads = operands[0].shape[1] // (3 * HEAD_DIM)
    return pl.pallas_call(
        kernel,
        grid=(tokens // SEQ_LEN,),
        in_specs=[pl.BlockSpec((SEQ_LEN, v.shape[1]), lambda i: (i, 0)) for v in operands],
        out_specs=pl.BlockSpec((SEQ_LEN, width), lambda i: (i, 0)),
        out_shape=jax.ShapeDtypeStruct((tokens, width), bf16),
        compiler_params=pltpu.CompilerParams(vmem_limit_bytes=40 * 2**20),
        cost_estimate=pl.CostEstimate(
            flops=flops * tokens * SEQ_LEN * heads * HEAD_DIM,
            bytes_accessed=2 * tokens * (width + sum(v.shape[1] for v in operands)),
            transcendentals=tokens * SEQ_LEN * heads,
        ),
    )(*operands)


def per_device(
    tokens,
    w_qkv,
    bias_qv,
    w_out,
    bias_out,
    gain_one,
    shift_one,
    w_in,
    bias_in,
    w_back,
    bias_back,
    gain_two,
    shift_two,
    cotangent,
):
    rows, cols = lax.axis_size("row"), lax.axis_size("col")
    r, n = lax.axis_index("row"), lax.axis_index("dp") & 1
    dp_size = lax.axis_size("dp")
    group, width_local = tokens.shape
    block = group // rows
    width = width_local * rows
    heads_tile = w_qkv.shape[2]
    head_piece = heads_tile // rows
    heads_width = cols * head_piece
    hid_tile = w_in.shape[1]
    hid_piece = hid_tile // rows
    half = hid_piece // 2
    hid_half = cols * half

    heads_rows = 3 * head_piece
    wq = jnp.transpose(w_qkv, (2, 0, 1)).reshape(rows, head_piece, 3, width_local)
    wq = jnp.transpose(wq, (0, 2, 1, 3)).reshape(rows, heads_rows, width_local)
    wo = w_out.reshape(rows, head_piece, width_local)
    first = trade(jnp.concatenate([wq, wo], 1), "row")
    first = jnp.transpose(first, (1, 0, 2)).reshape(-1, width)
    first = jnp.concatenate([to_rel(first[:heads_rows], 1), first[heads_rows:]], 0)
    hid_bias = lax.dynamic_slice(bias_in, (r * hid_piece,), (hid_piece,))
    head_bias = lax.dynamic_slice(bias_qv, (0, r * head_piece), (2, head_piece)).reshape(-1)
    bias_row = jnp.concatenate([hid_bias, head_bias])
    bias_rows = jnp.pad(bias_row[None], ((0, 15), (0, width - bias_row.shape[0])))

    wi = jnp.transpose(w_in).reshape(rows, hid_piece, width_local)
    wi = lax.dynamic_slice_in_dim(wi, n * half, half, 1)
    wb = w_back.reshape(rows, hid_piece, width_local)
    wb = lax.dynamic_slice_in_dim(wb, n * half, half, 1)
    vectors = jnp.stack([bias_out, gain_one, shift_one, bias_back, gain_two, shift_two])
    vectors = jnp.pad(vectors, ((0, 10), (0, 0)))
    vectors = jnp.broadcast_to(vectors[None], (rows,) + vectors.shape)
    mixed = trade(after(jnp.concatenate([wi, wb, vectors], 1), first), "row")
    mixed = jnp.transpose(mixed, (1, 0, 2)).reshape(-1, width)
    wi, wb = mixed[:half], mixed[half : 2 * half]
    vectors = mixed[2 * half :].astype(f32)
    bias_out_f, gain_one_f, shift_one_f, bias_back_f, gain_two_f, shift_two_f = [
        vectors[i] for i in range(6)
    ]

    def both_halves(mine):
        other = swap(mine, "dp", 1)
        return jnp.concatenate([jnp.where(n == 0, mine, other), jnp.where(n == 0, other, mine)], 0)

    begin = jnp.concatenate([first, bias_rows], 0)
    steps = [(begin, begin)]
    steps.append(line_step(begin, begin, 1))
    steps[1], _ = lax.optimization_barrier((steps[1], wi))
    wi = spread(wi, "col").reshape(hid_half, width)
    steps.append(line_step(*steps[1], 2))
    steps.append(line_step(*steps[2], 3))
    line = [begin] + line_blocks(steps)
    wq_all = in_col_order([b[:heads_rows] for b in line]).reshape(3 * heads_width, width)
    bias_at = heads_rows + head_piece
    wo_all = in_col_order([b[heads_rows:bias_at] for b in line]).reshape(heads_width, width)
    col_bias = in_col_order([b[bias_at, : bias_row.shape[0]] for b in line]).astype(f32)
    bias_q = col_bias[:, hid_piece : hid_piece + head_piece]
    bias_v = col_bias[:, hid_piece + head_piece :]
    bias_qkv = jnp.concatenate([bias_q, jnp.zeros_like(bias_q), bias_v], 1).reshape(-1)
    bias_in_f = jnp.transpose(col_bias[:, :hid_piece].reshape(cols, 2, half), (1, 0, 2)).reshape(-1)

    across = swap(tokens, "row", 2)
    beside = swap(tokens, "row", 1)
    diagonal = swap(across, "row", 1)
    tokens_all = jnp.concatenate([tokens, across, beside, diagonal], 1)

    wb = spread(after(wb, line[-1]), "col").reshape(hid_half, width)
    tokens_all, wi = lax.optimization_barrier((tokens_all, wi))
    wi_all = both_halves(wi)
    cot = after(cotangent, wb).reshape(rows, block, width_local)
    cot = jnp.transpose(trade(cot, "row"), (1, 0, 2)).reshape(block, width).astype(f32)

    joined = (dot(tokens_all, wq_all, 1, 1) + bias_qkv).astype(bf16)
    context = by_sequence(attend_kernel, [joined], heads_width, 4)
    context, wb, wi_all = lax.optimization_barrier((context, wb, wi_all))
    wb_all = both_halves(wb)
    context = to_rel(context, 0)

    send = dot(context[2 * block :], wo_all, 1, 0).astype(bf16)
    keep = dot(context[: 2 * block], wo_all, 1, 0)
    attended = row_reduce(keep[:block], keep[block:], send[:block], send[block:], 0) + bias_out_f
    tokens_own = lax.dynamic_slice_in_dim(tokens_all, r * block, block, 0)
    tokens_own = from_rel(tokens_own, 1).astype(f32)
    normed_one, inv_one = normalize(tokens_own + attended)
    hidden_one = normed_one * gain_one_f + shift_one_f

    def chips(values):
        over = swap(values, "row", 2)
        near = jnp.concatenate([values, swap(values, "row", 1)], 0)
        return near, jnp.concatenate([over, swap(over, "row", 1)], 0)

    def reduce_chips(near, far):
        return row_reduce(near[:block], far[:block], near[block:], far[block:], 0)

    hidden = chips(hidden_one.astype(bf16))
    pre_act, cdf, activated, mlp = [], [], [], []
    for h in hidden:
        pre = dot(h, wi_all, 1, 1) + bias_in_f
        pre_act.append(pre)
        cdf.append(0.5 * (1.0 + lax.erf(pre * 0.7071067811865476)))
        activated.append((pre * cdf[-1]).astype(bf16))
        mlp.append(dot(activated[-1], wb_all, 1, 0))
    mlp_out = reduce_chips(*mlp) + bias_back_f
    normed_two, inv_two = normalize(hidden_one + mlp_out)
    output = (normed_two * gain_two_f + shift_two_f).astype(bf16)

    d_two = norm_backward(cot, normed_two, inv_two, gain_two_f)
    d_mlp_low = d_two.astype(bf16)
    d_mlp = chips(d_mlp_low)
    d_pre, d_hid = [], []
    for k in range(2):
        d_activated = dot(d_mlp[k], wb_all, 1, 1)
        pdf = jnp.exp(-0.5 * pre_act[k] * pre_act[k]) * 0.3989422804014327
        d_pre.append((d_activated * (cdf[k] + pre_act[k] * pdf)).astype(bf16))
        d_hid.append(dot(d_pre[k], wi_all, 1, 0))
    grad_wb = sum(dot(a, b, 0, 0) for a, b in zip(activated, d_mlp)).astype(bf16)
    d_hidden = d_two + reduce_chips(*d_hid)
    d_hidden, _ = lax.optimization_barrier((d_hidden, grad_wb))

    def row_trade(values):
        sent = [lax.dynamic_slice_in_dim(values, r ^ j, 1, 0) for j in range(rows)]
        got = jnp.concatenate([sent[0]] + [swap(sent[j], "row", j) for j in range(1, rows)], 0)
        return jnp.concatenate(
            [lax.dynamic_slice_in_dim(got, r ^ a, 1, 0) for a in range(rows)], 0
        )

    output = jnp.transpose(output.reshape(block, rows, width_local), (1, 0, 2))
    output = row_trade(output).reshape(group, width_local)
    grad_wi = sum(dot(a, b, 0, 0) for a, b in zip(d_pre, hidden)).astype(bf16)
    grad_wi_ready = grad_wi

    def half_of(grad, k):
        return lax.dynamic_slice_in_dim(grad, k * hid_half, hid_half, 0)

    wb_other = swap(half_of(grad_wb, 1 - n), "dp", 1)
    wi_other = swap(half_of(grad_wi, 1 - n), "dp", 1)

    d_one = norm_backward(d_hidden, normed_one, inv_one, gain_one_f)
    d_att = d_one.astype(bf16)
    over = swap(d_att, "row", 2)
    over, _ = lax.optimization_barrier((over, grad_wi_ready))
    d_att_all = jnp.concatenate([d_att, over, swap(d_att, "row", 1), swap(over, "row", 1)], 0)
    d_att_all, wb_other = lax.optimization_barrier((d_att_all, wb_other))

    def by_owner(values):
        each = values.shape[2] // 2
        own, other = [
            lax.dynamic_slice_in_dim(values, k * each, each, 2) for k in (n, 1 - n)
        ]
        paired = (own.astype(f32) + swap(other, "dp", 1).astype(f32)).astype(bf16)
        raw = trade(paired.reshape(-1, each, width_local), ("row", "col"))
        got = jnp.sum(raw.reshape(rows, cols, each, width_local).astype(f32), 1)
        low = dp_sum(got, 2).astype(bf16)
        back = swap(low, "dp", 1)
        both = [jnp.where(n == 0, low, back), jnp.where(n == 0, back, low)]
        return jnp.concatenate(both, 1).astype(f32)

    grad_wo = dot(context, d_att_all, 0, 0).astype(bf16).reshape(cols, head_piece, rows, width_local)
    grad_wo = jnp.transpose(grad_wo, (2, 0, 1, 3))

    d_context = from_rel(dot(d_att_all, wo_all, 1, 1).astype(bf16), 0)
    d_joined = by_sequence(attend_back_kernel, [joined, d_context], 3 * heads_width, 10)
    vector_grads = jnp.stack(
        [
            jnp.sum(d_att, 0, dtype=f32),
            jnp.sum(d_hidden * normed_one, 0),
            jnp.sum(d_hidden, 0),
            jnp.sum(d_mlp_low, 0, dtype=f32),
            jnp.sum(cot * normed_two, 0),
            jnp.sum(cot, 0),
        ]
    )
    hid_sums = sum(jnp.sum(d, 0, dtype=f32) for d in d_pre).reshape(2, cols, half)
    hid_sums = jnp.transpose(hid_sums, (1, 0, 2)).reshape(cols, hid_piece)
    head_sums = jnp.sum(d_joined, 0, dtype=f32).reshape(cols, 3 * head_piece)
    col_sums = jnp.concatenate(
        [hid_sums, head_sums[:, :head_piece], head_sums[:, 2 * head_piece :]], 1
    )
    col_sums = jnp.where((jnp.arange(rows) == r)[None, :, None], col_sums[:, None], 0.0)
    small = jnp.concatenate([vector_grads, col_sums.reshape(-1, width)], 0)
    small = butterfly(small, "col")
    wi_other = after(wi_other, small)
    hid_grads = [
        (half_of(grad, n).astype(f32) + other.astype(f32)).astype(bf16).reshape(cols, half, width)
        for grad, other in ((grad_wb, wb_other), (grad_wi, wi_other))
    ]
    hid_grads = jnp.concatenate(hid_grads, 1).reshape(-1, width)
    hid_grads = lax.psum_scatter(hid_grads, "col", scatter_dimension=0, tiled=True)
    grad_wq = []
    for a in range(rows):
        j = r ^ a
        place = (((j & 1) << 1) | (j >> 1)) * width_local
        owned = lax.dynamic_slice_in_dim(tokens_all, place, width_local, 1)
        grad_wq.append(dot(d_joined, owned, 0, 0).astype(bf16).reshape(cols, heads_rows, -1))
    grad_wq = jnp.concatenate([jnp.stack(grad_wq), grad_wo], 2)
    grad_wq, small = lax.optimization_barrier((grad_wq, small))
    d_joined_late = after(d_joined, grad_wq)
    grad_wq = by_owner(grad_wq)
    grad_w_out = grad_wq[:, heads_rows:].reshape(heads_tile, width_local)
    grad_wq = grad_wq[:, :heads_rows].reshape(rows, 3, head_piece, width_local)
    grad_w_qkv = jnp.transpose(grad_wq, (1, 3, 0, 2)).reshape(3, width_local, heads_tile)

    split = 2 * width_local
    d_one_rel = to_rel(d_one, 1)
    own_rows = (jnp.arange(rows) == r)[:, None, None]

    def with_own(values, own):
        values = values.reshape(rows, block, split)
        return (values + jnp.where(own_rows, own[None], 0.0)).reshape(group, split)

    keep = with_own(dot(d_joined_late, wq_all[:, :split], 1, 0), d_one_rel[:, :split])
    send = with_own(dot(d_joined_late, wq_all[:, split:], 1, 0), d_one_rel[:, split:]).astype(bf16)
    grad_tokens = row_reduce(
        keep[:, :width_local],
        keep[:, width_local:],
        send[:, :width_local],
        send[:, width_local:],
        1,
    )

    small = butterfly(butterfly(small, "row"), "dp")
    vector_grads = lax.dynamic_slice_in_dim(small[:6], r * width_local, width_local, 1)
    col_sums = small[6:].reshape(cols, rows, hid_piece + 2 * head_piece)
    col_sums = lax.dynamic_slice_in_dim(col_sums, lax.axis_index("col"), 1, 0)[0]
    grad_bias_in = col_sums[:, :hid_piece].reshape(hid_tile)
    head_sums = col_sums[:, hid_piece:].reshape(rows, 2, head_piece)
    grad_bias_qv = jnp.transpose(head_sums, (1, 0, 2)).reshape(2, heads_tile)

    hid_grads = dp_sum(after(hid_grads, send), 2).astype(bf16)
    if dp_size == 2:
        hid_grads = jnp.transpose(hid_grads.reshape(2 * half, rows, width_local), (1, 0, 2))
        hid_grads = jnp.broadcast_to(hid_grads[None], (2,) + hid_grads.shape)
        hid_grads = trade(hid_grads.reshape(2 * rows, 2 * half, width_local), ("dp", "row"))
        hid_grads = hid_grads.reshape(2, rows, 2, half, width_local)
    else:
        hid_grads = both_halves(hid_grads.reshape(1, 2 * half, width))
        hid_grads = jnp.transpose(hid_grads.reshape(4 * half, rows, width_local), (1, 0, 2))
        hid_grads = trade(hid_grads, "row").reshape(rows, 2, 2, half, width_local)
        hid_grads = jnp.transpose(hid_grads, (1, 0, 2, 3, 4))
    hid_grads = jnp.transpose(hid_grads, (2, 1, 0, 3, 4)).reshape(2, hid_tile, width_local)
    grad_w_back = hid_grads[0].astype(f32)
    grad_w_in = jnp.transpose(hid_grads[1]).astype(f32)

    return (
        output,
        grad_tokens,
        grad_w_qkv,
        grad_bias_qv,
        grad_w_out,
        vector_grads[0],
        vector_grads[1],
        vector_grads[2],
        grad_w_in,
        grad_bias_in,
        grad_w_back,
        vector_grads[3],
        vector_grads[4],
        vector_grads[5],
    )


def solution(mesh):
    in_specs = (
        P(("dp", "col"), "row"),
        P(None, "row", "col"),
        P(None, "col"),
        P("col", "row"),
        P("row"),
        P("row"),
        P("row"),
        P("row", "col"),
        P("col"),
        P("col", "row"),
        P("row"),
        P("row"),
        P("row"),
        P(("dp", "col"), "row"),
    )
    out_specs = (
        P(("dp", "col"), "row"),
        P(("dp", "col"), "row"),
        P(None, "row", "col"),
        P(None, "col"),
        P("col", "row"),
        P("row"),
        P("row"),
        P("row"),
        P("row", "col"),
        P("col"),
        P("col", "row"),
        P("row"),
        P("row"),
        P("row"),
    )
    return jax.shard_map(
        per_device, mesh=mesh, in_specs=in_specs, out_specs=out_specs, check_vma=False
    )
```
